256 devices in a mesh: row: 16 (over y, x), col: 8 (over z), rep: 2 (over core).
Axes of the slice: x: 4, y: 4, z: 8, core: 2. Of those that a mesh axis runs over, the one named last changes fastest.
Arguments:
- features: float32 [32768, 128], P(('row', 'col')), may hold values from -6 to 6
- cotangent: float32 [32768, 256], P(('row', 'col')), may hold values from -6 to 6
- w_self: float32 [128, 256], replicated, may hold values from -0.5 to 0.5
- w_neigh: float32 [128, 256], replicated, may hold values from -1.5 to 1.5
- bias: float32 [256], replicated, may hold values from -3 to 3
- tiles: float32 [16, 8, 184, 128, 128], P('row', 'col'), may hold values from 0 to 2.1, as said below
- tile_dst: int32 [16, 8, 184], P('row', 'col'), may hold values from 0 to 31
- tile_src: int32 [16, 8, 184], P('row', 'col'), may hold values from 0 to 15
- tile_count: int32 [16, 8], P('row', 'col'), may hold values from 61 to 184, as said below
Outputs:
- hidden: float32 [32768, 256], P(('row', 'col'), 'rep')
- grad_features: float32 [32768, 128], P(('row', 'col'), 'rep')
- grad_self: float32 [128, 256], P(None, 'rep')
- grad_neigh: float32 [128, 256], P(None, 'rep')
- grad_bias: float32 [256], P('rep')
The draws below stay inside these ranges and needn't reach their ends.
Inputs may be any that keep to these rules, and one draw needn't show every extreme that they name: `tiles`: entries are 0 (no edge) or an edge weight. Slots at positions tile_count and beyond are ignored; some cell has all 184 slots live.
All inputs are finite; a program needn't handle non-finite values.
Results may differ from the reference program's by a relative error of at most 0.0003.
Values sent between devices are 32-bit elements; how exact they have to be, the bound alone decides.
A program may use at most 128 MiB of HBM per device.

```python
import jax
import jax.numpy as jnp
from jax import lax

NPD = 2
TPD = 184
BLK = 128
FEAT = 128
HID = 256
GRID_ROWS = 16
GRID_COLS = 8
NODES = 32768


def destination_draw(key):
    dest_key = jax.random.fold_in(key, 23)
    return jax.random.randint(dest_key, (GRID_ROWS, GRID_COLS, TPD), 0, GRID_ROWS * NPD, jnp.int32)


def draw_tiles(key, part):
    destinations = destination_draw(key).reshape(GRID_ROWS * GRID_COLS, TPD)
    key = jax.random.fold_in(key, 11)
    cell_keys = jax.random.split(key, GRID_ROWS * GRID_COLS)
    kind_key, level_key = jax.random.split(jax.random.fold_in(key, 13))
    node_shape = (GRID_COLS, GRID_ROWS * NPD, BLK)
    kinds = jax.random.randint(kind_key, node_shape, 0, 16, jnp.int32)
    expected = 2.0 * TPD / (3.0 * NPD) * (BLK / 8.0)
    levels = jnp.minimum(1.0, jax.random.uniform(level_key, node_shape, jnp.float32, 0.1, 3.0) / expected)
    node_factor = jnp.where(kinds == 0, 0.0, jnp.where(kinds == 1, levels, 1.0)).astype(jnp.float32)
    column_ids = jnp.arange(GRID_ROWS * GRID_COLS, dtype=jnp.int32) % GRID_COLS

    def one_cell(inputs):
        cell_key, column, dst_local = inputs
        mask_key, weight_key = jax.random.split(cell_key)
        present = jax.random.bernoulli(mask_key, 0.125, (TPD, BLK, BLK)).astype(jnp.float32)
        values = jax.random.uniform(weight_key, (TPD, BLK, BLK), jnp.float32, 0.5, 1.5)
        row_factor = node_factor[column][dst_local]
        return present * values * row_factor[:, :, None]
    cells = lax.map(one_cell, (cell_keys, column_ids, destinations))
    return cells.reshape(GRID_ROWS, GRID_COLS, TPD, BLK, BLK)


def draw_tile_dst(key, part):
    return destination_draw(key)


def draw_tile_src(key, part):
    key = jax.random.fold_in(key, 37)
    return jax.random.randint(key, (GRID_ROWS, GRID_COLS, TPD), 0, GRID_COLS * NPD, jnp.int32)


def draw_tile_count(key, part):
    key = jax.random.fold_in(key, 41)
    count_key, full_key = jax.random.split(key)
    counts = jax.random.randint(count_key, (GRID_ROWS, GRID_COLS), TPD // 3, TPD + 1, jnp.int32)
    full_cell = jax.random.randint(full_key, (), 0, GRID_ROWS * GRID_COLS, jnp.int32)
    positions = jnp.arange(GRID_ROWS * GRID_COLS, dtype=jnp.int32).reshape(GRID_ROWS, GRID_COLS)
    return jnp.where(positions == full_cell, TPD, counts).astype(jnp.int32)


def steps_of(rng, shape, cuts, low, top_value):
    def one(dim, parts):
        draws = jax.random.uniform(jax.random.fold_in(jax.random.fold_in(rng, 6), dim), (parts,), jnp.float32, low / len(cuts), top_value / len(cuts))
        return jnp.repeat(jnp.exp(draws), shape[dim] // parts).reshape((-1,) + (1,) * (len(shape) - dim - 1))

    gain = one(*cuts[0])
    for cut in cuts[1:]:
        gain = gain * one(*cut)
    return gain


def centred(own_key, dims, deviation, limit, shards=(), kind=jnp.bfloat16):
    factor_of = steps_of(own_key, dims, shards, -0.22, 0.18) if shards else 1.0
    result = jax.random.normal(own_key, dims, jnp.float32) * deviation * factor_of
    return jnp.minimum(jnp.maximum(result, -limit), limit).astype(kind)


def setup_inputs(seed: int = 0) -> dict:
    streams_of = jax.random.split(jax.random.key(seed), 10)
    return {
        "features": centred(streams_of[0], (NODES, FEAT), 1.0, 6.0, ((0, 128),), jnp.float32),
        "cotangent": centred(streams_of[1], (NODES, HID), 1.0, 6.0, ((0, 128),), jnp.float32),
        "w_self": centred(streams_of[2], (FEAT, HID), FEAT ** -0.5, 0.5, (), jnp.float32),
        "w_neigh": centred(streams_of[3], (FEAT, HID), (FEAT // 8) ** -0.5, 1.5, (), jnp.float32),
        "bias": centred(streams_of[4], (HID,), 0.5, 3.0, (), jnp.float32),
        "tiles": draw_tiles(jax.random.fold_in(streams_of[9], 71), 0),
        "tile_dst": draw_tile_dst(jax.random.fold_in(streams_of[9], 71), 0),
        "tile_src": draw_tile_src(jax.random.fold_in(streams_of[9], 71), 0),
        "tile_count": draw_tile_count(jax.random.fold_in(streams_of[9], 71), 0),
    }


def global_blocks(cell, dst_local, src_local):
    grid_row = cell // GRID_COLS
    grid_col = cell % GRID_COLS
    dst_global = ((dst_local // NPD) * GRID_COLS + grid_col) * NPD + dst_local % NPD
    src_global = grid_row * GRID_COLS * NPD + src_local
    return dst_global.astype(jnp.int32), src_global.astype(jnp.int32)


def reference(features, cotangent, w_self, w_neigh, bias, tiles, tile_dst, tile_src, tile_count):
    highest = lax.Precision.HIGHEST
    block_count = NODES // BLK
    cell_total = GRID_ROWS * GRID_COLS
    slot_index = jnp.arange(TPD, dtype=jnp.int32)
    feature_blocks = features.reshape(block_count, BLK, FEAT)
    cell_tiles = tiles.reshape(cell_total, TPD, BLK, BLK)
    cell_dst = tile_dst.reshape(cell_total, TPD)
    cell_src = tile_src.reshape(cell_total, TPD)
    cell_count = tile_count.reshape(cell_total)
    cell_ids = jnp.arange(cell_total, dtype=jnp.int32)
    scan_inputs = (cell_ids, cell_tiles, cell_dst, cell_src, cell_count)

    def forward_cell(carry, inputs):
        sums, degree = carry
        cell, weights, dst_local, src_local, count = inputs
        live_mask = (slot_index < count).astype(features.dtype)
        dst_global, src_global = global_blocks(cell, dst_local, src_local)
        gathered = feature_blocks[src_global]
        products = jnp.einsum('tab,tbf->taf', weights, gathered, precision=highest) * live_mask[:, None, None]
        row_weight = jnp.sum(weights, axis=2) * live_mask[:, None]
        return (sums.at[dst_global].add(products), degree.at[dst_global].add(row_weight)), None

    start = (jnp.zeros((block_count, BLK, FEAT), features.dtype), jnp.zeros((block_count, BLK), features.dtype))
    (sums, degree), _ = lax.scan(forward_cell, start, scan_inputs)
    inverse = 1.0 / jnp.maximum(degree.reshape(NODES), 1.0)
    aggregate = sums.reshape(NODES, FEAT) * inverse[:, None]
    preact = jnp.dot(features, w_self, precision=highest) + jnp.dot(aggregate, w_neigh, precision=highest) + bias
    gating = jax.nn.sigmoid(preact)
    hidden = preact * gating
    grad_pre = cotangent * (gating * (1.0 + preact * (1.0 - gating)))
    factor = float(NODES) ** -0.5
    grad_self = jnp.dot(features.T, grad_pre, precision=highest) * factor
    grad_neigh = jnp.dot(aggregate.T, grad_pre, precision=highest) * factor
    grad_bias = jnp.sum(grad_pre, axis=0) * factor
    scaled = jnp.dot(grad_pre, w_neigh.T, precision=highest) * inverse[:, None]
    value_blocks = scaled.reshape(block_count, BLK, FEAT)

    def backward_cell(carry, inputs):
        cell, weights, dst_local, src_local, count = inputs
        live_mask = (slot_index < count).astype(features.dtype)
        dst_global, src_global = global_blocks(cell, dst_local, src_local)
        gathered = value_blocks[dst_global]
        products = jnp.einsum('tab,taf->tbf', weights, gathered, precision=highest) * live_mask[:, None, None]
        return carry.at[src_global].add(products), None

    back, _ = lax.scan(backward_cell, jnp.zeros((block_count, BLK, FEAT), features.dtype), scan_inputs)
    grad_features = jnp.dot(grad_pre, w_self.T, precision=highest) + back.reshape(NODES, FEAT)
    return hidden, grad_features, grad_self, grad_neigh, grad_bias
```

```python
import functools

import jax
import jax.numpy as jnp
from jax import lax
from jax.experimental import pallas as pl
from jax.experimental.pallas import tpu as pltpu
from jax.sharding import PartitionSpec as P

MESH = pl.DeviceIdType.MESH
F32 = jnp.float32
BF16 = jnp.bfloat16
VMEM = pltpu.VMEM
DMA = pltpu.SemaphoreType.DMA
MIB = 1 << 20


def split(value):
    high = value.astype(BF16)
    low = (value - high.astype(F32)).astype(BF16)
    return high, low


def dot3(left, right, dims=((1,), (0,))):
    left_high, left_low = split(left)
    right_high, right_low = split(right)

    def one(a, b):
        return lax.dot_general(a, b, (dims, ((), ())), preferred_element_type=F32)

    return one(left_high, right_high) + (one(left_high, right_low) + one(left_low, right_high))


def remote(src, dst, send, recv, **where):
    return pltpu.make_async_remote_copy(
        src_ref=src, dst_ref=dst, send_sem=send, recv_sem=recv, device_id=where, device_id_type=MESH
    )


def greet(partners):
    barrier = pltpu.get_barrier_semaphore()
    for where in partners:
        pl.semaphore_signal(barrier, inc=1, device_id=where, device_id_type=MESH)
    pl.semaphore_wait(barrier, len(partners))


def gather_kernel(cols, feat, stacked, held, ring_send, ring_recv, pair_send, pair_recv):
    z = lax.axis_index("col")
    rep = lax.axis_index("rep")
    other = 1 - rep
    half = feat.shape[1] // 2
    steps = cols // 2
    step_of = {0: 1, 1: -1}
    greet(({"col": (z + 1) % cols}, {"col": (z + cols - 1) % cols}, {"rep": other}))

    def put(block, value):
        high, low = split(value)
        width = value.shape[1]
        stacked[block, :width, :width] = high
        stacked[block, :width, width:] = low
        stacked[block, width:, :width] = high
        stacked[block, width:, width:] = jnp.zeros_like(high)

    def rows(chunk):
        return pl.ds(chunk * half, half)

    def ring(way, step, chunk):
        origin = (z - step_of[way] * (step - 1) + cols) % cols
        dst = held.at[origin, rep, rows(chunk)]
        src = feat.at[rep, rows(chunk)] if step == 1 else dst
        return remote(
            src, dst, ring_send.at[way, step - 1, chunk], ring_recv.at[way, step - 1, chunk],
            col=(z + step_of[way] + cols) % cols,
        )

    def arrival(way, step, chunk):
        origin = (z - step_of[way] * step + cols) % cols
        dst = held.at[origin, rep, rows(chunk)]
        return remote(
            dst, dst, ring_send.at[way, step - 1, chunk], ring_recv.at[way, step - 1, chunk],
            col=(z + step_of[way] + cols) % cols,
        )

    def pair(way, step, chunk, core):
        origin = (z - step_of[way] * step + cols) % cols
        dst = held.at[origin, core, rows(chunk)]
        return remote(
            dst, dst, pair_send.at[way, step - 1, chunk], pair_recv.at[way, step - 1, chunk], rep=other
        )

    def messages(step):
        if step < steps:
            return [(way, chunk) for chunk in (0, 1) for way in (0, 1)]
        return [(0, 0), (1, 1)]

    for step in range(1, steps + 1):
        for way, chunk in messages(step):
            if step > 1:
                arrival(way, step - 1, chunk).wait_recv()
            ring(way, step, chunk).start()
            if step > 1:
                pair(way, step - 1, chunk, rep).start()
        if step > 1:
            for way, chunk in messages(step - 1):
                if (way, chunk) not in messages(step):
                    arrival(way, step - 1, chunk).wait_recv()
                    pair(way, step - 1, chunk, rep).start()
        if step == 1:
            for core in (0, 1):
                put(z * 2 + core, feat[core])
        else:
            for way in (0, 1):
                origin = (z - step_of[way] * (step - 1) + cols) % cols
                put(origin * 2 + rep, held[origin, rep])
    for way, chunk in messages(steps):
        arrival(way, steps, chunk).wait_recv()
        pair(way, steps, chunk, rep).start()
    far = (z + steps) % cols
    put(far * 2 + rep, held[far, rep])
    for step in range(1, steps + 1):
        for way, chunk in messages(step):
            pair(way, step, chunk, other).wait_recv()
        for way in (0, 1) if step < steps else (0,):
            origin = (z - step_of[way] * step + cols) % cols
            put(origin * 2 + other, held[origin, other])
    for step in range(1, steps + 1):
        for way, chunk in messages(step):
            ring(way, step, chunk).wait_send()
            pair(way, step, chunk, rep).wait_send()


def gather_features(feat, cols):
    block, width = feat.shape[1:]
    sems = (2, cols // 2, 2)
    return pl.pallas_call(
        functools.partial(gather_kernel, cols),
        out_shape=jax.ShapeDtypeStruct((cols * 2, 2 * width, 2 * width), BF16),
        in_specs=[pl.BlockSpec(memory_space=VMEM)],
        out_specs=pl.BlockSpec(memory_space=VMEM),
        scratch_shapes=[VMEM((cols, 2, block, width), F32), DMA(sems), DMA(sems), DMA(sems), DMA(sems)],
        compiler_params=pltpu.CompilerParams(
            collective_id=0, has_side_effects=True, vmem_limit_bytes=32 * MIB
        ),
        name="gather_features",
    )(feat)


UNROLL = 4


def fetch_own(count, dst, src, tiles, held, dst_list, src_list, sems, dummy):
    rep = lax.axis_index("rep")

    def copy(slot, place):
        return pltpu.make_async_copy(tiles.at[slot], held.at[place], sems.at[place])

    def look(slot, place):
        block = dst[0, 0, slot]
        own = (block & 1) == rep

        @pl.when(own)
        def _():
            copy(slot, place).start()
            dst_list[place] = block >> 1
            src_list[place] = src[0, 0, slot]

        return place + own.astype(jnp.int32)

    total = lax.fori_loop(0, count[0, 0], look, 0)
    groups = (total + (UNROLL - 1)) // UNROLL

    def pad(place, carry):
        copy(0, place).start()
        dst_list[place] = dummy[0]
        src_list[place] = dummy[1]
        return carry

    lax.fori_loop(total, groups * UNROLL, pad, 0)
    return groups, copy


def forward_kernel(count, dst, src, tiles, stacked, sums, held, weight, dst_list, src_list, sems):
    block = held.shape[1]
    live = sums.shape[0] - 1
    groups, copy = fetch_own(count, dst, src, tiles, held, dst_list, src_list, sems, (4 * live, 0))
    sums[...] = jnp.zeros_like(sums)
    weight[...] = jnp.zeros_like(weight)

    def step(group, carry):
        for u in range(UNROLL):
            copy(0, group * UNROLL + u).wait()
        parts = []
        for u in range(UNROLL):
            place = group * UNROLL + u
            tile = held[place]
            high, low = split(tile)
            product = jnp.dot(
                jnp.concatenate([high, low], axis=1), stacked[src_list[place]], preferred_element_type=F32
            )
            target = dst_list[place]
            parts.append((target, product[:, :block] + product[:, block:], tile))
        for target, value, tile in parts:
            sums[target >> 2, target & 3, pl.ds(8, block)] += value
            weight[target] += tile
        return carry

    lax.fori_loop(0, groups, step, 0)
    ones = jnp.ones((8, block), F32)

    def degree(target, carry):
        sums[target >> 2, target & 3, pl.ds(0, 8)] = lax.dot_general(
            ones, weight[target], (((1,), (1,)), ((), ())),
            precision=lax.Precision.HIGHEST, preferred_element_type=F32,
        )
        return carry

    lax.fori_loop(0, 4 * live, degree, 0)


def backward_kernel(count, dst, src, tiles, stacked, sums, held, dst_list, src_list, sems):
    block = held.shape[1]
    live = sums.shape[0] - 1
    groups, copy = fetch_own(count, dst, src, tiles, held, dst_list, src_list, sems, (0, live))
    sums[...] = jnp.zeros_like(sums)

    def step(group, carry):
        for u in range(UNROLL):
            copy(0, group * UNROLL + u).wait()
        parts = []
        for u in range(UNROLL):
            place = group * UNROLL + u
            high, low = split(held[place])
            right = jnp.concatenate(
                [
                    jnp.concatenate([high, low], axis=1),
                    jnp.concatenate([high, jnp.zeros_like(high)], axis=1),
                ],
                axis=0,
            )
            product = jnp.dot(stacked[dst_list[place]], right, preferred_element_type=F32)
            parts.append((src_list[place], product[:, :block] + product[:, block:]))
        for target, value in parts:
            sums[target] += value
        return carry

    lax.fori_loop(0, groups, step, 0)


def tile_call(kernel, name, out_shape, scratch, count, dst, src, tiles, stacked):
    slots, block = tiles.shape[:2]
    padded = slots + UNROLL
    smem = pl.BlockSpec(memory_space=pltpu.SMEM)
    vmem = pl.BlockSpec(memory_space=VMEM)
    return pl.pallas_call(
        kernel,
        out_shape=jax.ShapeDtypeStruct(out_shape, F32),
        in_specs=[smem, smem, smem, pl.BlockSpec(memory_space=pl.ANY), vmem],
        out_specs=vmem,
        scratch_shapes=[VMEM((padded, block, block), F32)]
        + scratch
        + [pltpu.SMEM((padded,), jnp.int32), pltpu.SMEM((padded,), jnp.int32), DMA((padded,))],
        compiler_params=pltpu.CompilerParams(vmem_limit_bytes=40 * MIB),
        name=name,
    )(count, dst, src, tiles, stacked)


SIDE = 4
DEG = 8


def middle_kernel(
    sums, feat, cot, w_self, w_neigh, bias,
    hidden_out, stacked, direct_out, grad_part,
    far1, near1, part1, far2, near2, gathered, hidden_half, hidden_got, direct_half, direct_got,
    grads, grads_got, grads_rows,
    rs_send, rs_recv, ag_send, ag_recv, pair_send, pair_recv, row_send, row_recv,
):
    row = lax.axis_index("row")
    rep = lax.axis_index("rep")
    other = 1 - rep
    rows = SIDE * SIDE
    block = feat.shape[1]
    width = feat.shape[2]
    hid = w_self.shape[1] // 2
    coords = (row % SIDE, row // SIDE)
    peers = [(row + off) % rows for off in range(1, rows)]
    greet([{"row": peer} for peer in peers] + [{"rep": other}])

    def index(axis, first, second):
        return (second, first) if axis == 0 else (first, second)

    def neighbour(axis, way):
        here = (coords[axis] + way + SIDE) % SIDE
        rest = coords[1 - axis]
        y, x = (rest, here) if axis == 0 else (here, rest)
        return y * SIDE + x

    low = block // 2
    spans = ((0, DEG + low), (DEG + low, low))
    cuts = (40, 32)
    ways = (1, -1)

    def line(axis, first, seconds):
        lo, n = spans[axis]
        start, size = seconds
        where = pl.ds(start, size)
        if axis == 0:
            return sums.at[where, first, pl.ds(lo, n)]
        return sums.at[first, where, pl.ds(lo, n)]

    def rs(axis, kind, way):
        first, second = coords[axis], coords[1 - axis]
        n = spans[axis][1]
        w = ways[way]
        mine = (0, 2) if way == 0 else (2, 2)
        rest = (2, 2) if way == 0 else (0, 2)
        sems = (rs_send.at[axis, kind, way], rs_recv.at[axis, kind, way])
        if kind < 3:
            to = neighbour(axis, w)
            if kind == 0:
                src = line(axis, (first + 2) % SIDE, mine)
                dst = far1.at[axis, way, :, pl.ds(0, n)]
            elif kind == 1:
                src = line(axis, (first + w + SIDE) % SIDE, rest)
                dst = near1.at[axis, way, pl.ds(rest[0], 2), pl.ds(0, n)]
            else:
                src = far1.at[axis, way, :, pl.ds(0, n)]
                dst = near1.at[axis, way, pl.ds(mine[0], 2), pl.ds(0, n)]
        else:
            to = neighbour(1 - axis, w)
            cut = cuts[axis]
            if kind == 3:
                lo, size = (0, cut) if way == 0 else (cut, n - cut)
                src = part1.at[axis, (second + 2) % SIDE, pl.ds(lo, size)]
                dst = far2.at[axis, way, pl.ds(0, size)]
            else:
                src = part1.at[axis, (second + w + SIDE) % SIDE, pl.ds(0, n)]
                dst = near2.at[axis, way, pl.ds(0, n)]
        return remote(src, dst, *sems, row=to)

    both = [(axis, way) for axis in (0, 1) for way in (0, 1)]
    for kind in (0, 1):
        for axis, way in both:
            rs(axis, kind, way).start()
    own_feat = feat[rep]
    pre_self = dot3(own_feat, w_self[...]) + bias[...]
    for axis, way in both:
        rs(axis, 0, way).wait_recv()
        first = coords[axis]
        n = spans[axis][1]
        mine = (0, 2) if way == 0 else (2, 2)
        far1[axis, way, :, pl.ds(0, n)] += line(axis, (first + ways[way] + SIDE) % SIDE, mine)[...]
        rs(axis, 2, way).start()
    for axis in (0, 1):
        for way in (0, 1):
            rs(axis, 1, way).wait_recv()
            rs(axis, 2, way).wait_recv()
        first, second = coords[axis], coords[1 - axis]
        lo, n = spans[axis]
        for off in (2, 1, 3, 0):
            at = (second + off) % SIDE
            y, x = index(axis, first, at)
            part1[axis, at, pl.ds(0, n)] = (
                sums[y, x, pl.ds(lo, n)] + near1[axis, 0, at, pl.ds(0, n)] + near1[axis, 1, at, pl.ds(0, n)]
            )
            if off == 2:
                for way in (0, 1):
                    rs(axis, 3, way).start()
    for axis in (0, 1):
        second = coords[1 - axis]
        n = spans[axis][1]
        cut = cuts[axis]
        for way in (0, 1):
            rs(axis, 3, way).wait_recv()
            at = (second + ways[way] + SIDE) % SIDE
            lo, size = (0, cut) if way == 0 else (cut, n - cut)
            part1[axis, at, pl.ds(lo, size)] += far2[axis, way, pl.ds(0, size)]
            rs(axis, 4, way).start()
    summed = []
    for axis in (0, 1):
        n = spans[axis][1]
        for way in (0, 1):
            rs(axis, 4, way).wait_recv()
        second = coords[1 - axis]
        summed.append(
            part1[axis, second, pl.ds(0, n)] + near2[axis, 0, pl.ds(0, n)] + near2[axis, 1, pl.ds(0, n)]
        )
    degree = summed[0][:1]
    inverse = 1.0 / jnp.maximum(degree, 1.0)
    inverse_down = jnp.broadcast_to(inverse, (block, block)).T
    total = jnp.concatenate([summed[0][DEG:], summed[1]], axis=0)
    aggregate = total * inverse_down
    preact = pre_self + dot3(aggregate, w_neigh[...])
    gating = jax.nn.sigmoid(preact)
    grad_pre = cot[rep] * (gating * (1.0 + preact * (1.0 - gating)))
    y0, x0 = coords[1], coords[0]
    gathered[y0, x0] = dot3(w_neigh[...], grad_pre, ((1,), (1,))) * inverse

    quarter = block // 4

    def place(axis, first, second):
        y, x = index(axis, first, second)
        return gathered.at[y, x]

    def ag(axis, kind, way, off=0, arrives=False):
        first, second = coords[axis], coords[1 - axis]
        w = ways[way]
        top = axis * (block // 2)
        if kind % 2 == 0:
            span = pl.ds(top, 2 * quarter)
        else:
            span = pl.ds(top + way * quarter, quarter)
        back = (kind % 2) + (1 if arrives else 0)
        if kind < 2:
            spot = place(axis, (first - w * back + 2 * SIDE) % SIDE, second)
            to = neighbour(axis, w)
            sems = (ag_send.at[axis, kind, way], ag_recv.at[axis, kind, way])
        else:
            spot = place(axis, (first + off) % SIDE, (second - w * back + 2 * SIDE) % SIDE)
            to = neighbour(1 - axis, w)
            at = 2 + (kind - 2) * SIDE + off
            sems = (ag_send.at[axis, at, way], ag_recv.at[axis, at, way])
        ref = spot.at[span]
        return remote(ref, ref, *sems, row=to)

    def convert(y, x):
        value = gathered[y, x]
        high, lo = split(value)
        stacked[y * SIDE + x, :, :block] = high
        stacked[y * SIDE + x, :, block:] = lo

    for axis, way in both:
        ag(axis, 0, way).start()
    for axis, way in both:
        ag(axis, 2, way, 0).start()
    hidden = preact * gating
    grad_self = dot3(own_feat.T, grad_pre)
    grad_neigh = dot3(aggregate.T, grad_pre)
    grad_bias = jnp.sum(grad_pre, axis=0, keepdims=True)
    share = 2 * width // rows
    for core in (0, 1):
        cols = slice(core * hid, (core + 1) * hid)
        hidden_half[core] = hidden[:, cols]
        grads[core, : rows // 2, :share] = grad_self[:, cols].reshape(rows // 2, share, hid)
        grads[core, rows // 2 :, :share] = grad_neigh[:, cols].reshape(rows // 2, share, hid)
        grads[core, :, share:] = jnp.broadcast_to(grad_bias[None, :, cols], (rows, 8, hid))
    grads_pair = remote(grads.at[other], grads_got, pair_send.at[0], pair_recv.at[0], rep=other)
    grads_pair.start()
    hidden_pair = remote(hidden_half.at[other], hidden_got, pair_send.at[1], pair_recv.at[1], rep=other)
    hidden_pair.start()
    for axis, way in both:
        ag(axis, 0, way, arrives=True).wait_recv()
        ag(axis, 1, way).start()
    for axis, way in both:
        off = 3 if way == 0 else 1
        for other_way in (0, 1):
            ag(axis, 2, other_way, off).start()
    direct = dot3(w_self[...], grad_pre, ((1,), (1,)))
    direct_half[...] = direct.reshape(2, width // 2, block)
    direct_pair = remote(direct_half.at[other], direct_got, pair_send.at[2], pair_recv.at[2], rep=other)
    direct_pair.start()
    grads_pair.wait_recv()
    grads[rep] += grads_got[...]
    for slot, peer in enumerate(peers):
        remote(
            grads.at[rep, peer], grads_rows.at[row], row_send.at[slot], row_recv.at[slot], row=peer
        ).start()
    grads_rows[row] = grads[rep, row]
    for axis, way in both:
        ag(axis, 1, way, arrives=True).wait_recv()
    for axis, way in both:
        ag(axis, 2, way, 2).start()
    for off in (0, 3, 1, 2):
        for axis, way in both:
            ag(axis, 2, way, off, arrives=True).wait_recv()
            ag(axis, 3, way, off).start()
    hidden_out[rep] = hidden_half[rep]
    hidden_pair.wait_recv()
    hidden_out[other] = hidden_got[...]
    direct_out[rep] = direct_half[rep]
    direct_pair.wait_recv()
    direct_out[other] = direct_got[...]
    for off in (0, 3, 1, 2):
        for axis, way in both:
            ag(axis, 3, way, off, arrives=True).wait_recv()
    for y in range(SIDE):
        for x in range(SIDE):
            convert(y, x)
    for slot in range(rows - 1):
        sender = (row + rows - (slot + 1)) % rows
        remote(
            grads.at[rep, row], grads_rows.at[sender], row_send.at[slot], row_recv.at[slot], row=peers[slot]
        ).wait_recv()
    value = grads_rows[0]
    for at in range(1, rows):
        value = value + grads_rows[at]
    grad_part[...] = value
    for axis, way in both:
        for kind in range(5):
            rs(axis, kind, way).wait_send()
        for kind in (0, 1):
            ag(axis, kind, way).wait_send()
        for off in range(SIDE):
            for kind in (2, 3):
                ag(axis, kind, way, off).wait_send()
    for copy in (grads_pair, hidden_pair, direct_pair):
        copy.wait_send()
    for slot, peer in enumerate(peers):
        remote(
            grads.at[rep, peer], grads_rows.at[row], row_send.at[slot], row_recv.at[slot], row=peer
        ).wait_send()


def middle(sums, feat, cot, w_self, w_neigh, bias):
    block, width = feat.shape[1:]
    hid = w_self.shape[1] // 2
    rows = SIDE * SIDE
    n = DEG + block // 2
    share = 2 * width // rows + 8
    vmem = pl.BlockSpec(memory_space=VMEM)
    shape = jax.ShapeDtypeStruct
    return pl.pallas_call(
        middle_kernel,
        out_shape=(
            shape((2, block, hid), F32),
            shape((rows, width, 2 * block), BF16),
            shape((2, width // 2, block), F32),
            shape((share, hid), F32),
        ),
        in_specs=[vmem] * 6,
        out_specs=(vmem,) * 4,
        scratch_shapes=[
            VMEM((2, 2, 2, n, width), F32),
            VMEM((2, 2, SIDE, n, width), F32),
            VMEM((2, SIDE, n, width), F32),
            VMEM((2, 2, n, width), F32),
            VMEM((2, 2, n, width), F32),
            VMEM((SIDE, SIDE, width, block), F32),
            VMEM((2, block, hid), F32),
            VMEM((block, hid), F32),
            VMEM((2, width // 2, block), F32),
            VMEM((width // 2, block), F32),
            VMEM((2, rows, share, hid), F32),
            VMEM((rows, share, hid), F32),
            VMEM((rows, share, hid), F32),
            DMA((2, 5, 2)),
            DMA((2, 5, 2)),
            DMA((2, 10, 2)),
            DMA((2, 10, 2)),
            DMA((3,)),
            DMA((3,)),
            DMA((rows - 1,)),
            DMA((rows - 1,)),
        ],
        compiler_params=pltpu.CompilerParams(
            collective_id=1, has_side_effects=True, vmem_limit_bytes=40 * MIB
        ),
        name="middle",
    )(sums, feat, cot, w_self, w_neigh, bias)


def last_kernel(
    cols, factor, sums, direct, grad_part,
    grad_feat, grad_weights, grad_bias,
    own, pair_got, ring_got, col_got, final,
    pair_send, pair_recv, ring_send, ring_recv, col_send, col_recv, row_send, row_recv,
):
    row = lax.axis_index("row")
    z = lax.axis_index("col")
    rep = lax.axis_index("rep")
    other = 1 - rep
    rows = SIDE * SIDE
    half = sums.shape[1] // 2
    share = final.shape[1]
    steps = cols // 2
    ways = (1, -1)
    row_peers = [(row + off) % rows for off in range(1, rows)]
    col_peers = [(z + off) % cols for off in range(1, cols)]
    greet(
        [{"rep": other}]
        + [{"col": peer} for peer in col_peers]
        + [{"row": peer} for peer in row_peers]
    )

    def pair(off):
        at = (z + off) % cols
        return remote(
            sums.at[pl.ds(2 * at, 2), pl.ds(other * half, half)], pair_got.at[at],
            pair_send.at[off], pair_recv.at[off], rep=other,
        )

    def merge(off):
        at = (z + off) % cols
        pair(off).wait_recv()
        own[at] = sums[pl.ds(2 * at, 2), pl.ds(pl.multiple_of(rep * half, half), half)] + pair_got[at]

    def ring(way, step, part):
        at = (z + ways[way] * (steps + 1 - step) + cols) % cols
        return remote(
            own.at[at, part], ring_got.at[way, step - 1, part],
            ring_send.at[way, step - 1, part], ring_recv.at[way, step - 1, part],
            col=(z + ways[way] + cols) % cols,
        )

    def to_col(slot, sender):
        return remote(
            grad_part, col_got.at[sender], col_send.at[slot], col_recv.at[slot], col=col_peers[slot]
        )

    def to_row(slot, sender):
        return remote(
            final.at[sender], final.at[sender], row_send.at[slot], row_recv.at[slot], row=row_peers[slot]
        )

    order = [steps]
    for off in range(steps - 1, 0, -1):
        order += [off, cols - off]
    order.append(0)
    for off in order:
        pair(off).start()
    for slot in range(cols - 1):
        to_col(slot, z).start()
    col_got[z] = grad_part[...]
    merge(steps)
    ring(0, 1, 0).start()
    ring(1, 1, 1).start()
    for step in range(2, steps + 1):
        off = steps + 1 - step
        for way in (0, 1):
            merge(off if way == 0 else cols - off)
        for part in (0, 1):
            for way in (0, 1):
                at = (z + ways[way] * off + cols) % cols
                if step > 2 or part == way:
                    ring(way, step - 1, part).wait_recv()
                    own[at, part] += ring_got[way, step - 2, part]
                ring(way, step, part).start()
        if step == 2:
            for slot in range(cols - 1):
                to_col(slot, (z + cols - (slot + 1)) % cols).wait_recv()
            value = col_got[0]
            for at in range(1, cols):
                value = value + col_got[at]
            value = value * factor
            final[row] = value[:share]
            grad_bias[...] = value[share:]
            for slot in range(rows - 1):
                to_row(slot, row).start()
    merge(0)
    for part in (0, 1):
        for way in (0, 1):
            ring(way, steps, part).wait_recv()
        grad_feat[part] = (
            direct[part] + own[z, part] + ring_got[0, steps - 1, part] + ring_got[1, steps - 1, part]
        )
    for slot in range(rows - 1):
        to_row(slot, (row + rows - (slot + 1)) % rows).wait_recv()
    grad_weights[...] = final[...]
    for off in order:
        pair(off).wait_send()
    for way in (0, 1):
        for step in range(1, steps + 1):
            for part in (0, 1):
                if step > 1 or part == way:
                    ring(way, step, part).wait_send()
    for slot in range(cols - 1):
        to_col(slot, z).wait_send()
    for slot in range(rows - 1):
        to_row(slot, row).wait_send()


def last(sums, direct, grad_part, cols, factor):
    width, block = sums.shape[1:]
    hid = grad_part.shape[1]
    rows = SIDE * SIDE
    share = 2 * width // rows
    vmem = pl.BlockSpec(memory_space=VMEM)
    shape = jax.ShapeDtypeStruct
    return pl.pallas_call(
        functools.partial(last_kernel, cols, factor),
        out_shape=(
            shape((2, width // 2, block), F32),
            shape((rows, share, hid), F32),
            shape((8, hid), F32),
        ),
        in_specs=[vmem] * 3,
        out_specs=(vmem,) * 3,
        scratch_shapes=[
            VMEM((cols, 2, width // 2, block), F32),
            VMEM((cols, 2, width // 2, block), F32),
            VMEM((2, cols // 2, 2, width // 2, block), F32),
            VMEM((cols, share + 8, hid), F32),
            VMEM((rows, share, hid), F32),
            DMA((cols,)),
            DMA((cols,)),
            DMA((2, cols // 2, 2)),
            DMA((2, cols // 2, 2)),
            DMA((cols - 1,)),
            DMA((cols - 1,)),
            DMA((rows - 1,)),
            DMA((rows - 1,)),
        ],
        compiler_params=pltpu.CompilerParams(
            collective_id=2, has_side_effects=True, vmem_limit_bytes=40 * MIB
        ),
        name="last",
    )(sums, direct, grad_part)


def shards(features, cotangent, w_self, w_neigh, bias, tiles, tile_dst, tile_src, tile_count):
    slots, block = tiles.shape[2:4]
    width = features.shape[1]
    hid = w_self.shape[1]
    cols = lax.axis_size("col")
    rows = lax.axis_size("row")
    tiles = tiles.reshape(slots, block, block)
    feat = features.reshape(2, block, width)
    cot = cotangent.reshape(2, block, hid)
    lists = (tile_count, tile_dst, tile_src, tiles)

    stacked = gather_features(feat, cols)
    sums = tile_call(
        forward_kernel, "forward", (SIDE + 1, SIDE, block + DEG, width),
        [VMEM((rows + 1, block, block), F32)], *lists, stacked,
    )
    hidden, scaled, direct, grad_part = middle(sums, feat, cot, w_self, w_neigh, bias.reshape(1, hid))
    back = tile_call(backward_kernel, "backward", (2 * cols + 1, width, block), [], *lists, scaled)
    factor = float(features.shape[0] * rows * cols) ** (-0.5)
    grad_feat, grad_weights, grad_bias = last(back, direct, grad_part, cols, factor)
    grad_weights = grad_weights.reshape(2, width, hid // 2)
    return (
        hidden.reshape(2 * block, hid // 2),
        grad_feat.transpose(0, 2, 1).reshape(2 * block, width // 2),
        grad_weights[0],
        grad_weights[1],
        grad_bias[0],
    )


def solution(mesh):
    return jax.shard_map(
        shards,
        mesh=mesh,
        in_specs=(
            P(("row", "col"), None),
            P(("row", "col"), None),
            P(),
            P(),
            P(),
            P("row", "col", None, None, None),
            P("row", "col", None),
            P("row", "col", None),
            P("row", "col"),
        ),
        out_specs=(
            P(("row", "col"), "rep"),
            P(("row", "col"), "rep"),
            P(None, "rep"),
            P(None, "rep"),
            P("rep"),
        ),
        check_vma=False,
    )
```

```python
import functools

import jax
import jax.numpy as jnp
from jax import lax
from jax.experimental import pallas as pl
from jax.experimental.pallas import tpu as pltpu
from jax.sharding import PartitionSpec as P

MESH = pl.DeviceIdType.MESH
F32 = jnp.float32
BF16 = jnp.bfloat16
VMEM = pltpu.VMEM
DMA = pltpu.SemaphoreType.DMA
MIB = 1 << 20


def split(value):
    high = value.astype(BF16)
    low = (value - high.astype(F32)).astype(BF16)
    return high, low


def dot3(left, right, dims=((1,), (0,))):
    left_high, left_low = left if isinstance(left, tuple) else split(left)
    right_high, right_low = right if isinstance(right, tuple) else split(right)

    def one(a, b):
        return lax.dot_general(a, b, (dims, ((), ())), preferred_element_type=F32)

    return one(left_high, right_high) + (one(left_high, right_low) + one(left_low, right_high))


def remote(src, dst, send, recv, **where):
    return pltpu.make_async_remote_copy(
        src_ref=src, dst_ref=dst, send_sem=send, recv_sem=recv, device_id=where, device_id_type=MESH
    )


def greet(partners):
    barrier = pltpu.get_barrier_semaphore()
    for where in partners:
        pl.semaphore_signal(barrier, inc=1, device_id=where, device_id_type=MESH)
    pl.semaphore_wait(barrier, len(partners))


LIST = 256


def make_lists(count, dst, src, lists, line, dummies):
    rep = lax.axis_index("rep")
    slots = dst.shape[2]
    line[...] = jnp.zeros_like(line)
    line[0:1, :slots] = dst[0]
    line[8:9, :slots] = src[0]
    wide = (8, LIST)
    block = jnp.broadcast_to(line[0:1], wide)
    source = jnp.broadcast_to(line[8:9], wide)
    slot = lax.broadcasted_iota(jnp.int32, wide, 1)
    own = ((block & 1) == rep) & (slot < count[0, 0]) & (slot < slots)
    own = own.astype(jnp.int32).astype(F32)
    square = (LIST, LIST)
    down = lax.broadcasted_iota(jnp.int32, square, 0)
    before = (down < lax.broadcasted_iota(jnp.int32, square, 1)).astype(jnp.int32).astype(F32).astype(BF16)
    place = jnp.dot(own.astype(BF16), before, preferred_element_type=F32)
    place = jnp.where(own > 0.5, place, -1.0)
    total = jnp.broadcast_to(jnp.sum(own, axis=1, keepdims=True), wide)
    chosen = (jnp.broadcast_to(place[0:1], square) == down.astype(F32)).astype(jnp.int32).astype(F32).astype(BF16)
    kind = lax.broadcasted_iota(jnp.int32, wide, 0)
    values = jnp.where(kind == 0, slot, jnp.where(kind % 2 == 1, block >> 1, source)).astype(F32).astype(BF16)
    listed = lax.dot_general(values, chosen, (((1,), (1,)), ((), ())), preferred_element_type=F32)
    beyond = slot.astype(F32) >= total
    listed = jnp.where(beyond & (kind == 3), float(dummies[0]), listed)
    listed = jnp.where(beyond & (kind == 4), float(dummies[1]), listed)
    listed = jnp.where(kind == 5, total, listed)
    lists[...] = listed.astype(jnp.int32)


def gather_kernel(
    cols, dummies, count, dst_far, src_far, feat_far, tiles,
    stacked, lists, tiles_here,
    feat, dst, src, held, line, ring_send, ring_recv, pair_send, pair_recv, load_sems,
):
    loads = [
        pltpu.make_async_copy(far, here, load_sems.at[at])
        for at, (far, here) in enumerate(((feat_far, feat), (dst_far, dst), (src_far, src), (tiles, tiles_here)))
    ]
    for load in loads:
        load.start()
    z = lax.axis_index("col")
    rep = lax.axis_index("rep")
    other = 1 - rep
    half = feat.shape[1] // 2
    steps = cols // 2
    step_of = {0: 1, 1: -1}
    greet(({"col": (z + 1) % cols}, {"col": (z + cols - 1) % cols}, {"rep": other}))
    for load in loads[:3]:
        load.wait()

    def put(block, value):
        high, low = split(value)
        width = value.shape[1]
        stacked[block, :width, :width] = high
        stacked[block, :width, width:] = low
        stacked[block, width:, :width] = high
        stacked[block, width:, width:] = jnp.zeros_like(high)

    def rows(chunk):
        return pl.ds(chunk * half, half)

    def ring(way, step, chunk):
        origin = (z - step_of[way] * (step - 1) + cols) % cols
        dst = held.at[origin, rep, rows(chunk)]
        src = feat.at[rep, rows(chunk)] if step == 1 else dst
        return remote(
            src, dst, ring_send.at[way, step - 1, chunk], ring_recv.at[way, step - 1, chunk],
            col=(z + step_of[way] + cols) % cols,
        )

    def arrival(way, step, chunk):
        origin = (z - step_of[way] * step + cols) % cols
        dst = held.at[origin, rep, rows(chunk)]
        return remote(
            dst, dst, ring_send.at[way, step - 1, chunk], ring_recv.at[way, step - 1, chunk],
            col=(z + step_of[way] + cols) % cols,
        )

    def pair(way, step, chunk, core):
        origin = (z - step_of[way] * step + cols) % cols
        dst = held.at[origin, core, rows(chunk)]
        return remote(
            dst, dst, pair_send.at[way, step - 1, chunk], pair_recv.at[way, step - 1, chunk], rep=other
        )

    def messages(step):
        if step < steps:
            return [(way, chunk) for chunk in (0, 1) for way in (0, 1)]
        return [(0, 0), (1, 1)]

    for step in range(1, steps + 1):
        for way, chunk in messages(step):
            if step > 1:
                arrival(way, step - 1, chunk).wait_recv()
            ring(way, step, chunk).start()
            if step > 1:
                pair(way, step - 1, chunk, rep).start()
        if step > 1:
            for way, chunk in messages(step - 1):
                if (way, chunk) not in messages(step):
                    arrival(way, step - 1, chunk).wait_recv()
                    pair(way, step - 1, chunk, rep).start()
        if step == 1:
            for core in (0, 1):
                put(z * 2 + core, feat[core])
            make_lists(count, dst, src, lists, line, dummies)
        else:
            for way in (0, 1):
                origin = (z - step_of[way] * (step - 1) + cols) % cols
                put(origin * 2 + rep, held[origin, rep])
    for way, chunk in messages(steps):
        arrival(way, steps, chunk).wait_recv()
        pair(way, steps, chunk, rep).start()
    far = (z + steps) % cols
    put(far * 2 + rep, held[far, rep])
    for step in range(1, steps + 1):
        for way, chunk in messages(step):
            pair(way, step, chunk, other).wait_recv()
        for way in (0, 1) if step < steps else (0,):
            origin = (z - step_of[way] * step + cols) % cols
            put(origin * 2 + other, held[origin, other])
    for step in range(1, steps + 1):
        for way, chunk in messages(step):
            ring(way, step, chunk).wait_send()
            pair(way, step, chunk, rep).wait_send()
    loads[3].wait()


def gather_features(count, dst, src, feat, tiles, cols, rows):
    block, width = feat.shape[1:]
    sems = (2, cols // 2, 2)
    vmem = pl.BlockSpec(memory_space=VMEM)
    far = pl.BlockSpec(memory_space=pl.ANY)
    return pl.pallas_call(
        functools.partial(gather_kernel, cols, (rows, 2 * cols)),
        out_shape=(
            jax.ShapeDtypeStruct((cols * 2, 2 * width, 2 * width), BF16),
            jax.ShapeDtypeStruct((8, LIST), jnp.int32),
            VMEM(tiles.shape, F32),
        ),
        in_specs=[pl.BlockSpec(memory_space=pltpu.SMEM), far, far, far, far],
        out_specs=(vmem, vmem, vmem),
        scratch_shapes=[
            VMEM(feat.shape, F32), VMEM(dst.shape, jnp.int32), VMEM(src.shape, jnp.int32),
            VMEM((cols, 2, block, width), F32), VMEM((16, LIST), jnp.int32),
            DMA(sems), DMA(sems), DMA(sems), DMA(sems), DMA((4,)),
        ],
        compiler_params=pltpu.CompilerParams(
            collective_id=0, has_side_effects=True, vmem_limit_bytes=24 * MIB
        ),
        name="gather_features",
    )(*[pltpu.with_memory_space_constraint(x, pltpu.HBM) if x is not count else x for x in (count, dst, src, feat, tiles)])


UNROLL = 16
SLOT, LOAD_DST, LOAD_SRC, ADD_DST, ADD_SRC, TOTAL = range(6)


def group_count(lists):
    return (lists[TOTAL, 0] + (UNROLL - 1)) // UNROLL


def forward_kernel(lists, tiles, stacked, sums, weight):
    block = tiles.shape[1]
    live = sums.shape[0] - 1
    sums[...] = jnp.zeros_like(sums)
    weight[...] = jnp.zeros_like(weight)

    def step(group, carry):
        parts = []
        for u in range(UNROLL):
            place = group * UNROLL + u
            tile = tiles[lists[SLOT, place]]
            high, low = split(tile)
            product = jnp.dot(
                jnp.concatenate([high, low], axis=1), stacked[lists[LOAD_SRC, place]], preferred_element_type=F32
            )
            parts.append((lists[ADD_DST, place], product[:, :block] + product[:, block:], tile))
        for target, value, tile in parts:
            sums[target >> 2, target & 3, pl.ds(8, block)] += value
            weight[target] += tile
        return carry

    lax.fori_loop(0, group_count(lists), step, 0)
    ones = jnp.ones((8, block), F32)
    for target in range(4 * live):
        sums[target >> 2, target & 3, pl.ds(0, 8)] = lax.dot_general(
            ones, weight[target], (((1,), (1,)), ((), ())),
            precision=lax.Precision.HIGHEST, preferred_element_type=F32,
        )


def backward_kernel(lists, tiles, stacked, hidden, sums, hidden_out, out_sem):
    copy = pltpu.make_async_copy(hidden, hidden_out, out_sem)
    copy.start()
    block = tiles.shape[1]
    sums[...] = jnp.zeros_like(sums)

    def step(group, carry):
        parts = []
        for u in range(UNROLL):
            place = group * UNROLL + u
            high, low = split(tiles[lists[SLOT, place]])
            right = jnp.concatenate(
                [
                    jnp.concatenate([high, low], axis=1),
                    jnp.concatenate([high, jnp.zeros_like(high)], axis=1),
                ],
                axis=0,
            )
            product = jnp.dot(stacked[lists[LOAD_DST, place]], right, preferred_element_type=F32)
            parts.append((lists[ADD_SRC, place], product[:, :block] + product[:, block:]))
        for target, value in parts:
            sums[target] += value
        return carry

    lax.fori_loop(0, group_count(lists), step, 0)
    copy.wait()


def forward(lists, tiles, stacked, out_shape):
    vmem = pl.BlockSpec(memory_space=VMEM)
    block = tiles.shape[1]
    return pl.pallas_call(
        forward_kernel,
        out_shape=jax.ShapeDtypeStruct(out_shape, F32),
        in_specs=[pl.BlockSpec(memory_space=pltpu.SMEM), vmem, vmem],
        out_specs=vmem,
        scratch_shapes=[VMEM((4 * out_shape[0] - 3, block, block), F32)],
        compiler_params=pltpu.CompilerParams(vmem_limit_bytes=32 * MIB),
        name="forward",
    )(lists, tiles, stacked)


def backward(lists, tiles, stacked, hidden, out_shape):
    vmem = pl.BlockSpec(memory_space=VMEM)
    shape = jax.ShapeDtypeStruct
    return pl.pallas_call(
        backward_kernel,
        out_shape=(shape(out_shape, F32), shape(hidden.shape, F32)),
        in_specs=[pl.BlockSpec(memory_space=pltpu.SMEM), vmem, vmem, vmem],
        out_specs=(vmem, pl.BlockSpec(memory_space=pl.ANY)),
        scratch_shapes=[DMA],
        compiler_params=pltpu.CompilerParams(vmem_limit_bytes=32 * MIB),
        name="backward",
    )(lists, tiles, stacked, hidden)


SIDE = 4
DEG = 8


def middle_kernel(
    sums, feat, cot, w_self, w_neigh, bias,
    hidden_out, stacked, direct_out, grad_part,
    near1, part1, near2, gathered, hidden_half, hidden_got, direct_half, direct_got,
    grads, grads_got, grads_rows,
    rs_send, rs_recv, ag_send, ag_recv, pair_send, pair_recv, row_send, row_recv,
):
    row = lax.axis_index("row")
    rep = lax.axis_index("rep")
    other = 1 - rep
    rows = SIDE * SIDE
    block = feat.shape[1]
    width = feat.shape[2]
    hid = w_self.shape[1] // 2
    coords = (row % SIDE, row // SIDE)
    peers = [(row + off) % rows for off in range(1, rows)]
    greet([{"row": peer} for peer in peers] + [{"rep": other}])

    low = block // 2
    spans = ((0, DEG + low), (DEG + low, low))
    far_first = (2, 1, 3)

    def at(axis, first, second):
        one = (coords[axis] + first + SIDE) % SIDE
        two = (coords[1 - axis] + second + SIDE) % SIDE
        return (two, one) if axis == 0 else (one, two)

    def device(axis, first, second):
        y, x = at(axis, first, second)
        return y * SIDE + x

    def rs1(axis, off, line):
        lo, n = spans[axis]
        y, x = at(axis, off, line)
        return remote(
            sums.at[y, x, pl.ds(lo, n)], near1.at[axis, off - 1, line, pl.ds(0, n)],
            rs_send.at[axis, line, off - 1], rs_recv.at[axis, line, off - 1], row=device(axis, off, 0),
        )

    def rs2(axis, off):
        n = spans[axis][1]
        return remote(
            part1.at[axis, off, pl.ds(0, n)], near2.at[axis, off - 1, pl.ds(0, n)],
            rs_send.at[axis, SIDE, off - 1], rs_recv.at[axis, SIDE, off - 1], row=device(axis, 0, off),
        )

    lines = far_first + (0,)
    for line in lines:
        for off in far_first:
            for axis in (0, 1):
                rs1(axis, off, line).start()
    own_feat = split(feat[rep])
    self_parts = split(w_self[...])
    neigh_parts = split(w_neigh[...])
    pre_self = dot3(own_feat, self_parts) + bias[...]
    for line in lines:
        for axis in (0, 1):
            for off in far_first:
                rs1(axis, off, line).wait_recv()
            lo, n = spans[axis]
            y, x = at(axis, 0, line)
            span = pl.ds(0, n)
            part1[axis, line, span] = (sums[y, x, pl.ds(lo, n)] + near1[axis, 0, line, span]) + (
                near1[axis, 1, line, span] + near1[axis, 2, line, span]
            )
            if line:
                rs2(axis, line).start()
    summed = []
    for axis in (0, 1):
        for off in far_first:
            rs2(axis, off).wait_recv()
        span = pl.ds(0, spans[axis][1])
        summed.append(
            (part1[axis, 0, span] + near2[axis, 0, span]) + (near2[axis, 1, span] + near2[axis, 2, span])
        )
    degree = summed[0][:1]
    inverse = 1.0 / jnp.maximum(degree, 1.0)
    inverse_down = jnp.broadcast_to(inverse, (block, block)).T
    total = jnp.concatenate([summed[0][DEG:], summed[1]], axis=0)
    aggregate = total * inverse_down
    preact = pre_self + dot3(aggregate, neigh_parts)
    gating = jax.nn.sigmoid(preact)
    grad_pre = cot[rep] * (gating * (1.0 + preact * (1.0 - gating)))
    grad_parts = split(grad_pre)
    y0, x0 = coords[1], coords[0]
    scaled = dot3(neigh_parts, grad_parts, ((1,), (1,))) * inverse
    gathered[y0, x0] = scaled

    def half_of(axis, first, second):
        y, x = at(axis, first, second)
        return gathered.at[y, x, pl.ds(axis * low, low)]

    def ag1(axis, off, arrives=False):
        ref = half_of(axis, -off if arrives else 0, 0)
        return remote(
            ref, ref, ag_send.at[axis, 0, off - 1], ag_recv.at[axis, 0, off - 1], row=device(axis, off, 0)
        )

    def ag2(axis, back, off, arrives=False):
        ref = half_of(axis, -back, -off if arrives else 0)
        return remote(
            ref, ref, ag_send.at[axis, 1 + back, off - 1], ag_recv.at[axis, 1 + back, off - 1],
            row=device(axis, 0, off),
        )

    def convert(axis, first, second):
        y, x = at(axis, first, second)
        span = pl.ds(axis * low, low)
        high, small = split(gathered[y, x, span])
        stacked[y * SIDE + x, span, :block] = high
        stacked[y * SIDE + x, span, block:] = small

    for off in far_first:
        for axis in (0, 1):
            ag1(axis, off).start()
    for off in far_first:
        for axis in (0, 1):
            ag2(axis, 0, off).start()
    hidden = preact * gating
    for core in (0, 1):
        hidden_half[core] = hidden[:, core * hid : (core + 1) * hid]
    hidden_pair = remote(hidden_half.at[other], hidden_got, pair_send.at[1], pair_recv.at[1], rep=other)
    hidden_pair.start()
    grad_self = dot3(feat[rep].T, grad_parts)
    grad_neigh = dot3(aggregate.T, grad_parts)
    grad_bias = jnp.sum(grad_pre, axis=0, keepdims=True)
    share = 2 * width // rows
    for core in (0, 1):
        cols = slice(core * hid, (core + 1) * hid)
        grads[core, : rows // 2, :share] = grad_self[:, cols].reshape(rows // 2, share, hid)
        grads[core, rows // 2 :, :share] = grad_neigh[:, cols].reshape(rows // 2, share, hid)
        grads[core, :, share:] = jnp.broadcast_to(grad_bias[None, :, cols], (rows, 8, hid))
    grads_pair = remote(grads.at[other], grads_got, pair_send.at[0], pair_recv.at[0], rep=other)
    grads_pair.start()
    for off in (1, 3, 2):
        for axis in (0, 1):
            ag1(axis, off, arrives=True).wait_recv()
            for ahead in far_first:
                ag2(axis, off, ahead).start()
    direct = dot3(self_parts, grad_parts, ((1,), (1,)))
    direct_half[...] = direct.reshape(2, width // 2, block)
    direct_pair = remote(direct_half.at[other], direct_got, pair_send.at[2], pair_recv.at[2], rep=other)
    direct_pair.start()
    grads_pair.wait_recv()
    grads[rep] += grads_got[...]
    for slot, peer in enumerate(peers):
        remote(
            grads.at[rep, peer], grads_rows.at[row], row_send.at[slot], row_recv.at[slot], row=peer
        ).start()
    grads_rows[row] = grads[rep, row]
    hidden_out[rep] = hidden_half[rep]
    direct_out[rep] = direct_half[rep]
    for axis in (0, 1):
        for off in (0, 1, 3, 2):
            convert(axis, -off, 0)
    hidden_pair.wait_recv()
    hidden_out[other] = hidden_got[...]
    direct_pair.wait_recv()
    direct_out[other] = direct_got[...]
    for back in (0, 1, 3, 2):
        for ahead in (1, 3, 2):
            for axis in (0, 1):
                ag2(axis, back, ahead, arrives=True).wait_recv()
                convert(axis, -back, -ahead)
    for slot in range(rows - 1):
        sender = (row + rows - (slot + 1)) % rows
        remote(
            grads.at[rep, row], grads_rows.at[sender], row_send.at[slot], row_recv.at[slot], row=peers[slot]
        ).wait_recv()
    value = grads_rows[0]
    for place in range(1, rows):
        value = value + grads_rows[place]
    grad_part[...] = value
    for axis in (0, 1):
        for off in far_first:
            for line in lines:
                rs1(axis, off, line).wait_send()
                ag2(axis, line, off).wait_send()
            rs2(axis, off).wait_send()
            ag1(axis, off).wait_send()
    for copy in (grads_pair, hidden_pair, direct_pair):
        copy.wait_send()
    for slot, peer in enumerate(peers):
        remote(
            grads.at[rep, peer], grads_rows.at[row], row_send.at[slot], row_recv.at[slot], row=peer
        ).wait_send()


def middle(sums, feat, cot, w_self, w_neigh, bias):
    block, width = feat.shape[1:]
    hid = w_self.shape[1] // 2
    rows = SIDE * SIDE
    n = DEG + block // 2
    share = 2 * width // rows + 8
    vmem = pl.BlockSpec(memory_space=VMEM)
    shape = jax.ShapeDtypeStruct
    return pl.pallas_call(
        middle_kernel,
        out_shape=(
            shape((2, block, hid), F32),
            shape((rows, width, 2 * block), BF16),
            shape((2, width // 2, block), F32),
            shape((share, hid), F32),
        ),
        in_specs=[vmem] * 6,
        out_specs=(vmem,) * 4,
        scratch_shapes=[
            VMEM((2, SIDE - 1, SIDE, n, width), F32),
            VMEM((2, SIDE, n, width), F32),
            VMEM((2, SIDE - 1, n, width), F32),
            VMEM((SIDE, SIDE, width, block), F32),
            VMEM((2, block, hid), F32),
            VMEM((block, hid), F32),
            VMEM((2, width // 2, block), F32),
            VMEM((width // 2, block), F32),
            VMEM((2, rows, share, hid), F32),
            VMEM((rows, share, hid), F32),
            VMEM((rows, share, hid), F32),
            DMA((2, SIDE + 1, SIDE - 1)),
            DMA((2, SIDE + 1, SIDE - 1)),
            DMA((2, SIDE + 1, SIDE - 1)),
            DMA((2, SIDE + 1, SIDE - 1)),
            DMA((3,)),
            DMA((3,)),
            DMA((rows - 1,)),
            DMA((rows - 1,)),
        ],
        compiler_params=pltpu.CompilerParams(
            collective_id=1, has_side_effects=True, vmem_limit_bytes=20 * MIB
        ),
        name="middle",
    )(sums, feat, cot, w_self, w_neigh, bias)


def last_kernel(
    cols, factor, sums, direct, grad_part,
    grad_feat, grad_weights, grad_bias,
    own, pair_got, ring_got, col_got, final,
    pair_send, pair_recv, ring_send, ring_recv, col_send, col_recv, row_send, row_recv,
):
    row = lax.axis_index("row")
    z = lax.axis_index("col")
    rep = lax.axis_index("rep")
    other = 1 - rep
    rows = SIDE * SIDE
    half = sums.shape[1] // 2
    share = final.shape[1]
    steps = cols // 2
    ways = (1, -1)
    row_peers = [(row + off) % rows for off in range(1, rows)]
    col_peers = [(z + off) % cols for off in range(1, cols)]
    greet(
        [{"rep": other}]
        + [{"col": peer} for peer in col_peers]
        + [{"row": peer} for peer in row_peers]
    )

    def pair(off):
        at = (z + off) % cols
        return remote(
            sums.at[pl.ds(2 * at, 2), pl.ds(other * half, half)], pair_got.at[at],
            pair_send.at[off], pair_recv.at[off], rep=other,
        )

    def merge(off):
        at = (z + off) % cols
        pair(off).wait_recv()
        own[at] = sums[pl.ds(2 * at, 2), pl.ds(pl.multiple_of(rep * half, half), half)] + pair_got[at]

    def ring(way, step, part):
        at = (z + ways[way] * (steps + 1 - step) + cols) % cols
        return remote(
            own.at[at, part], ring_got.at[way, step - 1, part],
            ring_send.at[way, step - 1, part], ring_recv.at[way, step - 1, part],
            col=(z + ways[way] + cols) % cols,
        )

    def to_col(slot, sender):
        return remote(
            grad_part, col_got.at[sender], col_send.at[slot], col_recv.at[slot], col=col_peers[slot]
        )

    def to_row(slot, sender):
        return remote(
            final.at[sender], final.at[sender], row_send.at[slot], row_recv.at[slot], row=row_peers[slot]
        )

    order = [steps]
    for off in range(steps - 1, 0, -1):
        order += [off, cols - off]
    order.append(0)
    for off in order:
        pair(off).start()
    col_got[z] = grad_part[...]
    merge(steps)
    ring(0, 1, 0).start()
    ring(1, 1, 1).start()
    for slot in range(cols - 1):
        to_col(slot, z).start()
    for step in range(2, steps + 1):
        off = steps + 1 - step
        for way in (0, 1):
            merge(off if way == 0 else cols - off)
        for part in (0, 1):
            for way in (0, 1):
                at = (z + ways[way] * off + cols) % cols
                if step > 2 or part == way:
                    ring(way, step - 1, part).wait_recv()
                    own[at, part] += ring_got[way, step - 2, part]
                ring(way, step, part).start()
        if step == 3:
            for slot in range(cols - 1):
                to_col(slot, (z + cols - (slot + 1)) % cols).wait_recv()
            value = col_got[0]
            for at in range(1, cols):
                value = value + col_got[at]
            value = value * factor
            final[row] = value[:share]
            grad_bias[...] = value[share:]
            for slot in range(rows - 1):
                to_row(slot, row).start()
    merge(0)
    for part in (0, 1):
        for way in (0, 1):
            ring(way, steps, part).wait_recv()
        grad_feat[part] = (
            direct[part] + own[z, part] + ring_got[0, steps - 1, part] + ring_got[1, steps - 1, part]
        )
    for slot in range(rows - 1):
        to_row(slot, (row + rows - (slot + 1)) % rows).wait_recv()
    grad_weights[...] = final[...]
    for off in order:
        pair(off).wait_send()
    for way in (0, 1):
        for step in range(1, steps + 1):
            for part in (0, 1):
                if step > 1 or part == way:
                    ring(way, step, part).wait_send()
    for slot in range(cols - 1):
        to_col(slot, z).wait_send()
    for slot in range(rows - 1):
        to_row(slot, row).wait_send()


def last(sums, direct, grad_part, cols, factor):
    width, block = sums.shape[1:]
    hid = grad_part.shape[1]
    rows = SIDE * SIDE
    share = 2 * width // rows
    vmem = pl.BlockSpec(memory_space=VMEM)
    return pl.pallas_call(
        functools.partial(last_kernel, cols, factor),
        out_shape=(
            VMEM((2, width // 2, block), F32),
            VMEM((rows, share, hid), F32),
            VMEM((8, hid), F32),
        ),
        in_specs=[vmem] * 3,
        out_specs=(vmem,) * 3,
        scratch_shapes=[
            VMEM((cols, 2, width // 2, block), F32),
            VMEM((cols, 2, width // 2, block), F32),
            VMEM((2, cols // 2, 2, width // 2, block), F32),
            VMEM((cols, share + 8, hid), F32),
            VMEM((rows, share, hid), F32),
            DMA((cols,)),
            DMA((cols,)),
            DMA((2, cols // 2, 2)),
            DMA((2, cols // 2, 2)),
            DMA((cols - 1,)),
            DMA((cols - 1,)),
            DMA((rows - 1,)),
            DMA((rows - 1,)),
        ],
        compiler_params=pltpu.CompilerParams(
            collective_id=2, has_side_effects=True, vmem_limit_bytes=16 * MIB
        ),
        name="last",
    )(sums, direct, grad_part)


def finish_kernel(grad_feat, grad_weights, grad_bias, feat_out, self_out, neigh_out, bias_out, sems):
    block = grad_feat.shape[2]
    pieces = [
        (grad_feat.at[0], feat_out.at[:, pl.ds(0, block)]),
        (grad_feat.at[1], feat_out.at[:, pl.ds(block, block)]),
        (grad_weights.at[0], self_out),
        (grad_weights.at[1], neigh_out),
        (grad_bias.at[pl.ds(0, 1)], bias_out),
    ]
    copies = [pltpu.make_async_copy(src, dst, sems.at[at]) for at, (src, dst) in enumerate(pieces)]
    for copy in copies:
        copy.start()
    for copy in copies:
        copy.wait()


def finish(grad_feat, grad_weights, grad_bias):
    half, block = grad_feat.shape[1:]
    hid = grad_bias.shape[1]
    vmem = pl.BlockSpec(memory_space=VMEM)
    far = pl.BlockSpec(memory_space=pl.ANY)
    shape = jax.ShapeDtypeStruct
    return pl.pallas_call(
        finish_kernel,
        out_shape=(
            shape((half, 2 * block), F32), shape((2 * half, hid), F32), shape((2 * half, hid), F32), shape((1, hid), F32)
        ),
        in_specs=[vmem] * 3,
        out_specs=(far,) * 4,
        scratch_shapes=[DMA((5,))],
        name="finish",
    )(grad_feat, grad_weights.reshape(2, 2 * half, hid), grad_bias)


def shards(features, cotangent, w_self, w_neigh, bias, tiles, tile_dst, tile_src, tile_count):
    slots, block = tiles.shape[2:4]
    width = features.shape[1]
    hid = w_self.shape[1]
    cols = lax.axis_size("col")
    rows = lax.axis_size("row")
    tiles = tiles.reshape(slots, block, block)
    feat = features.reshape(2, block, width)
    cot = cotangent.reshape(2, block, hid)

    stacked, lists, tiles = gather_features(tile_count, tile_dst, tile_src, feat, tiles, cols, rows)
    sums = forward(lists, tiles, stacked, (SIDE + 1, SIDE, block + DEG, width))
    hidden, scaled, direct, grad_part = middle(sums, feat, cot, w_self, w_neigh, bias.reshape(1, hid))
    back, hidden = backward(lists, tiles, scaled, hidden, (2 * cols + 1, width, block))
    factor = float(features.shape[0] * rows * cols) ** (-0.5)
    grad_feat, grad_self, grad_neigh, grad_bias = finish(*last(back, direct, grad_part, cols, factor))
    return (
        hidden.reshape(2 * block, hid // 2), grad_feat.T, grad_self, grad_neigh, grad_bias.reshape(hid // 2)
    )


def solution(mesh):
    return jax.shard_map(
        shards,
        mesh=mesh,
        in_specs=(
            P(("row", "col"), None),
            P(("row", "col"), None),
            P(),
            P(),
            P(),
            P("row", "col", None, None, None),
            P("row", "col", None),
            P("row", "col", None),
            P("row", "col"),
        ),
        out_specs=(
            P(("row", "col"), "rep"),
            P(("row", "col"), "rep"),
            P(None, "rep"),
            P(None, "rep"),
            P("rep"),
        ),
        check_vma=False,
    )
```

```python
import functools

import jax
import jax.numpy as jnp
from jax import lax
from jax.experimental import pallas as pl
from jax.experimental.pallas import tpu as pltpu
from jax.sharding import PartitionSpec as P

MESH = pl.DeviceIdType.MESH
F32 = jnp.float32
BF16 = jnp.bfloat16
VMEM = pltpu.VMEM
DMA = pltpu.SemaphoreType.DMA
MIB = 1 << 20


def split(value):
    high = value.astype(BF16)
    low = (value - high.astype(F32)).astype(BF16)
    return high, low


def dot3(left, right, dims=((1,), (0,))):
    left_high, left_low = left if isinstance(left, tuple) else split(left)
    right_high, right_low = right if isinstance(right, tuple) else split(right)

    def one(a, b):
        return lax.dot_general(a, b, (dims, ((), ())), preferred_element_type=F32)

    return one(left_high, right_high) + (one(left_high, right_low) + one(left_low, right_high))


def remote(src, dst, send, recv, **where):
    return pltpu.make_async_remote_copy(
        src_ref=src, dst_ref=dst, send_sem=send, recv_sem=recv, device_id=where, device_id_type=MESH
    )


def greet(partners):
    barrier = pltpu.get_barrier_semaphore()
    for where in partners:
        pl.semaphore_signal(barrier, inc=1, device_id=where, device_id_type=MESH)
    pl.semaphore_wait(barrier, len(partners))


LIST = 256


def make_lists(count, dst, src, lists, line, dummies):
    rep = lax.axis_index("rep")
    slots = dst.shape[2]
    line[...] = jnp.zeros_like(line)
    line[0:1, :slots] = dst[0]
    line[8:9, :slots] = src[0]
    wide = (8, LIST)
    block = jnp.broadcast_to(line[0:1], wide)
    source = jnp.broadcast_to(line[8:9], wide)
    slot = lax.broadcasted_iota(jnp.int32, wide, 1)
    own = ((block & 1) == rep) & (slot < count[0, 0]) & (slot < slots)
    own = own.astype(jnp.int32).astype(F32)
    square = (LIST, LIST)
    down = lax.broadcasted_iota(jnp.int32, square, 0)
    before = (down < lax.broadcasted_iota(jnp.int32, square, 1)).astype(jnp.int32).astype(F32).astype(BF16)
    place = jnp.dot(own.astype(BF16), before, preferred_element_type=F32)
    place = jnp.where(own > 0.5, place, -1.0)
    total = jnp.broadcast_to(jnp.sum(own, axis=1, keepdims=True), wide)
    chosen = (jnp.broadcast_to(place[0:1], square) == down.astype(F32)).astype(jnp.int32).astype(F32).astype(BF16)
    kind = lax.broadcasted_iota(jnp.int32, wide, 0)
    values = jnp.where(kind == 0, slot, jnp.where(kind % 2 == 1, block >> 1, source)).astype(F32).astype(BF16)
    listed = lax.dot_general(values, chosen, (((1,), (1,)), ((), ())), preferred_element_type=F32)
    beyond = slot.astype(F32) >= total
    listed = jnp.where(beyond & (kind == 3), float(dummies[0]), listed)
    listed = jnp.where(beyond & (kind == 4), float(dummies[1]), listed)
    listed = jnp.where(kind == 5, total, listed)
    lists[...] = listed.astype(jnp.int32)


def gather_kernel(
    cols, dummies, count, dst_far, src_far, feat_far, tiles,
    stacked, lists, tiles_here,
    feat, dst, src, held, line, ring_send, ring_recv, pair_send, pair_recv, load_sems,
):
    loads = [
        pltpu.make_async_copy(far, here, load_sems.at[at])
        for at, (far, here) in enumerate(((feat_far, feat), (dst_far, dst), (src_far, src), (tiles, tiles_here)))
    ]
    for load in loads:
        load.start()
    z = lax.axis_index("col")
    rep = lax.axis_index("rep")
    other = 1 - rep
    rows = feat.shape[1]
    ways = (1, -1)
    greet([{"col": (z + off + cols) % cols} for off in (1, -1, 2, -2)] + [{"rep": other}])
    for load in loads[:3]:
        load.wait()

    def put(block, value):
        high, low = split(value)
        width = value.shape[1]
        stacked[block, :width, :width] = high
        stacked[block, :width, width:] = low
        stacked[block, width:, :width] = high
        stacked[block, width:, width:] = jnp.zeros_like(high)

    hops = (1, 2, 1, 2)

    def spot(way, kind, core, steps):
        origin = (z - ways[way] * steps + cols) % cols
        if kind < 3:
            return held.at[origin, core]
        return held.at[origin, core, pl.ds(way * (rows // 2), rows // 2)]

    def ring(way, kind, arrives=False):
        back = 2 * (kind // 2)
        dst = spot(way, kind, rep, back + (hops[kind] if arrives else 0))
        src = feat.at[rep] if kind < 2 and not arrives else dst
        return remote(
            src, dst, ring_send.at[way, kind], ring_recv.at[way, kind],
            col=(z + ways[way] * hops[kind] + cols) % cols,
        )

    def pair(way, kind, core):
        dst = spot(way, kind, core, 2 * (kind // 2) + hops[kind])
        return remote(dst, dst, pair_send.at[way, kind], pair_recv.at[way, kind], rep=other)

    def take(kind, way, core):
        steps = 2 * (kind // 2) + hops[kind]
        origin = (z - ways[way] * steps + cols) % cols
        put(origin * 2 + core, held[origin, core])

    for kind in (1, 0):
        for way in (0, 1):
            ring(way, kind).start()
    for way in (0, 1):
        ring(way, 1, arrives=True).wait_recv()
        for kind in (3, 2):
            ring(way, kind).start()
    for kind in (0, 1):
        for way in (0, 1):
            if kind == 0:
                ring(way, kind, arrives=True).wait_recv()
            pair(way, kind, rep).start()
    for core in (0, 1):
        put(z * 2 + core, feat[core])
    make_lists(count, dst, src, lists, line, dummies)
    for kind in (0, 1):
        for way in (0, 1):
            take(kind, way, rep)
    for kind in (2, 3):
        for way in (0, 1):
            ring(way, kind, arrives=True).wait_recv()
            pair(way, kind, rep).start()
    for kind in (0, 1):
        for way in (0, 1):
            pair(way, kind, other).wait_recv()
            take(kind, way, other)
    for way in (0, 1):
        take(2, way, rep)
    take(3, 0, rep)
    for kind in (2, 3):
        for way in (0, 1):
            pair(way, kind, other).wait_recv()
            if kind == 2 or way == 1:
                take(kind, way, other)
    for kind in range(4):
        for way in (0, 1):
            ring(way, kind).wait_send()
            pair(way, kind, rep).wait_send()
    loads[3].wait()


def gather_features(count, dst, src, feat, tiles, cols, rows):
    block, width = feat.shape[1:]
    sems = (2, 4)
    vmem = pl.BlockSpec(memory_space=VMEM)
    far = pl.BlockSpec(memory_space=pl.ANY)
    return pl.pallas_call(
        functools.partial(gather_kernel, cols, (rows, 2 * cols)),
        out_shape=(
            jax.ShapeDtypeStruct((cols * 2, 2 * width, 2 * width), BF16),
            jax.ShapeDtypeStruct((8, LIST), jnp.int32),
            VMEM(tiles.shape, F32),
        ),
        in_specs=[pl.BlockSpec(memory_space=pltpu.SMEM), far, far, far, far],
        out_specs=(vmem, vmem, vmem),
        scratch_shapes=[
            VMEM(feat.shape, F32), VMEM(dst.shape, jnp.int32), VMEM(src.shape, jnp.int32),
            VMEM((cols, 2, block, width), F32), VMEM((16, LIST), jnp.int32),
            DMA(sems), DMA(sems), DMA(sems), DMA(sems), DMA((4,)),
        ],
        compiler_params=pltpu.CompilerParams(
            collective_id=0, has_side_effects=True, vmem_limit_bytes=24 * MIB
        ),
        name="gather_features",
    )(*[pltpu.with_memory_space_constraint(x, pltpu.HBM) if x is not count else x for x in (count, dst, src, feat, tiles)])


LARGE, SMALL = 32, 8
SLOT, LOAD_DST, LOAD_SRC, ADD_DST, ADD_SRC, TOTAL = range(6)


def over_tiles(lists, step):
    total = lists[TOTAL, 0]
    large = total // LARGE

    def run(size, start):
        def body(group, carry):
            step(start + group * size, size)
            return carry

        return body

    lax.fori_loop(0, large, run(LARGE, 0), 0)
    rest = total - large * LARGE
    lax.fori_loop(0, (rest + (SMALL - 1)) // SMALL, run(SMALL, large * LARGE), 0)


def forward_kernel(lists, tiles, stacked, sums, weight):
    block = tiles.shape[1]
    live = sums.shape[0] - 1
    sums[...] = jnp.zeros_like(sums)
    weight[...] = jnp.zeros_like(weight)

    def step(start, size):
        parts = []
        for u in range(size):
            place = start + u
            tile = tiles[lists[SLOT, place]]
            high, low = split(tile)
            product = jnp.dot(
                jnp.concatenate([high, low], axis=1), stacked[lists[LOAD_SRC, place]], preferred_element_type=F32
            )
            parts.append((lists[ADD_DST, place], product[:, :block] + product[:, block:], tile))
        for target, value, tile in parts:
            sums[target >> 2, target & 3, pl.ds(8, block)] += value
            weight[target] += tile

    over_tiles(lists, step)
    for target in range(4 * live):
        degree = jnp.sum(weight[target].T, axis=0, keepdims=True)
        sums[target >> 2, target & 3, pl.ds(0, 8)] = jnp.broadcast_to(degree, (8, block))


def backward_kernel(lists, tiles, stacked, hidden, sums, hidden_out, out_sem):
    copy = pltpu.make_async_copy(hidden, hidden_out, out_sem)
    copy.start()
    block = tiles.shape[1]
    sums[...] = jnp.zeros_like(sums)

    def step(start, size):
        parts = []
        for u in range(size):
            place = start + u
            high, low = split(tiles[lists[SLOT, place]])
            right = jnp.concatenate(
                [
                    jnp.concatenate([high, low], axis=1),
                    jnp.concatenate([high, jnp.zeros_like(high)], axis=1),
                ],
                axis=0,
            )
            product = jnp.dot(stacked[lists[LOAD_DST, place]], right, preferred_element_type=F32)
            parts.append((lists[ADD_SRC, place], product[:, :block] + product[:, block:]))
        for target, value in parts:
            sums[target] += value

    over_tiles(lists, step)
    copy.wait()


def forward(lists, tiles, stacked, out_shape):
    vmem = pl.BlockSpec(memory_space=VMEM)
    block = tiles.shape[1]
    return pl.pallas_call(
        forward_kernel,
        out_shape=jax.ShapeDtypeStruct(out_shape, F32),
        in_specs=[pl.BlockSpec(memory_space=pltpu.SMEM), vmem, vmem],
        out_specs=vmem,
        scratch_shapes=[VMEM((4 * out_shape[0] - 3, block, block), F32)],
        compiler_params=pltpu.CompilerParams(vmem_limit_bytes=32 * MIB),
        name="forward",
    )(lists, tiles, stacked)


def backward(lists, tiles, stacked, hidden, out_shape):
    vmem = pl.BlockSpec(memory_space=VMEM)
    shape = jax.ShapeDtypeStruct
    return pl.pallas_call(
        backward_kernel,
        out_shape=(shape(out_shape, F32), shape(hidden.shape, F32)),
        in_specs=[pl.BlockSpec(memory_space=pltpu.SMEM), vmem, vmem, vmem],
        out_specs=(vmem, pl.BlockSpec(memory_space=pl.ANY)),
        scratch_shapes=[DMA],
        compiler_params=pltpu.CompilerParams(vmem_limit_bytes=32 * MIB),
        name="backward",
    )(lists, tiles, stacked, hidden)


SIDE = 4
DEG = 8


def middle_kernel(
    sums, feat, cot, w_self, w_neigh, bias,
    hidden_out, stacked, direct_out, grad_part,
    near1, part1, near2, gathered, hidden_half, hidden_got, direct_half, direct_got,
    grads, grads_got, grads_col,
    rs_send, rs_recv, ag_send, ag_recv, pair_send, pair_recv, col_send, col_recv,
):
    row = lax.axis_index("row")
    rep = lax.axis_index("rep")
    other = 1 - rep
    rows = SIDE * SIDE
    block = feat.shape[1]
    width = feat.shape[2]
    hid = w_self.shape[1] // 2
    coords = (row % SIDE, row // SIDE)
    low = block // 2
    spans = ((0, DEG + low), (DEG + low, low))
    far_first = (2, 1, 3)

    def at(axis, first, second):
        one = (coords[axis] + first + SIDE) % SIDE
        two = (coords[1 - axis] + second + SIDE) % SIDE
        return (two, one) if axis == 0 else (one, two)

    def device(axis, first, second):
        y, x = at(axis, first, second)
        return y * SIDE + x

    z = lax.axis_index("col")
    cols = grads.shape[1]
    around = (4, 3, 5, 2, 6, 1, 7)
    greet(
        [{"row": device(axis, off, 0)} for axis in (0, 1) for off in far_first]
        + [{"col": (z + off) % cols} for off in around]
        + [{"rep": other}]
    )

    def rs1(axis, off, line):
        lo, n = spans[axis]
        y, x = at(axis, off, line)
        return remote(
            sums.at[y, x, pl.ds(lo, n)], near1.at[axis, off - 1, line, pl.ds(0, n)],
            rs_send.at[axis, line, off - 1], rs_recv.at[axis, line, off - 1], row=device(axis, off, 0),
        )

    def rs2(axis, off):
        n = spans[axis][1]
        return remote(
            part1.at[axis, off, pl.ds(0, n)], near2.at[axis, off - 1, pl.ds(0, n)],
            rs_send.at[axis, SIDE, off - 1], rs_recv.at[axis, SIDE, off - 1], row=device(axis, 0, off),
        )

    lines = far_first + (0,)
    for line in lines:
        for off in far_first:
            for axis in (0, 1):
                rs1(axis, off, line).start()
    own_feat = split(feat[rep])
    self_parts = split(w_self[...])
    neigh_parts = split(w_neigh[...])
    pre_self = dot3(own_feat, self_parts) + bias[...]
    for line in lines:
        for axis in (0, 1):
            for off in far_first:
                rs1(axis, off, line).wait_recv()
            lo, n = spans[axis]
            y, x = at(axis, 0, line)
            span = pl.ds(0, n)
            part1[axis, line, span] = (sums[y, x, pl.ds(lo, n)] + near1[axis, 0, line, span]) + (
                near1[axis, 1, line, span] + near1[axis, 2, line, span]
            )
            if line:
                rs2(axis, line).start()
    summed = []
    for axis in (0, 1):
        for off in far_first:
            rs2(axis, off).wait_recv()
        span = pl.ds(0, spans[axis][1])
        summed.append(
            (part1[axis, 0, span] + near2[axis, 0, span]) + (near2[axis, 1, span] + near2[axis, 2, span])
        )
    degree = summed[0][:1]
    inverse = 1.0 / jnp.maximum(degree, 1.0)
    inverse_down = jnp.broadcast_to(inverse, (block, block)).T
    total = jnp.concatenate([summed[0][DEG:], summed[1]], axis=0)
    aggregate = total * inverse_down
    preact = pre_self + dot3(aggregate, neigh_parts)
    gating = jax.nn.sigmoid(preact)
    grad_pre = cot[rep] * (gating * (1.0 + preact * (1.0 - gating)))
    grad_parts = split(grad_pre)
    y0, x0 = coords[1], coords[0]
    scaled = dot3(neigh_parts, grad_parts, ((1,), (1,))) * inverse
    gathered[y0, x0] = scaled

    def half_of(axis, first, second):
        y, x = at(axis, first, second)
        return gathered.at[y, x, pl.ds(axis * low, low)]

    def ag1(axis, off, arrives=False):
        ref = half_of(axis, -off if arrives else 0, 0)
        return remote(
            ref, ref, ag_send.at[axis, 0, off - 1], ag_recv.at[axis, 0, off - 1], row=device(axis, off, 0)
        )

    def ag2(axis, back, off, arrives=False):
        ref = half_of(axis, -back, -off if arrives else 0)
        return remote(
            ref, ref, ag_send.at[axis, 1 + back, off - 1], ag_recv.at[axis, 1 + back, off - 1],
            row=device(axis, 0, off),
        )

    def convert(axis, first, second):
        y, x = at(axis, first, second)
        span = pl.ds(axis * low, low)
        high, small = split(gathered[y, x, span])
        stacked[y * SIDE + x, span, :block] = high
        stacked[y * SIDE + x, span, block:] = small

    for off in far_first:
        for axis in (0, 1):
            ag1(axis, off).start()
    for off in far_first:
        for axis in (0, 1):
            ag2(axis, 0, off).start()
    hidden = preact * gating
    for core in (0, 1):
        hidden_half[core] = hidden[:, core * hid : (core + 1) * hid]
    hidden_pair = remote(hidden_half.at[other], hidden_got, pair_send.at[1], pair_recv.at[1], rep=other)
    hidden_pair.start()
    grad_self = dot3(feat[rep].T, grad_parts)
    grad_neigh = dot3(aggregate.T, grad_parts)
    grad_bias = jnp.sum(grad_pre, axis=0, keepdims=True)
    share = 2 * width // cols
    for core in (0, 1):
        span = slice(core * hid, (core + 1) * hid)
        grads[core, : cols // 2, :share] = grad_self[:, span].reshape(cols // 2, share, hid)
        grads[core, cols // 2 :, :share] = grad_neigh[:, span].reshape(cols // 2, share, hid)
        grads[core, :, share:] = jnp.broadcast_to(grad_bias[None, :, span], (cols, 8, hid))
    grads_pair = remote(grads.at[other], grads_got, pair_send.at[0], pair_recv.at[0], rep=other)
    grads_pair.start()
    for off in (1, 3, 2):
        for axis in (0, 1):
            ag1(axis, off, arrives=True).wait_recv()
            for ahead in far_first:
                ag2(axis, off, ahead).start()
    direct = dot3(self_parts, grad_parts, ((1,), (1,)))
    direct_half[...] = direct.reshape(2, width // 2, block)
    direct_pair = remote(direct_half.at[other], direct_got, pair_send.at[2], pair_recv.at[2], rep=other)
    direct_pair.start()
    grads_pair.wait_recv()
    grads[rep] += grads_got[...]

    def to_col(off, arrives=False):
        return remote(
            grads.at[rep, (z + off) % cols], grads_col.at[(z + cols - off) % cols if arrives else z],
            col_send.at[off - 1], col_recv.at[off - 1], col=(z + off) % cols,
        )

    for off in around:
        to_col(off).start()
    grads_col[z] = grads[rep, z]
    hidden_out[rep] = hidden_half[rep]
    direct_out[rep] = direct_half[rep]
    for axis in (0, 1):
        for off in (0, 1, 3, 2):
            convert(axis, -off, 0)
    hidden_pair.wait_recv()
    hidden_out[other] = hidden_got[...]
    direct_pair.wait_recv()
    direct_out[other] = direct_got[...]
    for back in (0, 1, 3, 2):
        for ahead in (1, 3, 2):
            for axis in (0, 1):
                ag2(axis, back, ahead, arrives=True).wait_recv()
                convert(axis, -back, -ahead)
    for off in around:
        to_col(off, arrives=True).wait_recv()
    value = grads_col[0]
    for place in range(1, cols):
        value = value + grads_col[place]
    grad_part[...] = value
    for axis in (0, 1):
        for off in far_first:
            for line in lines:
                rs1(axis, off, line).wait_send()
                ag2(axis, line, off).wait_send()
            rs2(axis, off).wait_send()
            ag1(axis, off).wait_send()
    for off in around:
        to_col(off).wait_send()
    for copy in (grads_pair, hidden_pair, direct_pair):
        copy.wait_send()


def middle(sums, feat, cot, w_self, w_neigh, bias, cols):
    block, width = feat.shape[1:]
    hid = w_self.shape[1] // 2
    rows = SIDE * SIDE
    n = DEG + block // 2
    share = 2 * width // cols + 8
    vmem = pl.BlockSpec(memory_space=VMEM)
    shape = jax.ShapeDtypeStruct
    return pl.pallas_call(
        middle_kernel,
        out_shape=(
            shape((2, block, hid), F32),
            shape((rows, width, 2 * block), BF16),
            shape((2, width // 2, block), F32),
            shape((share, hid), F32),
        ),
        in_specs=[vmem] * 6,
        out_specs=(vmem,) * 4,
        scratch_shapes=[
            VMEM((2, SIDE - 1, SIDE, n, width), F32),
            VMEM((2, SIDE, n, width), F32),
            VMEM((2, SIDE - 1, n, width), F32),
            VMEM((SIDE, SIDE, width, block), F32),
            VMEM((2, block, hid), F32),
            VMEM((block, hid), F32),
            VMEM((2, width // 2, block), F32),
            VMEM((width // 2, block), F32),
            VMEM((2, cols, share, hid), F32),
            VMEM((cols, share, hid), F32),
            VMEM((cols, share, hid), F32),
            DMA((2, SIDE + 1, SIDE - 1)),
            DMA((2, SIDE + 1, SIDE - 1)),
            DMA((2, SIDE + 1, SIDE - 1)),
            DMA((2, SIDE + 1, SIDE - 1)),
            DMA((3,)),
            DMA((3,)),
            DMA((cols - 1,)),
            DMA((cols - 1,)),
        ],
        compiler_params=pltpu.CompilerParams(
            collective_id=1, has_side_effects=True, vmem_limit_bytes=20 * MIB
        ),
        name="middle",
    )(sums, feat, cot, w_self, w_neigh, bias)


def last_kernel(
    cols, factor, sums, direct, grad_part,
    grad_feat, grad_weights, grad_bias,
    own, pair_got, got_one, got_two, got_three, got_four, got_x, line, got_y, final,
    pair_send, pair_recv, ring_send, ring_recv, col_send, col_recv, row_send, row_recv,
):
    row = lax.axis_index("row")
    z = lax.axis_index("col")
    rep = lax.axis_index("rep")
    other = 1 - rep
    half = sums.shape[1] // 2
    share = final.shape[1]
    ways = (1, -1)
    x, y = row % SIDE, row // SIDE
    far_first = (2, 1, 3)
    x_peers = {off: y * SIDE + (x + off) % SIDE for off in far_first}
    y_peers = {off: ((y + off) % SIDE) * SIDE + x for off in far_first}
    greet(
        [{"col": (z + off) % cols} for off in range(1, cols)]
        + [{"row": peer} for peer in list(x_peers.values()) + list(y_peers.values())]
        + [{"rep": other}]
    )

    def ahead(off):
        return (z + off + 2 * cols) % cols

    def pair(off):
        at = ahead(off)
        return remote(
            sums.at[pl.ds(2 * at, 2), pl.ds(other * half, half)], pair_got.at[at],
            pair_send.at[off + 3], pair_recv.at[off + 3], rep=other,
        )

    def merge(off):
        at = ahead(off)
        pair(off).wait_recv()
        own[at] = sums[pl.ds(2 * at, 2), pl.ds(pl.multiple_of(rep * half, half), half)] + pair_got[at]

    hops = (1, 2, 1, 2, 2)
    got = (got_one, got_two, got_three, got_four, got_two)

    def ring(way, kind):
        at = ahead(ways[way] * (kind % 4 + 1 if kind < 4 else 2))
        src, dst = own.at[at], got[kind].at[way]
        if kind in (1, 3, 4):
            part = 1 - way if kind == 4 else way
            src = src.at[part]
            if kind != 3:
                dst = dst.at[part]
        return remote(
            src, dst, ring_send.at[way, kind], ring_recv.at[way, kind], col=ahead(ways[way] * hops[kind])
        )

    def to_x(off, arrives=False):
        return remote(
            grad_part, got_x.at[(x + SIDE - off) % SIDE if arrives else x],
            row_send.at[0, off - 1], row_recv.at[0, off - 1], row=x_peers[off],
        )

    def to_y(off, arrives=False):
        return remote(
            line, got_y.at[(y + SIDE - off) % SIDE if arrives else y],
            row_send.at[1, off - 1], row_recv.at[1, off - 1], row=y_peers[off],
        )

    def to_col(off, arrives=False):
        ref = final.at[ahead(-off) if arrives else z]
        return remote(ref, ref, col_send.at[off - 1], col_recv.at[off - 1], col=ahead(off))

    order = (3, -3, 4, 1, -1, 2, -2, 0)
    around = (4, 3, 5, 2, 6, 1, 7)
    for off in order:
        pair(off).start()
    for off in far_first:
        to_x(off).start()
    got_x[x] = grad_part[...]
    for off in order[:5]:
        merge(off)
        for way in (0, 1):
            if off == 4 or off * ways[way] > 0:
                ring(way, abs(off) - 1).start()
    merge(2)
    merge(-2)
    for off in far_first:
        to_x(off, arrives=True).wait_recv()
    line[...] = (got_x[0] + got_x[1]) + (got_x[2] + got_x[3])
    for off in far_first:
        to_y(off).start()
    got_y[y] = line[...]
    for way in (0, 1):
        ring(way, 2).wait_recv()
        own[ahead(2 * ways[way])] += got_three[way]
        ring(way, 4).start()
    for way in (0, 1):
        ring(way, 3).wait_recv()
        own[ahead(2 * ways[way]), way] += got_four[way]
        ring(way, 1).start()
    merge(0)
    for off in far_first:
        to_y(off, arrives=True).wait_recv()
    value = ((got_y[0] + got_y[1]) + (got_y[2] + got_y[3])) * factor
    final[z] = value[:share]
    for off in around:
        to_col(off).start()
    grad_bias[...] = value[share:]
    for way in (0, 1):
        ring(way, 0).wait_recv()
    grad_feat[...] = (direct[...] + own[z]) + (got_one[0] + got_one[1])
    for way in (0, 1):
        ring(way, 4).wait_recv()
        ring(way, 1).wait_recv()
    grad_feat[...] += got_two[0] + got_two[1]
    for off in around:
        to_col(off, arrives=True).wait_recv()
    grad_weights[...] = final[...]
    for off in order:
        pair(off).wait_send()
    for way in (0, 1):
        for kind in range(5):
            ring(way, kind).wait_send()
    for off in around:
        to_col(off).wait_send()
    for off in far_first:
        to_x(off).wait_send()
        to_y(off).wait_send()


def last(sums, direct, grad_part, cols, factor):
    width, block = sums.shape[1:]
    hid = grad_part.shape[1]
    share = 2 * width // cols
    vmem = pl.BlockSpec(memory_space=VMEM)
    return pl.pallas_call(
        functools.partial(last_kernel, cols, factor),
        out_shape=(
            VMEM((2, width // 2, block), F32),
            VMEM((cols, share, hid), F32),
            VMEM((8, hid), F32),
        ),
        in_specs=[vmem] * 3,
        out_specs=(vmem,) * 3,
        scratch_shapes=[
            VMEM((cols, 2, width // 2, block), F32),
            VMEM((cols, 2, width // 2, block), F32),
            VMEM((2, 2, width // 2, block), F32),
            VMEM((2, 2, width // 2, block), F32),
            VMEM((2, 2, width // 2, block), F32),
            VMEM((2, width // 2, block), F32),
            VMEM((SIDE, share + 8, hid), F32),
            VMEM((share + 8, hid), F32),
            VMEM((SIDE, share + 8, hid), F32),
            VMEM((cols, share, hid), F32),
            DMA((cols,)),
            DMA((cols,)),
            DMA((2, 5)),
            DMA((2, 5)),
            DMA((cols - 1,)),
            DMA((cols - 1,)),
            DMA((2, SIDE - 1)),
            DMA((2, SIDE - 1)),
        ],
        compiler_params=pltpu.CompilerParams(
            collective_id=2, has_side_effects=True, vmem_limit_bytes=16 * MIB
        ),
        name="last",
    )(sums, direct, grad_part)


def finish_kernel(grad_feat, grad_weights, grad_bias, feat_out, self_out, neigh_out, bias_out, sems):
    block = grad_feat.shape[2]
    pieces = [
        (grad_feat.at[0], feat_out.at[:, pl.ds(0, block)]),
        (grad_feat.at[1], feat_out.at[:, pl.ds(block, block)]),
        (grad_weights.at[0], self_out),
        (grad_weights.at[1], neigh_out),
        (grad_bias.at[pl.ds(0, 1)], bias_out),
    ]
    copies = [pltpu.make_async_copy(src, dst, sems.at[at]) for at, (src, dst) in enumerate(pieces)]
    for copy in copies:
        copy.start()
    for copy in copies:
        copy.wait()


def finish(grad_feat, grad_weights, grad_bias):
    half, block = grad_feat.shape[1:]
    hid = grad_bias.shape[1]
    vmem = pl.BlockSpec(memory_space=VMEM)
    far = pl.BlockSpec(memory_space=pl.ANY)
    shape = jax.ShapeDtypeStruct
    return pl.pallas_call(
        finish_kernel,
        out_shape=(
            shape((half, 2 * block), F32), shape((2 * half, hid), F32), shape((2 * half, hid), F32), shape((1, hid), F32)
        ),
        in_specs=[vmem] * 3,
        out_specs=(far,) * 4,
        scratch_shapes=[DMA((5,))],
        compiler_params=pltpu.CompilerParams(vmem_limit_bytes=8 * MIB),
        name="finish",
    )(grad_feat, grad_weights.reshape(2, 2 * half, hid), grad_bias)


def shards(features, cotangent, w_self, w_neigh, bias, tiles, tile_dst, tile_src, tile_count):
    slots, block = tiles.shape[2:4]
    width = features.shape[1]
    hid = w_self.shape[1]
    cols = lax.axis_size("col")
    rows = lax.axis_size("row")
    tiles = tiles.reshape(slots, block, block)
    feat = features.reshape(2, block, width)
    cot = cotangent.reshape(2, block, hid)

    stacked, lists, tiles = gather_features(tile_count, tile_dst, tile_src, feat, tiles, cols, rows)
    sums = forward(lists, tiles, stacked, (SIDE + 1, SIDE, block + DEG, width))
    hidden, scaled, direct, grad_part = middle(sums, feat, cot, w_self, w_neigh, bias.reshape(1, hid), cols)
    back, hidden = backward(lists, tiles, scaled, hidden, (2 * cols + 1, width, block))
    factor = float(features.shape[0] * rows * cols) ** (-0.5)
    grad_feat, grad_self, grad_neigh, grad_bias = finish(*last(back, direct, grad_part, cols, factor))
    return (
        hidden.reshape(2 * block, hid // 2), grad_feat.T, grad_self, grad_neigh, grad_bias.reshape(hid // 2)
    )


def solution(mesh):
    return jax.shard_map(
        shards,
        mesh=mesh,
        in_specs=(
            P(("row", "col"), None),
            P(("row", "col"), None),
            P(),
            P(),
            P(),
            P("row", "col", None, None, None),
            P("row", "col", None),
            P("row", "col", None),
            P("row", "col"),
        ),
        out_specs=(
            P(("row", "col"), "rep"),
            P(("row", "col"), "rep"),
            P(None, "rep"),
            P(None, "rep"),
            P("rep"),
        ),
        check_vma=False,
    )
```

```python
import functools

import jax
import jax.numpy as jnp
from jax import lax
from jax.experimental import pallas as pl
from jax.experimental.pallas import tpu as pltpu
from jax.sharding import PartitionSpec as P

MESH = pl.DeviceIdType.MESH
F32 = jnp.float32
BF16 = jnp.bfloat16
VMEM = pltpu.VMEM
DMA = pltpu.SemaphoreType.DMA
MIB = 1 << 20


def split(value):
    high = value.astype(BF16)
    low = (value - high.astype(F32)).astype(BF16)
    return high, low


def dot3(left, right, dims=((1,), (0,))):
    left_high, left_low = left if isinstance(left, tuple) else split(left)
    right_high, right_low = right if isinstance(right, tuple) else split(right)

    def one(a, b):
        return lax.dot_general(a, b, (dims, ((), ())), preferred_element_type=F32)

    return one(left_high, right_high) + (one(left_high, right_low) + one(left_low, right_high))


def remote(src, dst, send, recv, **where):
    return pltpu.make_async_remote_copy(
        src_ref=src, dst_ref=dst, send_sem=send, recv_sem=recv, device_id=where, device_id_type=MESH
    )


def greet(partners):
    barrier = pltpu.get_barrier_semaphore()
    for where in partners:
        pl.semaphore_signal(barrier, inc=1, device_id=where, device_id_type=MESH)
    pl.semaphore_wait(barrier, len(partners))


LIST = 256


def make_lists(count, dst, src, lists, line, dummies):
    rep = lax.axis_index("rep")
    slots = dst.shape[2]
    line[...] = jnp.zeros_like(line)
    line[0:1, :slots] = dst[0]
    line[8:9, :slots] = src[0]
    wide = (8, LIST)
    block = jnp.broadcast_to(line[0:1], wide)
    source = jnp.broadcast_to(line[8:9], wide)
    slot = lax.broadcasted_iota(jnp.int32, wide, 1)
    own = ((block & 1) == rep) & (slot < count[0, 0]) & (slot < slots)
    own = own.astype(jnp.int32).astype(F32)
    square = (LIST, LIST)
    down = lax.broadcasted_iota(jnp.int32, square, 0)
    before = (down < lax.broadcasted_iota(jnp.int32, square, 1)).astype(jnp.int32).astype(F32).astype(BF16)
    place = jnp.dot(own.astype(BF16), before, preferred_element_type=F32)
    place = jnp.where(own > 0.5, place, -1.0)
    total = jnp.broadcast_to(jnp.sum(own, axis=1, keepdims=True), wide)
    chosen = (jnp.broadcast_to(place[0:1], square) == down.astype(F32)).astype(jnp.int32).astype(F32).astype(BF16)
    kind = lax.broadcasted_iota(jnp.int32, wide, 0)
    values = jnp.where(kind == 0, slot, jnp.where(kind % 2 == 1, block >> 1, source)).astype(F32).astype(BF16)
    listed = lax.dot_general(values, chosen, (((1,), (1,)), ((), ())), preferred_element_type=F32)
    beyond = slot.astype(F32) >= total
    listed = jnp.where(beyond & (kind == 3), float(dummies[0]), listed)
    listed = jnp.where(beyond & (kind == 4), float(dummies[1]), listed)
    listed = jnp.where(kind == 5, total, listed)
    lists[...] = listed.astype(jnp.int32)


def gather_kernel(
    cols, dummies, count, dst_far, src_far, feat_far, tiles,
    stacked, lists, tiles_here,
    feat, dst, src, held, line, ring_send, ring_recv, pair_send, pair_recv, load_sems,
):
    loads = [
        pltpu.make_async_copy(far, here, load_sems.at[at])
        for at, (far, here) in enumerate(((feat_far, feat), (dst_far, dst), (src_far, src), (tiles, tiles_here)))
    ]
    for load in loads:
        load.start()
    z = lax.axis_index("col")
    rep = lax.axis_index("rep")
    other = 1 - rep
    rows = feat.shape[1]
    ways = (1, -1)
    greet([{"col": (z + off + cols) % cols} for off in (1, -1, 2, -2)] + [{"rep": other}])
    for load in loads[:3]:
        load.wait()

    def put(block, value):
        high, low = split(value)
        width = value.shape[1]
        stacked[block, :width, :width] = high
        stacked[block, :width, width:] = low
        stacked[block, width:, :width] = high
        stacked[block, width:, width:] = jnp.zeros_like(high)

    hops = (1, 2, 1, 2)

    def spot(way, kind, core, steps, turn):
        origin = (z - ways[way] * steps + cols) % cols
        part = way if turn == 0 else 1 - way
        return held.at[origin, core, pl.ds(part * (rows // 2), rows // 2)]

    def ring(way, kind, turn, arrives=False):
        back = 2 * (kind // 2)
        dst = spot(way, kind, rep, back + (hops[kind] if arrives else 0), turn)
        part = way if turn == 0 else 1 - way
        src = feat.at[rep, pl.ds(part * (rows // 2), rows // 2)] if kind < 2 and not arrives else dst
        return remote(
            src, dst, ring_send.at[way, kind, turn], ring_recv.at[way, kind, turn],
            col=(z + ways[way] * hops[kind] + cols) % cols,
        )

    def pair(way, kind, turn, core):
        dst = spot(way, kind, core, 2 * (kind // 2) + hops[kind], turn)
        return remote(dst, dst, pair_send.at[way, kind, turn], pair_recv.at[way, kind, turn], rep=other)

    def take(kind, way, core):
        steps = 2 * (kind // 2) + hops[kind]
        origin = (z - ways[way] * steps + cols) % cols
        put(origin * 2 + core, held[origin, core])

    both = (0, 1)
    for kind in (1, 0):
        for turn in both:
            for way in both:
                ring(way, kind, turn).start()
    for turn in both:
        for way in both:
            ring(way, 1, turn, arrives=True).wait_recv()
            if turn == 0:
                ring(way, 3, 0).start()
            ring(way, 2, turn).start()
            pair(way, 1, turn, rep).start()
    for turn in both:
        for way in both:
            ring(way, 0, turn, arrives=True).wait_recv()
            pair(way, 0, turn, rep).start()
    for core in both:
        put(z * 2 + core, feat[core])
    make_lists(count, dst, src, lists, line, dummies)
    for kind in (0, 1):
        for way in both:
            take(kind, way, rep)
    for turn in both:
        for kind in (2, 3) if turn == 0 else (2,):
            for way in both:
                ring(way, kind, turn, arrives=True).wait_recv()
                pair(way, kind, turn, rep).start()
    for kind in (1, 0):
        for way in both:
            for turn in both:
                pair(way, kind, turn, other).wait_recv()
            take(kind, way, other)
    for way in both:
        take(2, way, rep)
    take(3, 0, rep)
    for way in both:
        for turn in both:
            pair(way, 2, turn, other).wait_recv()
        take(2, way, other)
    for way in both:
        pair(way, 3, 0, other).wait_recv()
    take(3, 0, other)
    for kind in range(4):
        for way in both:
            for turn in both if kind < 3 else (0,):
                ring(way, kind, turn).wait_send()
                pair(way, kind, turn, rep).wait_send()
    loads[3].wait()


def gather_features(count, dst, src, feat, tiles, cols, rows):
    block, width = feat.shape[1:]
    sems = (2, 4, 2)
    vmem = pl.BlockSpec(memory_space=VMEM)
    far = pl.BlockSpec(memory_space=pl.ANY)
    return pl.pallas_call(
        functools.partial(gather_kernel, cols, (rows, 2 * cols)),
        out_shape=(
            jax.ShapeDtypeStruct((cols * 2, 2 * width, 2 * width), BF16),
            jax.ShapeDtypeStruct((8, LIST), jnp.int32),
            VMEM(tiles.shape, F32),
        ),
        in_specs=[pl.BlockSpec(memory_space=pltpu.SMEM), far, far, far, far],
        out_specs=(vmem, vmem, vmem),
        scratch_shapes=[
            VMEM(feat.shape, F32), VMEM(dst.shape, jnp.int32), VMEM(src.shape, jnp.int32),
            VMEM((cols, 2, block, width), F32), VMEM((16, LIST), jnp.int32),
            DMA(sems), DMA(sems), DMA(sems), DMA(sems), DMA((4,)),
        ],
        compiler_params=pltpu.CompilerParams(
            collective_id=0, has_side_effects=True, vmem_limit_bytes=24 * MIB
        ),
        name="gather_features",
    )(*[pltpu.with_memory_space_constraint(x, pltpu.HBM) if x is not count else x for x in (count, dst, src, feat, tiles)])


LARGE, SMALL = 32, 8
SLOT, LOAD_DST, LOAD_SRC, ADD_DST, ADD_SRC, TOTAL = range(6)


def over_tiles(lists, step):
    total = lists[TOTAL, 0]
    large = total // LARGE

    def run(size, start):
        def body(group, carry):
            step(start + group * size, size)
            return carry

        return body

    lax.fori_loop(0, large, run(LARGE, 0), 0)
    rest = total - large * LARGE
    lax.fori_loop(0, (rest + (SMALL - 1)) // SMALL, run(SMALL, large * LARGE), 0)


def forward_kernel(lists, tiles, stacked, sums, weight):
    block = tiles.shape[1]
    live = sums.shape[0] - 1
    sums[...] = jnp.zeros_like(sums)
    weight[...] = jnp.zeros_like(weight)

    def step(start, size):
        parts = []
        for u in range(size):
            place = start + u
            tile = tiles[lists[SLOT, place]]
            high, low = split(tile)
            product = jnp.dot(
                jnp.concatenate([high, low], axis=1), stacked[lists[LOAD_SRC, place]], preferred_element_type=F32
            )
            parts.append((lists[ADD_DST, place], product[:, :block] + product[:, block:], tile))
        for target, value, tile in parts:
            sums[target >> 2, target & 3, pl.ds(8, block)] += value
            weight[target] += tile

    over_tiles(lists, step)
    for target in range(4 * live):
        degree = jnp.sum(weight[target].T, axis=0, keepdims=True)
        sums[target >> 2, target & 3, pl.ds(0, 8)] = jnp.broadcast_to(degree, (8, block))


def backward_kernel(lists, tiles, stacked, hidden, sums, hidden_out, out_sem):
    copy = pltpu.make_async_copy(hidden, hidden_out, out_sem)
    copy.start()
    block = tiles.shape[1]
    sums[...] = jnp.zeros_like(sums)

    def step(start, size):
        parts = []
        for u in range(size):
            place = start + u
            high, low = split(tiles[lists[SLOT, place]])
            right = jnp.concatenate(
                [
                    jnp.concatenate([high, low], axis=1),
                    jnp.concatenate([high, jnp.zeros_like(high)], axis=1),
                ],
                axis=0,
            )
            product = jnp.dot(stacked[lists[LOAD_DST, place]], right, preferred_element_type=F32)
            parts.append((lists[ADD_SRC, place], product[:, :block] + product[:, block:]))
        for target, value in parts:
            sums[target] += value

    over_tiles(lists, step)
    copy.wait()


def forward(lists, tiles, stacked, out_shape):
    vmem = pl.BlockSpec(memory_space=VMEM)
    block = tiles.shape[1]
    return pl.pallas_call(
        forward_kernel,
        out_shape=jax.ShapeDtypeStruct(out_shape, F32),
        in_specs=[pl.BlockSpec(memory_space=pltpu.SMEM), vmem, vmem],
        out_specs=vmem,
        scratch_shapes=[VMEM((4 * out_shape[0] - 3, block, block), F32)],
        compiler_params=pltpu.CompilerParams(vmem_limit_bytes=32 * MIB),
        name="forward",
    )(lists, tiles, stacked)


def backward(lists, tiles, stacked, hidden, out_shape):
    vmem = pl.BlockSpec(memory_space=VMEM)
    shape = jax.ShapeDtypeStruct
    return pl.pallas_call(
        backward_kernel,
        out_shape=(shape(out_shape, F32), shape(hidden.shape, F32)),
        in_specs=[pl.BlockSpec(memory_space=pltpu.SMEM), vmem, vmem, vmem],
        out_specs=(vmem, pl.BlockSpec(memory_space=pl.ANY)),
        scratch_shapes=[DMA],
        compiler_params=pltpu.CompilerParams(vmem_limit_bytes=32 * MIB),
        name="backward",
    )(lists, tiles, stacked, hidden)


SIDE = 4
DEG = 8


def middle_kernel(
    sums, feat, cot, w_self, w_neigh, bias,
    hidden_out, stacked, direct_out, grad_part,
    far1, near1, part1, near2, gathered, hidden_half, hidden_got, direct_half, direct_got,
    grads, grads_got, grads_col,
    rs_send, rs_recv, ag_send, ag_recv, pair_send, pair_recv, col_send, col_recv, near_in,
):
    row = lax.axis_index("row")
    rep = lax.axis_index("rep")
    other = 1 - rep
    rows = SIDE * SIDE
    block = feat.shape[1]
    width = feat.shape[2]
    hid = w_self.shape[1] // 2
    coords = (row % SIDE, row // SIDE)
    low = block // 2
    spans = ((0, DEG + low), (DEG + low, low))
    far_first = (2, 1, 3)

    def at(axis, first, second):
        one = (coords[axis] + first + SIDE) % SIDE
        two = (coords[1 - axis] + second + SIDE) % SIDE
        return (two, one) if axis == 0 else (one, two)

    def device(axis, first, second):
        y, x = at(axis, first, second)
        return y * SIDE + x

    z = lax.axis_index("col")
    cols = grads.shape[1]
    around = (4, 3, 5, 2, 6, 1, 7)
    greet(
        [{"row": device(axis, off, 0)} for axis in (0, 1) for off in far_first]
        + [{"col": (z + off + cols) % cols} for off in (1, -1, 2, -2)]
        + [{"rep": other}]
    )
    for off in (2, -2):
        pl.semaphore_signal(near_in, inc=1, device_id={"col": (z + off + cols) % cols}, device_id_type=MESH)

    relay = {2: 0, 1: 0, 3: 1, 0: 1}
    ways = (1, -1)

    def rs0(axis, line):
        lo, n = spans[axis]
        y, x = at(axis, 2, line)
        return remote(
            sums.at[y, x, pl.ds(lo, n)], far1.at[axis, line, pl.ds(0, n)],
            rs_send.at[axis, 0, line], rs_recv.at[axis, 0, line], row=device(axis, ways[relay[line]], 0),
        )

    def rs1(axis, way, line):
        lo, n = spans[axis]
        y, x = at(axis, ways[way], line)
        if relay[line] == way:
            src = far1.at[axis, line, pl.ds(0, n)]
        else:
            src = sums.at[y, x, pl.ds(lo, n)]
        return remote(
            src, near1.at[axis, way, line, pl.ds(0, n)],
            rs_send.at[axis, 1 + way, line], rs_recv.at[axis, 1 + way, line], row=device(axis, ways[way], 0),
        )

    def rs2(axis, off):
        n = spans[axis][1]
        return remote(
            part1.at[axis, off, pl.ds(0, n)], near2.at[axis, off - 1, pl.ds(0, n)],
            rs_send.at[axis, 3, off], rs_recv.at[axis, 3, off], row=device(axis, 0, off),
        )

    lines = (2, 3, 1, 0)
    for line in (2, 3, 1):
        for axis in (0, 1):
            rs0(axis, line).start()
    for line in (2, 3, 1):
        for axis in (0, 1):
            rs1(axis, 1 - relay[line], line).start()
    for axis in (0, 1):
        rs0(axis, 0).start()
    own_feat = split(feat[rep])
    self_parts = split(w_self[...])
    neigh_parts = split(w_neigh[...])
    pre_self = dot3(own_feat, self_parts) + bias[...]
    for line in lines:
        for axis in (0, 1):
            rs0(axis, line).wait_recv()
            way = relay[line]
            lo, n = spans[axis]
            y, x = at(axis, ways[way], line)
            far1[axis, line, pl.ds(0, n)] += sums[y, x, pl.ds(lo, n)]
            rs1(axis, way, line).start()
            if line == 1:
                rs1(axis, 1 - relay[0], 0).start()
    for line in lines:
        for axis in (0, 1):
            for way in (0, 1):
                rs1(axis, way, line).wait_recv()
            lo, n = spans[axis]
            y, x = at(axis, 0, line)
            span = pl.ds(0, n)
            part1[axis, line, span] = sums[y, x, pl.ds(lo, n)] + (
                near1[axis, 0, line, span] + near1[axis, 1, line, span]
            )
            if line:
                rs2(axis, line).start()
    summed = []
    for axis in (0, 1):
        for off in far_first:
            rs2(axis, off).wait_recv()
        span = pl.ds(0, spans[axis][1])
        summed.append(
            (part1[axis, 0, span] + near2[axis, 0, span]) + (near2[axis, 1, span] + near2[axis, 2, span])
        )
    degree = summed[0][:1]
    inverse = 1.0 / jnp.maximum(degree, 1.0)
    inverse_down = jnp.broadcast_to(inverse, (block, block)).T
    total = jnp.concatenate([summed[0][DEG:], summed[1]], axis=0)
    aggregate = total * inverse_down
    preact = pre_self + dot3(aggregate, neigh_parts)
    gating = jax.nn.sigmoid(preact)
    grad_pre = cot[rep] * (gating * (1.0 + preact * (1.0 - gating)))
    grad_parts = split(grad_pre)
    y0, x0 = coords[1], coords[0]
    scaled = dot3(neigh_parts, grad_parts, ((1,), (1,))) * inverse
    gathered[y0, x0] = scaled

    def half_of(axis, first, second):
        y, x = at(axis, first, second)
        return gathered.at[y, x, pl.ds(axis * low, low)]

    def ag1(axis, off, arrives=False):
        ref = half_of(axis, -off if arrives else 0, 0)
        return remote(
            ref, ref, ag_send.at[axis, 0, off - 1], ag_recv.at[axis, 0, off - 1], row=device(axis, off, 0)
        )

    def ag2(axis, back, off, arrives=False):
        ref = half_of(axis, -back, -off if arrives else 0)
        return remote(
            ref, ref, ag_send.at[axis, 1 + back, off - 1], ag_recv.at[axis, 1 + back, off - 1],
            row=device(axis, 0, off),
        )

    def convert(axis, first, second):
        y, x = at(axis, first, second)
        span = pl.ds(axis * low, low)
        high, small = split(gathered[y, x, span])
        stacked[y * SIDE + x, span, :block] = high
        stacked[y * SIDE + x, span, block:] = small

    for off in far_first:
        for axis in (0, 1):
            ag1(axis, off).start()
    for off in far_first:
        for axis in (0, 1):
            ag2(axis, 0, off).start()
    hidden = preact * gating
    for core in (0, 1):
        hidden_half[core] = hidden[:, core * hid : (core + 1) * hid]
    hidden_pair = remote(hidden_half.at[other], hidden_got, pair_send.at[1], pair_recv.at[1], rep=other)
    hidden_pair.start()
    grad_self = dot3(feat[rep].T, grad_parts)
    grad_neigh = dot3(aggregate.T, grad_parts)
    grad_bias = jnp.sum(grad_pre, axis=0, keepdims=True)
    share = 2 * width // cols
    for core in (0, 1):
        span = slice(core * hid, (core + 1) * hid)
        grads[core, : cols // 2, :share] = grad_self[:, span].reshape(cols // 2, share, hid)
        grads[core, cols // 2 :, :share] = grad_neigh[:, span].reshape(cols // 2, share, hid)
        grads[core, :, share:] = jnp.broadcast_to(grad_bias[None, :, span], (cols, 8, hid))
    grads_pair = remote(grads.at[other], grads_got, pair_send.at[0], pair_recv.at[0], rep=other)
    grads_pair.start()
    for off in (1, 3, 2):
        for axis in (0, 1):
            ag1(axis, off, arrives=True).wait_recv()
            for ahead in far_first:
                ag2(axis, off, ahead).start()
    direct = dot3(self_parts, grad_parts, ((1,), (1,)))
    direct_half[...] = direct.reshape(2, width // 2, block)
    direct_pair = remote(direct_half.at[other], direct_got, pair_send.at[2], pair_recv.at[2], rep=other)
    direct_pair.start()
    grads_pair.wait_recv()
    grads[rep] += grads_got[...]

    def to_col(off, arrives=False):
        return remote(
            grads.at[rep, (z + off) % cols], grads_col.at[(z + cols - off) % cols if arrives else z],
            col_send.at[off - 1], col_recv.at[off - 1], col=(z + off) % cols,
        )

    pl.semaphore_wait(near_in, 2)
    for off in around:
        to_col(off).start()
    grads_col[z] = grads[rep, z]
    hidden_out[rep] = hidden_half[rep]
    direct_out[rep] = direct_half[rep]
    for axis in (0, 1):
        for off in (0, 1, 3, 2):
            convert(axis, -off, 0)
    hidden_pair.wait_recv()
    hidden_out[other] = hidden_got[...]
    direct_pair.wait_recv()
    direct_out[other] = direct_got[...]
    for back in (0, 1, 3, 2):
        for ahead in (1, 3, 2):
            for axis in (0, 1):
                ag2(axis, back, ahead, arrives=True).wait_recv()
                convert(axis, -back, -ahead)
    for off in around:
        to_col(off, arrives=True).wait_recv()
    value = grads_col[0]
    for place in range(1, cols):
        value = value + grads_col[place]
    grad_part[...] = value
    for axis in (0, 1):
        for off in far_first:
            for back in range(SIDE):
                ag2(axis, back, off).wait_send()
            rs2(axis, off).wait_send()
            ag1(axis, off).wait_send()
        for line in lines:
            rs0(axis, line).wait_send()
            for way in (0, 1):
                rs1(axis, way, line).wait_send()
    for off in around:
        to_col(off).wait_send()
    for copy in (grads_pair, hidden_pair, direct_pair):
        copy.wait_send()


def middle(sums, feat, cot, w_self, w_neigh, bias, cols):
    block, width = feat.shape[1:]
    hid = w_self.shape[1] // 2
    rows = SIDE * SIDE
    n = DEG + block // 2
    share = 2 * width // cols + 8
    vmem = pl.BlockSpec(memory_space=VMEM)
    shape = jax.ShapeDtypeStruct
    return pl.pallas_call(
        middle_kernel,
        out_shape=(
            shape((2, block, hid), F32),
            shape((rows, width, 2 * block), BF16),
            shape((2, width // 2, block), F32),
            shape((share, hid), F32),
        ),
        in_specs=[vmem] * 6,
        out_specs=(vmem,) * 4,
        scratch_shapes=[
            VMEM((2, SIDE, n, width), F32),
            VMEM((2, 2, SIDE, n, width), F32),
            VMEM((2, SIDE, n, width), F32),
            VMEM((2, SIDE - 1, n, width), F32),
            VMEM((SIDE, SIDE, width, block), F32),
            VMEM((2, block, hid), F32),
            VMEM((block, hid), F32),
            VMEM((2, width // 2, block), F32),
            VMEM((width // 2, block), F32),
            VMEM((2, cols, share, hid), F32),
            VMEM((cols, share, hid), F32),
            VMEM((cols, share, hid), F32),
            DMA((2, 4, SIDE)),
            DMA((2, 4, SIDE)),
            DMA((2, SIDE + 1, SIDE - 1)),
            DMA((2, SIDE + 1, SIDE - 1)),
            DMA((3,)),
            DMA((3,)),
            DMA((cols - 1,)),
            DMA((cols - 1,)),
            pltpu.SemaphoreType.REGULAR,
        ],
        compiler_params=pltpu.CompilerParams(
            collective_id=1, has_side_effects=True, vmem_limit_bytes=20 * MIB
        ),
        name="middle",
    )(sums, feat, cot, w_self, w_neigh, bias)


def last_kernel(
    cols, factor, sums, direct, grad_part,
    grad_feat, grad_weights, grad_bias,
    own, pair_got, got_one, got_two, got_three, got_four, got_x, line, got_y, final,
    pair_send, pair_recv, ring_send, ring_recv, col_send, col_recv, row_send, row_recv,
):
    row = lax.axis_index("row")
    z = lax.axis_index("col")
    rep = lax.axis_index("rep")
    other = 1 - rep
    half = sums.shape[1] // 2
    share = final.shape[1]
    ways = (1, -1)
    x, y = row % SIDE, row // SIDE
    far_first = (2, 1, 3)
    x_peers = {off: y * SIDE + (x + off) % SIDE for off in far_first}
    y_peers = {off: ((y + off) % SIDE) * SIDE + x for off in far_first}
    greet(
        [{"col": (z + off + cols) % cols} for off in (1, -1, 2, -2)]
        + [{"row": peer} for peer in list(x_peers.values()) + list(y_peers.values())]
        + [{"rep": other}]
    )

    def ahead(off):
        return (z + off + 2 * cols) % cols

    def pair(off):
        at = ahead(off)
        return remote(
            sums.at[pl.ds(2 * at, 2), pl.ds(other * half, half)], pair_got.at[at],
            pair_send.at[off + 3], pair_recv.at[off + 3], rep=other,
        )

    def merge(off):
        at = ahead(off)
        pair(off).wait_recv()
        own[at] = sums[pl.ds(2 * at, 2), pl.ds(pl.multiple_of(rep * half, half), half)] + pair_got[at]

    hops = (1, 2, 1, 2, 2)
    got = (got_one, got_two, got_three, got_four, got_two)

    def ring(way, kind):
        at = ahead(ways[way] * (kind % 4 + 1 if kind < 4 else 2))
        src, dst = own.at[at], got[kind].at[way]
        if kind in (1, 3, 4):
            part = 1 - way if kind == 4 else way
            src = src.at[part]
            if kind != 3:
                dst = dst.at[part]
        return remote(
            src, dst, ring_send.at[way, kind], ring_recv.at[way, kind], col=ahead(ways[way] * hops[kind])
        )

    def to_x(off, arrives=False):
        return remote(
            grad_part, got_x.at[(x + SIDE - off) % SIDE if arrives else x],
            row_send.at[0, off - 1], row_recv.at[0, off - 1], row=x_peers[off],
        )

    def to_y(off, arrives=False):
        return remote(
            line, got_y.at[(y + SIDE - off) % SIDE if arrives else y],
            row_send.at[1, off - 1], row_recv.at[1, off - 1], row=y_peers[off],
        )

    def to_col(off, arrives=False):
        ref = final.at[ahead(-off) if arrives else z]
        return remote(ref, ref, col_send.at[off - 1], col_recv.at[off - 1], col=ahead(off))

    order = (3, -3, 4, 1, -1, 2, -2, 0)
    around = (4, 3, 5, 2, 6, 1, 7)
    for off in order:
        pair(off).start()
    for off in far_first:
        to_x(off).start()
    got_x[x] = grad_part[...]
    for off in order[:5]:
        merge(off)
        for way in (0, 1):
            if off == 4 or off * ways[way] > 0:
                ring(way, abs(off) - 1).start()
    merge(2)
    merge(-2)
    for off in far_first:
        to_x(off, arrives=True).wait_recv()
    line[...] = (got_x[0] + got_x[1]) + (got_x[2] + got_x[3])
    for off in far_first:
        to_y(off).start()
    got_y[y] = line[...]
    for way in (0, 1):
        ring(way, 2).wait_recv()
        own[ahead(2 * ways[way])] += got_three[way]
        ring(way, 4).start()
    for way in (0, 1):
        ring(way, 3).wait_recv()
        own[ahead(2 * ways[way]), way] += got_four[way]
        ring(way, 1).start()
    merge(0)
    for off in far_first:
        to_y(off, arrives=True).wait_recv()
    value = ((got_y[0] + got_y[1]) + (got_y[2] + got_y[3])) * factor
    final[z] = value[:share]
    for off in around:
        to_col(off).start()
    grad_bias[...] = value[share:]
    for way in (0, 1):
        ring(way, 0).wait_recv()
    grad_feat[...] = (direct[...] + own[z]) + (got_one[0] + got_one[1])
    for way in (0, 1):
        ring(way, 4).wait_recv()
        ring(way, 1).wait_recv()
    grad_feat[...] += got_two[0] + got_two[1]
    for off in around:
        to_col(off, arrives=True).wait_recv()
    grad_weights[...] = final[...]
    for off in order:
        pair(off).wait_send()
    for way in (0, 1):
        for kind in range(5):
            ring(way, kind).wait_send()
    for off in around:
        to_col(off).wait_send()
    for off in far_first:
        to_x(off).wait_send()
        to_y(off).wait_send()


def last(sums, direct, grad_part, cols, factor):
    width, block = sums.shape[1:]
    hid = grad_part.shape[1]
    share = 2 * width // cols
    vmem = pl.BlockSpec(memory_space=VMEM)
    return pl.pallas_call(
        functools.partial(last_kernel, cols, factor),
        out_shape=(
            VMEM((2, width // 2, block), F32),
            VMEM((cols, share, hid), F32),
            VMEM((8, hid), F32),
        ),
        in_specs=[vmem] * 3,
        out_specs=(vmem,) * 3,
        scratch_shapes=[
            VMEM((cols, 2, width // 2, block), F32),
            VMEM((cols, 2, width // 2, block), F32),
            VMEM((2, 2, width // 2, block), F32),
            VMEM((2, 2, width // 2, block), F32),
            VMEM((2, 2, width // 2, block), F32),
            VMEM((2, width // 2, block), F32),
            VMEM((SIDE, share + 8, hid), F32),
            VMEM((share + 8, hid), F32),
            VMEM((SIDE, share + 8, hid), F32),
            VMEM((cols, share, hid), F32),
            DMA((cols,)),
            DMA((cols,)),
            DMA((2, 5)),
            DMA((2, 5)),
            DMA((cols - 1,)),
            DMA((cols - 1,)),
            DMA((2, SIDE - 1)),
            DMA((2, SIDE - 1)),
        ],
        compiler_params=pltpu.CompilerParams(
            collective_id=2, has_side_effects=True, vmem_limit_bytes=16 * MIB
        ),
        name="last",
    )(sums, direct, grad_part)


def finish_kernel(grad_feat, grad_weights, grad_bias, feat_out, self_out, neigh_out, bias_out, sems):
    block = grad_feat.shape[2]
    pieces = [
        (grad_feat.at[0], feat_out.at[:, pl.ds(0, block)]),
        (grad_feat.at[1], feat_out.at[:, pl.ds(block, block)]),
        (grad_weights.at[0], self_out),
        (grad_weights.at[1], neigh_out),
        (grad_bias.at[pl.ds(0, 1)], bias_out),
    ]
    copies = [pltpu.make_async_copy(src, dst, sems.at[at]) for at, (src, dst) in enumerate(pieces)]
    for copy in copies:
        copy.start()
    for copy in copies:
        copy.wait()


def finish(grad_feat, grad_weights, grad_bias):
    half, block = grad_feat.shape[1:]
    hid = grad_bias.shape[1]
    vmem = pl.BlockSpec(memory_space=VMEM)
    far = pl.BlockSpec(memory_space=pl.ANY)
    shape = jax.ShapeDtypeStruct
    return pl.pallas_call(
        finish_kernel,
        out_shape=(
            shape((half, 2 * block), F32), shape((2 * half, hid), F32), shape((2 * half, hid), F32), shape((1, hid), F32)
        ),
        in_specs=[vmem] * 3,
        out_specs=(far,) * 4,
        scratch_shapes=[DMA((5,))],
        compiler_params=pltpu.CompilerParams(vmem_limit_bytes=8 * MIB),
        name="finish",
    )(grad_feat, grad_weights.reshape(2, 2 * half, hid), grad_bias)


def shards(features, cotangent, w_self, w_neigh, bias, tiles, tile_dst, tile_src, tile_count):
    slots, block = tiles.shape[2:4]
    width = features.shape[1]
    hid = w_self.shape[1]
    cols = lax.axis_size("col")
    rows = lax.axis_size("row")
    tiles = tiles.reshape(slots, block, block)
    feat = features.reshape(2, block, width)
    cot = cotangent.reshape(2, block, hid)

    stacked, lists, tiles = gather_features(tile_count, tile_dst, tile_src, feat, tiles, cols, rows)
    sums = forward(lists, tiles, stacked, (SIDE + 1, SIDE, block + DEG, width))
    hidden, scaled, direct, grad_part = middle(sums, feat, cot, w_self, w_neigh, bias.reshape(1, hid), cols)
    back, hidden = backward(lists, tiles, scaled, hidden, (2 * cols + 1, width, block))
    factor = float(features.shape[0] * rows * cols) ** (-0.5)
    grad_feat, grad_self, grad_neigh, grad_bias = finish(*last(back, direct, grad_part, cols, factor))
    return (
        hidden.reshape(2 * block, hid // 2), grad_feat.T, grad_self, grad_neigh, grad_bias.reshape(hid // 2)
    )


def solution(mesh):
    return jax.shard_map(
        shards,
        mesh=mesh,
        in_specs=(
            P(("row", "col"), None),
            P(("row", "col"), None),
            P(),
            P(),
            P(),
            P("row", "col", None, None, None),
            P("row", "col", None),
            P("row", "col", None),
            P("row", "col"),
        ),
        out_specs=(
            P(("row", "col"), "rep"),
            P(("row", "col"), "rep"),
            P(None, "rep"),
            P(None, "rep"),
            P("rep"),
        ),
        check_vma=False,
    )
```

```python
import functools

import jax
import jax.numpy as jnp
from jax import lax
from jax.experimental import pallas as pl
from jax.experimental.pallas import tpu as pltpu
from jax.sharding import PartitionSpec as P

MESH = pl.DeviceIdType.MESH
F32 = jnp.float32
BF16 = jnp.bfloat16
VMEM = pltpu.VMEM
DMA = pltpu.SemaphoreType.DMA
MIB = 1 << 20


def split(value):
    high = value.astype(BF16)
    low = (value - high.astype(F32)).astype(BF16)
    return high, low


def dot3(left, right, dims=((1,), (0,))):
    left_high, left_low = left if isinstance(left, tuple) else split(left)
    right_high, right_low = right if isinstance(right, tuple) else split(right)

    def one(a, b):
        return lax.dot_general(a, b, (dims, ((), ())), preferred_element_type=F32)

    return one(left_high, right_high) + (one(left_high, right_low) + one(left_low, right_high))


def remote(src, dst, send, recv, **where):
    return pltpu.make_async_remote_copy(
        src_ref=src, dst_ref=dst, send_sem=send, recv_sem=recv, device_id=where, device_id_type=MESH
    )


def greet(partners):
    barrier = pltpu.get_barrier_semaphore()
    for where in partners:
        pl.semaphore_signal(barrier, inc=1, device_id=where, device_id_type=MESH)
    pl.semaphore_wait(barrier, len(partners))


LIST = 256


def make_lists(count, dst, src, lists, line, dummies):
    rep = lax.axis_index("rep")
    slots = dst.shape[2]
    line[...] = jnp.zeros_like(line)
    line[0:1, :slots] = dst[0]
    line[8:9, :slots] = src[0]
    wide = (8, LIST)
    block = jnp.broadcast_to(line[0:1], wide)
    source = jnp.broadcast_to(line[8:9], wide)
    slot = lax.broadcasted_iota(jnp.int32, wide, 1)
    own = ((block & 1) == rep) & (slot < count[0, 0]) & (slot < slots)
    own = own.astype(jnp.int32).astype(F32)
    square = (LIST, LIST)
    down = lax.broadcasted_iota(jnp.int32, square, 0)
    before = (down < lax.broadcasted_iota(jnp.int32, square, 1)).astype(jnp.int32).astype(F32).astype(BF16)
    place = jnp.dot(own.astype(BF16), before, preferred_element_type=F32)
    place = jnp.where(own > 0.5, place, -1.0)
    total = jnp.broadcast_to(jnp.sum(own, axis=1, keepdims=True), wide)
    chosen = (jnp.broadcast_to(place[0:1], square) == down.astype(F32)).astype(jnp.int32).astype(F32).astype(BF16)
    kind = lax.broadcasted_iota(jnp.int32, wide, 0)
    values = jnp.where(kind == 0, slot, jnp.where(kind % 2 == 1, block >> 1, source)).astype(F32).astype(BF16)
    listed = lax.dot_general(values, chosen, (((1,), (1,)), ((), ())), preferred_element_type=F32)
    beyond = slot.astype(F32) >= total
    listed = jnp.where(beyond & (kind == 3), float(dummies[0]), listed)
    listed = jnp.where(beyond & (kind == 4), float(dummies[1]), listed)
    listed = jnp.where(kind == 5, total, listed)
    lists[...] = listed.astype(jnp.int32)


def gather_kernel(
    cols, dummies, count, dst_far, src_far, feat_far, tiles,
    stacked, lists, tiles_here,
    feat, dst, src, held, line, ring_send, ring_recv, pair_send, pair_recv, load_sems,
):
    loads = [
        pltpu.make_async_copy(far, here, load_sems.at[at])
        for at, (far, here) in enumerate(((feat_far, feat), (dst_far, dst), (src_far, src), (tiles, tiles_here)))
    ]
    for load in loads:
        load.start()
    z = lax.axis_index("col")
    rep = lax.axis_index("rep")
    other = 1 - rep
    rows = feat.shape[1]
    ways = (1, -1)
    greet([{"col": (z + off + cols) % cols} for off in (1, -1, 2, -2)] + [{"rep": other}])
    for load in loads[:3]:
        load.wait()

    def put(block, value):
        high, low = split(value)
        width = value.shape[1]
        stacked[block, :width, :width] = high
        stacked[block, :width, width:] = low
        stacked[block, width:, :width] = high
        stacked[block, width:, width:] = jnp.zeros_like(high)

    hops = (1, 2, 1, 2)

    def spot(way, kind, core, steps, turn):
        origin = (z - ways[way] * steps + cols) % cols
        part = way if turn == 0 else 1 - way
        return held.at[origin, core, pl.ds(part * (rows // 2), rows // 2)]

    def ring(way, kind, turn, arrives=False):
        back = 2 * (kind // 2)
        dst = spot(way, kind, rep, back + (hops[kind] if arrives else 0), turn)
        part = way if turn == 0 else 1 - way
        src = feat.at[rep, pl.ds(part * (rows // 2), rows // 2)] if kind < 2 and not arrives else dst
        return remote(
            src, dst, ring_send.at[way, kind, turn], ring_recv.at[way, kind, turn],
            col=(z + ways[way] * hops[kind] + cols) % cols,
        )

    def pair(way, kind, turn, core):
        dst = spot(way, kind, core, 2 * (kind // 2) + hops[kind], turn)
        return remote(dst, dst, pair_send.at[way, kind, turn], pair_recv.at[way, kind, turn], rep=other)

    def take(kind, way, core):
        steps = 2 * (kind // 2) + hops[kind]
        origin = (z - ways[way] * steps + cols) % cols
        put(origin * 2 + core, held[origin, core])

    both = (0, 1)
    for turn in both:
        for way in both:
            ring(way, 1, turn).start()
    for turn in both:
        for way in both:
            ring(way, 1, turn).wait_send()
            ring(way, 0, turn).start()
    for turn in both:
        for way in both:
            ring(way, 1, turn, arrives=True).wait_recv()
            if turn == 0:
                ring(way, 3, 0).start()
            ring(way, 2, turn).start()
            pair(way, 1, turn, rep).start()
    for turn in both:
        for way in both:
            ring(way, 0, turn, arrives=True).wait_recv()
            pair(way, 0, turn, rep).start()
    for core in both:
        put(z * 2 + core, feat[core])
    make_lists(count, dst, src, lists, line, dummies)
    for kind in (0, 1):
        for way in both:
            take(kind, way, rep)
    for turn in both:
        for kind in (2, 3) if turn == 0 else (2,):
            for way in both:
                ring(way, kind, turn, arrives=True).wait_recv()
                pair(way, kind, turn, rep).start()
    for kind in (1, 0):
        for way in both:
            for turn in both:
                pair(way, kind, turn, other).wait_recv()
            take(kind, way, other)
    for way in both:
        take(2, way, rep)
    take(3, 0, rep)
    for way in both:
        for turn in both:
            pair(way, 2, turn, other).wait_recv()
        take(2, way, other)
    for way in both:
        pair(way, 3, 0, other).wait_recv()
    take(3, 0, other)
    for kind in range(4):
        for way in both:
            for turn in both if kind < 3 else (0,):
                if kind != 1:
                    ring(way, kind, turn).wait_send()
                pair(way, kind, turn, rep).wait_send()
    loads[3].wait()


def gather_features(count, dst, src, feat, tiles, cols, rows):
    block, width = feat.shape[1:]
    sems = (2, 4, 2)
    vmem = pl.BlockSpec(memory_space=VMEM)
    far = pl.BlockSpec(memory_space=pl.ANY)
    return pl.pallas_call(
        functools.partial(gather_kernel, cols, (rows, 2 * cols)),
        out_shape=(
            jax.ShapeDtypeStruct((cols * 2, 2 * width, 2 * width), BF16),
            jax.ShapeDtypeStruct((8, LIST), jnp.int32),
            VMEM(tiles.shape, F32),
        ),
        in_specs=[pl.BlockSpec(memory_space=pltpu.SMEM), far, far, far, far],
        out_specs=(vmem, vmem, vmem),
        scratch_shapes=[
            VMEM(feat.shape, F32), VMEM(dst.shape, jnp.int32), VMEM(src.shape, jnp.int32),
            VMEM((cols, 2, block, width), F32), VMEM((16, LIST), jnp.int32),
            DMA(sems), DMA(sems), DMA(sems), DMA(sems), DMA((4,)),
        ],
        compiler_params=pltpu.CompilerParams(
            collective_id=0, has_side_effects=True, vmem_limit_bytes=24 * MIB
        ),
        name="gather_features",
    )(*[pltpu.with_memory_space_constraint(x, pltpu.HBM) if x is not count else x for x in (count, dst, src, feat, tiles)])


LARGE, SMALL = 32, 8
SLOT, LOAD_DST, LOAD_SRC, ADD_DST, ADD_SRC, TOTAL = range(6)


def over_tiles(lists, step):
    total = lists[TOTAL, 0]
    large = total // LARGE

    def run(size, start):
        def body(group, carry):
            step(start + group * size, size)
            return carry

        return body

    lax.fori_loop(0, large, run(LARGE, 0), 0)
    rest = total - large * LARGE
    lax.fori_loop(0, (rest + (SMALL - 1)) // SMALL, run(SMALL, large * LARGE), 0)


def forward_kernel(lists, tiles, stacked, sums, weight):
    block = tiles.shape[1]
    live = sums.shape[0] - 1
    sums[...] = jnp.zeros_like(sums)
    weight[...] = jnp.zeros_like(weight)

    def step(start, size):
        parts = []
        for u in range(size):
            place = start + u
            tile = tiles[lists[SLOT, place]]
            high, low = split(tile)
            product = jnp.dot(
                jnp.concatenate([high, low], axis=1), stacked[lists[LOAD_SRC, place]], preferred_element_type=F32
            )
            parts.append((lists[ADD_DST, place], product[:, :block] + product[:, block:], tile))
        for target, value, tile in parts:
            sums[target >> 2, target & 3, pl.ds(8, block)] += value
            weight[target] += tile

    over_tiles(lists, step)
    for target in range(4 * live):
        degree = jnp.sum(weight[target].T, axis=0, keepdims=True)
        sums[target >> 2, target & 3, pl.ds(0, 8)] = jnp.broadcast_to(degree, (8, block))


def backward_kernel(lists, tiles, stacked, hidden, sums, hidden_out, out_sem):
    copy = pltpu.make_async_copy(hidden, hidden_out, out_sem)
    copy.start()
    block = tiles.shape[1]
    sums[...] = jnp.zeros_like(sums)

    def step(start, size):
        parts = []
        for u in range(size):
            place = start + u
            high, low = split(tiles[lists[SLOT, place]])
            right = jnp.concatenate(
                [
                    jnp.concatenate([high, low], axis=1),
                    jnp.concatenate([high, jnp.zeros_like(high)], axis=1),
                ],
                axis=0,
            )
            product = jnp.dot(stacked[lists[LOAD_DST, place]], right, preferred_element_type=F32)
            parts.append((lists[ADD_SRC, place], product[:, :block] + product[:, block:]))
        for target, value in parts:
            sums[target] += value

    over_tiles(lists, step)
    copy.wait()


def forward(lists, tiles, stacked, out_shape):
    vmem = pl.BlockSpec(memory_space=VMEM)
    block = tiles.shape[1]
    return pl.pallas_call(
        forward_kernel,
        out_shape=jax.ShapeDtypeStruct(out_shape, F32),
        in_specs=[pl.BlockSpec(memory_space=pltpu.SMEM), vmem, vmem],
        out_specs=vmem,
        scratch_shapes=[VMEM((4 * out_shape[0] - 3, block, block), F32)],
        compiler_params=pltpu.CompilerParams(vmem_limit_bytes=32 * MIB),
        name="forward",
    )(lists, tiles, stacked)


def backward(lists, tiles, stacked, hidden, out_shape):
    vmem = pl.BlockSpec(memory_space=VMEM)
    shape = jax.ShapeDtypeStruct
    return pl.pallas_call(
        backward_kernel,
        out_shape=(shape(out_shape, F32), shape(hidden.shape, F32)),
        in_specs=[pl.BlockSpec(memory_space=pltpu.SMEM), vmem, vmem, vmem],
        out_specs=(vmem, pl.BlockSpec(memory_space=pl.ANY)),
        scratch_shapes=[DMA],
        compiler_params=pltpu.CompilerParams(vmem_limit_bytes=32 * MIB),
        name="backward",
    )(lists, tiles, stacked, hidden)


SIDE = 4
DEG = 8


def middle_kernel(
    sums, feat, cot, w_self, w_neigh, bias,
    hidden_out, stacked, direct_out, grad_part,
    far1, near1, part1, near2, gathered, hidden_half, hidden_got, direct_half, direct_got,
    grads, grads_got, grads_col,
    rs_send, rs_recv, ag_send, ag_recv, pair_send, pair_recv, col_send, col_recv, near_in,
):
    row = lax.axis_index("row")
    rep = lax.axis_index("rep")
    other = 1 - rep
    rows = SIDE * SIDE
    block = feat.shape[1]
    width = feat.shape[2]
    hid = w_self.shape[1] // 2
    coords = (row % SIDE, row // SIDE)
    low = block // 2
    spans = ((0, DEG + low), (DEG + low, low))
    far_first = (2, 1, 3)

    def at(axis, first, second):
        one = (coords[axis] + first + SIDE) % SIDE
        two = (coords[1 - axis] + second + SIDE) % SIDE
        return (two, one) if axis == 0 else (one, two)

    def device(axis, first, second):
        y, x = at(axis, first, second)
        return y * SIDE + x

    z = lax.axis_index("col")
    cols = grads.shape[1]
    around = (4, 3, 5, 2, 6, 1, 7)
    greet(
        [{"row": device(axis, off, 0)} for axis in (0, 1) for off in (1, -1)]
        + [{"col": (z + off + cols) % cols} for off in (1, -1)]
        + [{"rep": other}]
    )

    def tell(reach):
        for off in (reach, -reach):
            pl.semaphore_signal(
                near_in.at[reach - 1], inc=1, device_id={"col": (z + off + cols) % cols}, device_id_type=MESH
            )

    relay = {2: 0, 1: 0, 3: 1, 0: 1}
    ways = (1, -1)

    def rs0(axis, line):
        lo, n = spans[axis]
        y, x = at(axis, 2, line)
        return remote(
            sums.at[y, x, pl.ds(lo, n)], far1.at[axis, line, pl.ds(0, n)],
            rs_send.at[axis, 0, line], rs_recv.at[axis, 0, line], row=device(axis, ways[relay[line]], 0),
        )

    def rs1(axis, way, line):
        lo, n = spans[axis]
        y, x = at(axis, ways[way], line)
        if relay[line] == way:
            src = far1.at[axis, line, pl.ds(0, n)]
        else:
            src = sums.at[y, x, pl.ds(lo, n)]
        return remote(
            src, near1.at[axis, way, line, pl.ds(0, n)],
            rs_send.at[axis, 1 + way, line], rs_recv.at[axis, 1 + way, line], row=device(axis, ways[way], 0),
        )

    def rs2(axis, off):
        n = spans[axis][1]
        return remote(
            part1.at[axis, off, pl.ds(0, n)], near2.at[axis, off - 1, pl.ds(0, n)],
            rs_send.at[axis, 3, off], rs_recv.at[axis, 3, off], row=device(axis, 0, off),
        )

    lines = (2, 3, 1, 0)
    for line in (2, 3, 1):
        for axis in (0, 1):
            rs0(axis, line).start()
    for line in (2, 3, 1):
        for axis in (0, 1):
            rs1(axis, 1 - relay[line], line).start()
    for axis in (0, 1):
        rs0(axis, 0).start()
    tell(1)
    own_feat = split(feat[rep])
    self_parts = split(w_self[...])
    neigh_parts = split(w_neigh[...])
    pre_self = dot3(own_feat, self_parts) + bias[...]
    for line in lines:
        for axis in (0, 1):
            rs0(axis, line).wait_recv()
            way = relay[line]
            lo, n = spans[axis]
            y, x = at(axis, ways[way], line)
            far1[axis, line, pl.ds(0, n)] += sums[y, x, pl.ds(lo, n)]
            rs1(axis, way, line).start()
            if line == 1:
                rs1(axis, 1 - relay[0], 0).start()
    pl.semaphore_wait(near_in.at[0], 2)
    tell(2)
    for line in lines:
        for axis in (0, 1):
            for way in (0, 1):
                rs1(axis, way, line).wait_recv()
            lo, n = spans[axis]
            y, x = at(axis, 0, line)
            span = pl.ds(0, n)
            part1[axis, line, span] = sums[y, x, pl.ds(lo, n)] + (
                near1[axis, 0, line, span] + near1[axis, 1, line, span]
            )
            if line:
                rs2(axis, line).start()
    summed = []
    for axis in (0, 1):
        for off in far_first:
            rs2(axis, off).wait_recv()
        span = pl.ds(0, spans[axis][1])
        summed.append(
            (part1[axis, 0, span] + near2[axis, 0, span]) + (near2[axis, 1, span] + near2[axis, 2, span])
        )
    degree = summed[0][:1]
    inverse = 1.0 / jnp.maximum(degree, 1.0)
    inverse_down = jnp.broadcast_to(inverse, (block, block)).T
    total = jnp.concatenate([summed[0][DEG:], summed[1]], axis=0)
    aggregate = total * inverse_down
    preact = pre_self + dot3(aggregate, neigh_parts)
    gating = jax.nn.sigmoid(preact)
    grad_pre = cot[rep] * (gating * (1.0 + preact * (1.0 - gating)))
    grad_parts = split(grad_pre)
    y0, x0 = coords[1], coords[0]
    scaled = dot3(neigh_parts, grad_parts, ((1,), (1,))) * inverse
    gathered[y0, x0] = scaled

    def half_of(axis, first, second):
        y, x = at(axis, first, second)
        return gathered.at[y, x, pl.ds(axis * low, low)]

    def ag1(axis, off, arrives=False):
        ref = half_of(axis, -off if arrives else 0, 0)
        return remote(
            ref, ref, ag_send.at[axis, 0, off - 1], ag_recv.at[axis, 0, off - 1], row=device(axis, off, 0)
        )

    def ag2(axis, back, off, arrives=False):
        ref = half_of(axis, -back, -off if arrives else 0)
        return remote(
            ref, ref, ag_send.at[axis, 1 + back, off - 1], ag_recv.at[axis, 1 + back, off - 1],
            row=device(axis, 0, off),
        )

    def convert(axis, first, second):
        y, x = at(axis, first, second)
        span = pl.ds(axis * low, low)
        high, small = split(gathered[y, x, span])
        stacked[y * SIDE + x, span, :block] = high
        stacked[y * SIDE + x, span, block:] = small

    for off in far_first:
        for axis in (0, 1):
            ag1(axis, off).start()
    for off in far_first:
        for axis in (0, 1):
            ag2(axis, 0, off).start()
    hidden = preact * gating
    for core in (0, 1):
        hidden_half[core] = hidden[:, core * hid : (core + 1) * hid]
    hidden_pair = remote(hidden_half.at[other], hidden_got, pair_send.at[1], pair_recv.at[1], rep=other)
    hidden_pair.start()
    grad_self = dot3(feat[rep].T, grad_parts)
    grad_neigh = dot3(aggregate.T, grad_parts)
    grad_bias = jnp.sum(grad_pre, axis=0, keepdims=True)
    share = 2 * width // cols
    for core in (0, 1):
        span = slice(core * hid, (core + 1) * hid)
        grads[core, : cols // 2, :share] = grad_self[:, span].reshape(cols // 2, share, hid)
        grads[core, cols // 2 :, :share] = grad_neigh[:, span].reshape(cols // 2, share, hid)
        grads[core, :, share:] = jnp.broadcast_to(grad_bias[None, :, span], (cols, 8, hid))
    grads_pair = remote(grads.at[other], grads_got, pair_send.at[0], pair_recv.at[0], rep=other)
    grads_pair.start()
    for off in (1, 3, 2):
        for axis in (0, 1):
            ag1(axis, off, arrives=True).wait_recv()
            for ahead in far_first:
                ag2(axis, off, ahead).start()
    direct = dot3(self_parts, grad_parts, ((1,), (1,)))
    direct_half[...] = direct.reshape(2, width // 2, block)
    direct_pair = remote(direct_half.at[other], direct_got, pair_send.at[2], pair_recv.at[2], rep=other)
    direct_pair.start()
    grads_pair.wait_recv()
    grads[rep] += grads_got[...]

    def to_col(off, arrives=False):
        return remote(
            grads.at[rep, (z + off) % cols], grads_col.at[(z + cols - off) % cols if arrives else z],
            col_send.at[off - 1], col_recv.at[off - 1], col=(z + off) % cols,
        )

    pl.semaphore_wait(near_in.at[1], 2)
    for off in around:
        to_col(off).start()
    grads_col[z] = grads[rep, z]
    hidden_out[rep] = hidden_half[rep]
    direct_out[rep] = direct_half[rep]
    for axis in (0, 1):
        for off in (0, 1, 3, 2):
            convert(axis, -off, 0)
    hidden_pair.wait_recv()
    hidden_out[other] = hidden_got[...]
    direct_pair.wait_recv()
    direct_out[other] = direct_got[...]
    for back in (0, 1, 3, 2):
        for ahead in (1, 3, 2):
            for axis in (0, 1):
                ag2(axis, back, ahead, arrives=True).wait_recv()
                convert(axis, -back, -ahead)
    for off in around:
        to_col(off, arrives=True).wait_recv()
    value = grads_col[0]
    for place in range(1, cols):
        value = value + grads_col[place]
    grad_part[...] = value
    for axis in (0, 1):
        for off in far_first:
            for back in range(SIDE):
                ag2(axis, back, off).wait_send()
            rs2(axis, off).wait_send()
            ag1(axis, off).wait_send()
        for line in lines:
            rs0(axis, line).wait_send()
            for way in (0, 1):
                rs1(axis, way, line).wait_send()
    for off in around:
        to_col(off).wait_send()
    for copy in (grads_pair, hidden_pair, direct_pair):
        copy.wait_send()


def middle(sums, feat, cot, w_self, w_neigh, bias, cols):
    block, width = feat.shape[1:]
    hid = w_self.shape[1] // 2
    rows = SIDE * SIDE
    n = DEG + block // 2
    share = 2 * width // cols + 8
    vmem = pl.BlockSpec(memory_space=VMEM)
    shape = jax.ShapeDtypeStruct
    return pl.pallas_call(
        middle_kernel,
        out_shape=(
            shape((2, block, hid), F32),
            shape((rows, width, 2 * block), BF16),
            shape((2, width // 2, block), F32),
            shape((share, hid), F32),
        ),
        in_specs=[vmem] * 6,
        out_specs=(vmem,) * 4,
        scratch_shapes=[
            VMEM((2, SIDE, n, width), F32),
            VMEM((2, 2, SIDE, n, width), F32),
            VMEM((2, SIDE, n, width), F32),
            VMEM((2, SIDE - 1, n, width), F32),
            VMEM((SIDE, SIDE, width, block), F32),
            VMEM((2, block, hid), F32),
            VMEM((block, hid), F32),
            VMEM((2, width // 2, block), F32),
            VMEM((width // 2, block), F32),
            VMEM((2, cols, share, hid), F32),
            VMEM((cols, share, hid), F32),
            VMEM((cols, share, hid), F32),
            DMA((2, 4, SIDE)),
            DMA((2, 4, SIDE)),
            DMA((2, SIDE + 1, SIDE - 1)),
            DMA((2, SIDE + 1, SIDE - 1)),
            DMA((3,)),
            DMA((3,)),
            DMA((cols - 1,)),
            DMA((cols - 1,)),
            pltpu.SemaphoreType.REGULAR((2,)),
        ],
        compiler_params=pltpu.CompilerParams(
            collective_id=1, has_side_effects=True, vmem_limit_bytes=20 * MIB
        ),
        name="middle",
    )(sums, feat, cot, w_self, w_neigh, bias)


def last_kernel(
    cols, factor, sums, direct, grad_part,
    grad_feat, grad_weights, grad_bias,
    own, pair_got, got_one, got_two, got_three, got_four, got_x, line, got_y, final,
    pair_send, pair_recv, ring_send, ring_recv, col_send, col_recv, row_send, row_recv, near_in,
):
    row = lax.axis_index("row")
    z = lax.axis_index("col")
    rep = lax.axis_index("rep")
    other = 1 - rep
    half = sums.shape[1] // 2
    share = final.shape[1]
    ways = (1, -1)
    x, y = row % SIDE, row // SIDE
    far_first = (2, 1, 3)
    x_peers = {off: y * SIDE + (x + off) % SIDE for off in far_first}
    y_peers = {off: ((y + off) % SIDE) * SIDE + x for off in far_first}
    next_to = (
        [{"col": (z + off + cols) % cols} for off in (1, -1)],
        [{"row": x_peers[off]} for off in (1, 3)],
        [{"row": y_peers[off]} for off in (1, 3)],
    )
    greet(next_to[0] + next_to[1] + next_to[2] + [{"rep": other}])

    def ahead(off):
        return (z + off + 2 * cols) % cols

    def pair(off):
        at = ahead(off)
        return remote(
            sums.at[pl.ds(2 * at, 2), pl.ds(other * half, half)], pair_got.at[at],
            pair_send.at[off + 3], pair_recv.at[off + 3], rep=other,
        )

    def merge(off):
        at = ahead(off)
        pair(off).wait_recv()
        own[at] = sums[pl.ds(2 * at, 2), pl.ds(pl.multiple_of(rep * half, half), half)] + pair_got[at]

    hops = (1, 2, 1, 2, 2)
    got = (got_one, got_two, got_three, got_four, got_two)

    def ring(way, kind):
        at = ahead(ways[way] * (kind % 4 + 1 if kind < 4 else 2))
        src, dst = own.at[at], got[kind].at[way]
        if kind in (1, 3, 4):
            part = 1 - way if kind == 4 else way
            src = src.at[part]
            if kind != 3:
                dst = dst.at[part]
        return remote(
            src, dst, ring_send.at[way, kind], ring_recv.at[way, kind], col=ahead(ways[way] * hops[kind])
        )

    def to_x(off, arrives=False):
        return remote(
            grad_part, got_x.at[(x + SIDE - off) % SIDE if arrives else x],
            row_send.at[0, off - 1], row_recv.at[0, off - 1], row=x_peers[off],
        )

    def to_y(off, arrives=False):
        return remote(
            line, got_y.at[(y + SIDE - off) % SIDE if arrives else y],
            row_send.at[1, off - 1], row_recv.at[1, off - 1], row=y_peers[off],
        )

    def to_col(off, arrives=False):
        ref = final.at[ahead(-off) if arrives else z]
        return remote(ref, ref, col_send.at[off - 1], col_recv.at[off - 1], col=ahead(off))

    order = (3, -3, 4, 1, -1, 2, -2, 0)
    around = (4, 3, 5, 2, 6, 1, 7)
    for off in order:
        pair(off).start()
    for off in (1, 3):
        to_x(off).start()
    for axis in range(3):
        for where in next_to[axis]:
            pl.semaphore_signal(near_in.at[axis], inc=1, device_id=where, device_id_type=MESH)
    got_x[x] = grad_part[...]
    for off in order[:5]:
        if off == 4:
            pl.semaphore_wait(near_in.at[0], 2)
            pl.semaphore_wait(near_in.at[1], 2)
            to_x(2).start()
        merge(off)
        for way in (0, 1):
            if off == 4 or off * ways[way] > 0:
                ring(way, abs(off) - 1).start()
    merge(2)
    merge(-2)
    for off in far_first:
        to_x(off, arrives=True).wait_recv()
    line[...] = (got_x[0] + got_x[1]) + (got_x[2] + got_x[3])
    pl.semaphore_wait(near_in.at[2], 2)
    for off in far_first:
        to_y(off).start()
    got_y[y] = line[...]
    for way in (0, 1):
        ring(way, 2).wait_recv()
        own[ahead(2 * ways[way])] += got_three[way]
        ring(way, 4).start()
    for way in (0, 1):
        ring(way, 3).wait_recv()
        own[ahead(2 * ways[way]), way] += got_four[way]
        ring(way, 1).start()
    merge(0)
    for off in far_first:
        to_y(off, arrives=True).wait_recv()
    value = ((got_y[0] + got_y[1]) + (got_y[2] + got_y[3])) * factor
    final[z] = value[:share]
    for off in around:
        to_col(off).start()
    grad_bias[...] = value[share:]
    for way in (0, 1):
        ring(way, 0).wait_recv()
    grad_feat[...] = (direct[...] + own[z]) + (got_one[0] + got_one[1])
    for way in (0, 1):
        ring(way, 4).wait_recv()
        ring(way, 1).wait_recv()
    grad_feat[...] += got_two[0] + got_two[1]
    for off in around:
        to_col(off, arrives=True).wait_recv()
    grad_weights[...] = final[...]
    for off in order:
        pair(off).wait_send()
    for way in (0, 1):
        for kind in range(5):
            ring(way, kind).wait_send()
    for off in around:
        to_col(off).wait_send()
    for off in far_first:
        to_x(off).wait_send()
        to_y(off).wait_send()


def last(sums, direct, grad_part, cols, factor):
    width, block = sums.shape[1:]
    hid = grad_part.shape[1]
    share = 2 * width // cols
    vmem = pl.BlockSpec(memory_space=VMEM)
    return pl.pallas_call(
        functools.partial(last_kernel, cols, factor),
        out_shape=(
            VMEM((2, width // 2, block), F32),
            VMEM((cols, share, hid), F32),
            VMEM((8, hid), F32),
        ),
        in_specs=[vmem] * 3,
        out_specs=(vmem,) * 3,
        scratch_shapes=[
            VMEM((cols, 2, width // 2, block), F32),
            VMEM((cols, 2, width // 2, block), F32),
            VMEM((2, 2, width // 2, block), F32),
            VMEM((2, 2, width // 2, block), F32),
            VMEM((2, 2, width // 2, block), F32),
            VMEM((2, width // 2, block), F32),
            VMEM((SIDE, share + 8, hid), F32),
            VMEM((share + 8, hid), F32),
            VMEM((SIDE, share + 8, hid), F32),
            VMEM((cols, share, hid), F32),
            DMA((cols,)),
            DMA((cols,)),
            DMA((2, 5)),
            DMA((2, 5)),
            DMA((cols - 1,)),
            DMA((cols - 1,)),
            DMA((2, SIDE - 1)),
            DMA((2, SIDE - 1)),
            pltpu.SemaphoreType.REGULAR((3,)),
        ],
        compiler_params=pltpu.CompilerParams(
            collective_id=2, has_side_effects=True, vmem_limit_bytes=16 * MIB
        ),
        name="last",
    )(sums, direct, grad_part)


def finish_kernel(grad_feat, grad_weights, grad_bias, feat_out, self_out, neigh_out, bias_out, sems):
    block = grad_feat.shape[2]
    pieces = [
        (grad_feat.at[0], feat_out.at[:, pl.ds(0, block)]),
        (grad_feat.at[1], feat_out.at[:, pl.ds(block, block)]),
        (grad_weights.at[0], self_out),
        (grad_weights.at[1], neigh_out),
        (grad_bias.at[pl.ds(0, 1)], bias_out),
    ]
    copies = [pltpu.make_async_copy(src, dst, sems.at[at]) for at, (src, dst) in enumerate(pieces)]
    for copy in copies:
        copy.start()
    for copy in copies:
        copy.wait()


def finish(grad_feat, grad_weights, grad_bias):
    half, block = grad_feat.shape[1:]
    hid = grad_bias.shape[1]
    vmem = pl.BlockSpec(memory_space=VMEM)
    far = pl.BlockSpec(memory_space=pl.ANY)
    shape = jax.ShapeDtypeStruct
    return pl.pallas_call(
        finish_kernel,
        out_shape=(
            shape((half, 2 * block), F32), shape((2 * half, hid), F32), shape((2 * half, hid), F32), shape((1, hid), F32)
        ),
        in_specs=[vmem] * 3,
        out_specs=(far,) * 4,
        scratch_shapes=[DMA((5,))],
        compiler_params=pltpu.CompilerParams(vmem_limit_bytes=8 * MIB),
        name="finish",
    )(grad_feat, grad_weights.reshape(2, 2 * half, hid), grad_bias)


def shards(features, cotangent, w_self, w_neigh, bias, tiles, tile_dst, tile_src, tile_count):
    slots, block = tiles.shape[2:4]
    width = features.shape[1]
    hid = w_self.shape[1]
    cols = lax.axis_size("col")
    rows = lax.axis_size("row")
    tiles = tiles.reshape(slots, block, block)
    feat = features.reshape(2, block, width)
    cot = cotangent.reshape(2, block, hid)

    stacked, lists, tiles = gather_features(tile_count, tile_dst, tile_src, feat, tiles, cols, rows)
    sums = forward(lists, tiles, stacked, (SIDE + 1, SIDE, block + DEG, width))
    hidden, scaled, direct, grad_part = middle(sums, feat, cot, w_self, w_neigh, bias.reshape(1, hid), cols)
    back, hidden = backward(lists, tiles, scaled, hidden, (2 * cols + 1, width, block))
    factor = float(features.shape[0] * rows * cols) ** (-0.5)
    grad_feat, grad_self, grad_neigh, grad_bias = finish(*last(back, direct, grad_part, cols, factor))
    return (
        hidden.reshape(2 * block, hid // 2), grad_feat.T, grad_self, grad_neigh, grad_bias.reshape(hid // 2)
    )


def solution(mesh):
    return jax.shard_map(
        shards,
        mesh=mesh,
        in_specs=(
            P(("row", "col"), None),
            P(("row", "col"), None),
            P(),
            P(),
            P(),
            P("row", "col", None, None, None),
            P("row", "col", None),
            P("row", "col", None),
            P("row", "col"),
        ),
        out_specs=(
            P(("row", "col"), "rep"),
            P(("row", "col"), "rep"),
            P(None, "rep"),
            P(None, "rep"),
            P("rep"),
        ),
        check_vma=False,
    )
```

```python
import functools

import jax
import jax.numpy as jnp
from jax import lax
from jax.experimental import pallas as pl
from jax.experimental.pallas import tpu as pltpu
from jax.sharding import PartitionSpec as P

MESH = pl.DeviceIdType.MESH
F32 = jnp.float32
BF16 = jnp.bfloat16
VMEM = pltpu.VMEM
DMA = pltpu.SemaphoreType.DMA
MIB = 1 << 20


def split(value):
    high = value.astype(BF16)
    low = (value - high.astype(F32)).astype(BF16)
    return high, low


def dot3(left, right, dims=((1,), (0,))):
    left_high, left_low = left if isinstance(left, tuple) else split(left)
    right_high, right_low = right if isinstance(right, tuple) else split(right)

    def one(a, b):
        return lax.dot_general(a, b, (dims, ((), ())), preferred_element_type=F32)

    return one(left_high, right_high) + (one(left_high, right_low) + one(left_low, right_high))


def remote(src, dst, send, recv, **where):
    return pltpu.make_async_remote_copy(
        src_ref=src, dst_ref=dst, send_sem=send, recv_sem=recv, device_id=where, device_id_type=MESH
    )


def greet(partners):
    barrier = pltpu.get_barrier_semaphore()
    for where in partners:
        pl.semaphore_signal(barrier, inc=1, device_id=where, device_id_type=MESH)
    pl.semaphore_wait(barrier, len(partners))


LIST = 256


def make_lists(count, dst, src, lists, line, dummies):
    rep = lax.axis_index("rep")
    slots = dst.shape[2]
    line[...] = jnp.zeros_like(line)
    line[0:1, :slots] = dst[0]
    line[8:9, :slots] = src[0]
    wide = (8, LIST)
    block = jnp.broadcast_to(line[0:1], wide)
    source = jnp.broadcast_to(line[8:9], wide)
    slot = lax.broadcasted_iota(jnp.int32, wide, 1)
    own = ((block & 1) == rep) & (slot < count[0, 0]) & (slot < slots)
    own = own.astype(jnp.int32).astype(F32)
    square = (LIST, LIST)
    down = lax.broadcasted_iota(jnp.int32, square, 0)
    before = (down < lax.broadcasted_iota(jnp.int32, square, 1)).astype(jnp.int32).astype(F32).astype(BF16)
    place = jnp.dot(own.astype(BF16), before, preferred_element_type=F32)
    place = jnp.where(own > 0.5, place, -1.0)
    total = jnp.broadcast_to(jnp.sum(own, axis=1, keepdims=True), wide)
    chosen = (jnp.broadcast_to(place[0:1], square) == down.astype(F32)).astype(jnp.int32).astype(F32).astype(BF16)
    kind = lax.broadcasted_iota(jnp.int32, wide, 0)
    values = jnp.where(kind == 0, slot, jnp.where(kind % 2 == 1, block >> 1, source)).astype(F32).astype(BF16)
    listed = lax.dot_general(values, chosen, (((1,), (1,)), ((), ())), preferred_element_type=F32)
    beyond = slot.astype(F32) >= total
    listed = jnp.where(beyond & (kind == 3), float(dummies[0]), listed)
    listed = jnp.where(beyond & (kind == 4), float(dummies[1]), listed)
    listed = jnp.where(kind == 5, total, listed)
    lists[...] = listed.astype(jnp.int32)


def gather_kernel(
    cols, dummies, count, dst_far, src_far, feat_far, tiles,
    stacked, lists, tiles_here,
    feat, dst, src, held, line, ring_send, ring_recv, pair_send, pair_recv, load_sems,
):
    loads = [
        pltpu.make_async_copy(far, here, load_sems.at[at])
        for at, (far, here) in enumerate(((feat_far, feat), (dst_far, dst), (src_far, src), (tiles, tiles_here)))
    ]
    for load in loads:
        load.start()
    z = lax.axis_index("col")
    rep = lax.axis_index("rep")
    other = 1 - rep
    rows = feat.shape[1]
    ways = (1, -1)
    greet([{"col": (z + off + cols) % cols} for off in (1, -1, 2, -2)] + [{"rep": other}])
    for load in loads[:3]:
        load.wait()

    def put(block, value):
        high, low = split(value)
        width = value.shape[1]
        stacked[block, :width, :width] = high
        stacked[block, :width, width:] = low
        stacked[block, width:, :width] = high
        stacked[block, width:, width:] = jnp.zeros_like(high)

    hops = (1, 2, 1, 2)

    def spot(way, kind, core, steps, turn):
        origin = (z - ways[way] * steps + cols) % cols
        part = way if turn == 0 else 1 - way
        return held.at[origin, core, pl.ds(part * (rows // 2), rows // 2)]

    def ring(way, kind, turn, arrives=False):
        back = 2 * (kind // 2)
        dst = spot(way, kind, rep, back + (hops[kind] if arrives else 0), turn)
        part = way if turn == 0 else 1 - way
        src = feat.at[rep, pl.ds(part * (rows // 2), rows // 2)] if kind < 2 and not arrives else dst
        return remote(
            src, dst, ring_send.at[way, kind, turn], ring_recv.at[way, kind, turn],
            col=(z + ways[way] * hops[kind] + cols) % cols,
        )

    def pair(way, kind, turn, core):
        dst = spot(way, kind, core, 2 * (kind // 2) + hops[kind], turn)
        return remote(dst, dst, pair_send.at[way, kind, turn], pair_recv.at[way, kind, turn], rep=other)

    def take(kind, way, core):
        steps = 2 * (kind // 2) + hops[kind]
        origin = (z - ways[way] * steps + cols) % cols
        put(origin * 2 + core, held[origin, core])

    both = (0, 1)
    for turn in both:
        for way in both:
            ring(way, 1, turn).start()
    for turn in both:
        for way in both:
            ring(way, 1, turn).wait_send()
            ring(way, 0, turn).start()
    for turn in both:
        for way in both:
            ring(way, 1, turn, arrives=True).wait_recv()
            if turn == 0:
                ring(way, 3, 0).start()
            ring(way, 2, turn).start()
            pair(way, 1, turn, rep).start()
    for turn in both:
        for way in both:
            ring(way, 0, turn, arrives=True).wait_recv()
            pair(way, 0, turn, rep).start()
    for core in both:
        put(z * 2 + core, feat[core])
    make_lists(count, dst, src, lists, line, dummies)
    for kind in (0, 1):
        for way in both:
            take(kind, way, rep)
    for turn in both:
        for kind in (2, 3) if turn == 0 else (2,):
            for way in both:
                ring(way, kind, turn, arrives=True).wait_recv()
                pair(way, kind, turn, rep).start()
    for kind in (1, 0):
        for way in both:
            for turn in both:
                pair(way, kind, turn, other).wait_recv()
            take(kind, way, other)
    for way in both:
        take(2, way, rep)
    take(3, 0, rep)
    loads[3].wait()
    for way in both:
        for turn in both:
            for kind in (0, 2):
                ring(way, kind, turn).wait_send()
            for kind in (0, 1):
                pair(way, kind, turn, rep).wait_send()
        ring(way, 3, 0).wait_send()
    for way in both:
        for turn in both:
            pair(way, 2, turn, other).wait_recv()
        take(2, way, other)
    for way in both:
        pair(way, 3, 0, other).wait_recv()
    take(3, 0, other)
    for kind in (2, 3):
        for way in both:
            for turn in both if kind < 3 else (0,):
                pair(way, kind, turn, rep).wait_send()


def gather_features(count, dst, src, feat, tiles, cols, rows):
    block, width = feat.shape[1:]
    sems = (2, 4, 2)
    vmem = pl.BlockSpec(memory_space=VMEM)
    far = pl.BlockSpec(memory_space=pl.ANY)
    return pl.pallas_call(
        functools.partial(gather_kernel, cols, (rows, 2 * cols)),
        out_shape=(
            jax.ShapeDtypeStruct((cols * 2, 2 * width, 2 * width), BF16),
            jax.ShapeDtypeStruct((8, LIST), jnp.int32),
            VMEM(tiles.shape, F32),
        ),
        in_specs=[pl.BlockSpec(memory_space=pltpu.SMEM), far, far, far, far],
        out_specs=(vmem, vmem, vmem),
        scratch_shapes=[
            VMEM(feat.shape, F32), VMEM(dst.shape, jnp.int32), VMEM(src.shape, jnp.int32),
            VMEM((cols, 2, block, width), F32), VMEM((16, LIST), jnp.int32),
            DMA(sems), DMA(sems), DMA(sems), DMA(sems), DMA((4,)),
        ],
        compiler_params=pltpu.CompilerParams(
            collective_id=0, has_side_effects=True, vmem_limit_bytes=24 * MIB
        ),
        name="gather_features",
    )(*[pltpu.with_memory_space_constraint(x, pltpu.HBM) if x is not count else x for x in (count, dst, src, feat, tiles)])


LARGE, SMALL = 32, 8
SLOT, LOAD_DST, LOAD_SRC, ADD_DST, ADD_SRC, TOTAL = range(6)


def over_tiles(lists, step):
    total = lists[TOTAL, 0]
    large = total // LARGE

    def run(size, start):
        def body(group, carry):
            step(start + group * size, size)
            return carry

        return body

    lax.fori_loop(0, large, run(LARGE, 0), 0)
    rest = total - large * LARGE
    lax.fori_loop(0, (rest + (SMALL - 1)) // SMALL, run(SMALL, large * LARGE), 0)


def forward_kernel(lists, tiles, stacked, sums, weight):
    block = tiles.shape[1]
    live = sums.shape[0] - 1
    sums[...] = jnp.zeros_like(sums)
    weight[...] = jnp.zeros_like(weight)

    def step(start, size):
        parts = []
        for u in range(size):
            place = start + u
            tile = tiles[lists[SLOT, place]]
            high, low = split(tile)
            product = jnp.dot(
                jnp.concatenate([high, low], axis=1), stacked[lists[LOAD_SRC, place]], preferred_element_type=F32
            )
            parts.append((lists[ADD_DST, place], product[:, :block] + product[:, block:], tile))
        for target, value, tile in parts:
            sums[target >> 2, target & 3, pl.ds(8, block)] += value
            weight[target] += tile

    over_tiles(lists, step)
    for target in range(4 * live):
        degree = jnp.sum(weight[target].T, axis=0, keepdims=True)
        sums[target >> 2, target & 3, pl.ds(0, 8)] = jnp.broadcast_to(degree, (8, block))


def backward_kernel(lists, tiles, stacked, hidden, sums, hidden_out, out_sem):
    copy = pltpu.make_async_copy(hidden, hidden_out, out_sem)
    copy.start()
    block = tiles.shape[1]
    sums[...] = jnp.zeros_like(sums)

    def step(start, size):
        parts = []
        for u in range(size):
            place = start + u
            high, low = split(tiles[lists[SLOT, place]])
            right = jnp.concatenate(
                [
                    jnp.concatenate([high, low], axis=1),
                    jnp.concatenate([high, jnp.zeros_like(high)], axis=1),
                ],
                axis=0,
            )
            product = jnp.dot(stacked[lists[LOAD_DST, place]], right, preferred_element_type=F32)
            parts.append((lists[ADD_SRC, place], product[:, :block] + product[:, block:]))
        for target, value in parts:
            sums[target] += value

    over_tiles(lists, step)
    copy.wait()


def forward(lists, tiles, stacked, out_shape):
    vmem = pl.BlockSpec(memory_space=VMEM)
    block = tiles.shape[1]
    return pl.pallas_call(
        forward_kernel,
        out_shape=jax.ShapeDtypeStruct(out_shape, F32),
        in_specs=[pl.BlockSpec(memory_space=pltpu.SMEM), vmem, vmem],
        out_specs=vmem,
        scratch_shapes=[VMEM((4 * out_shape[0] - 3, block, block), F32)],
        compiler_params=pltpu.CompilerParams(vmem_limit_bytes=32 * MIB),
        name="forward",
    )(lists, tiles, stacked)


def backward(lists, tiles, stacked, hidden, out_shape):
    vmem = pl.BlockSpec(memory_space=VMEM)
    shape = jax.ShapeDtypeStruct
    return pl.pallas_call(
        backward_kernel,
        out_shape=(shape(out_shape, F32), shape(hidden.shape, F32)),
        in_specs=[pl.BlockSpec(memory_space=pltpu.SMEM), vmem, vmem, vmem],
        out_specs=(vmem, pl.BlockSpec(memory_space=pl.ANY)),
        scratch_shapes=[DMA],
        compiler_params=pltpu.CompilerParams(vmem_limit_bytes=32 * MIB),
        name="backward",
    )(lists, tiles, stacked, hidden)


SIDE = 4
DEG = 8


def middle_kernel(
    sums, feat, cot, w_self, w_neigh, bias,
    hidden_out, stacked, direct_out, grad_part,
    far1, near1, part1, near2, gathered, hidden_half, hidden_got, direct_half, direct_got,
    grads, grads_got, grads_col,
    rs_send, rs_recv, ag_send, ag_recv, pair_send, pair_recv, col_send, col_recv, near_in,
):
    row = lax.axis_index("row")
    rep = lax.axis_index("rep")
    other = 1 - rep
    rows = SIDE * SIDE
    block = feat.shape[1]
    width = feat.shape[2]
    hid = w_self.shape[1] // 2
    coords = (row % SIDE, row // SIDE)
    low = block // 2
    spans = ((0, DEG + low), (DEG + low, low))
    far_first = (2, 1, 3)

    def at(axis, first, second):
        one = (coords[axis] + first + SIDE) % SIDE
        two = (coords[1 - axis] + second + SIDE) % SIDE
        return (two, one) if axis == 0 else (one, two)

    def device(axis, first, second):
        y, x = at(axis, first, second)
        return y * SIDE + x

    z = lax.axis_index("col")
    cols = grads.shape[1]
    around = (4, 3, 5, 2, 6, 1, 7)
    greet(
        [{"row": device(axis, off, 0)} for axis in (0, 1) for off in (1, -1)]
        + [{"col": (z + off + cols) % cols} for off in (1, -1)]
        + [{"rep": other}]
    )

    def tell(reach):
        for off in (reach, -reach):
            pl.semaphore_signal(
                near_in.at[reach - 1], inc=1, device_id={"col": (z + off + cols) % cols}, device_id_type=MESH
            )

    relay = {2: 0, 1: 0, 3: 1, 0: 1}
    ways = (1, -1)

    def rs0(axis, line):
        lo, n = spans[axis]
        y, x = at(axis, 2, line)
        return remote(
            sums.at[y, x, pl.ds(lo, n)], far1.at[axis, line, pl.ds(0, n)],
            rs_send.at[axis, 0, line], rs_recv.at[axis, 0, line], row=device(axis, ways[relay[line]], 0),
        )

    def rs1(axis, way, line):
        lo, n = spans[axis]
        y, x = at(axis, ways[way], line)
        if relay[line] == way:
            src = far1.at[axis, line, pl.ds(0, n)]
        else:
            src = sums.at[y, x, pl.ds(lo, n)]
        return remote(
            src, near1.at[axis, way, line, pl.ds(0, n)],
            rs_send.at[axis, 1 + way, line], rs_recv.at[axis, 1 + way, line], row=device(axis, ways[way], 0),
        )

    def rs2(axis, off):
        n = spans[axis][1]
        return remote(
            part1.at[axis, off, pl.ds(0, n)], near2.at[axis, off - 1, pl.ds(0, n)],
            rs_send.at[axis, 3, off], rs_recv.at[axis, 3, off], row=device(axis, 0, off),
        )

    lines = (2, 3, 1, 0)
    for line in (2, 3, 1):
        for axis in (0, 1):
            rs0(axis, line).start()
    for line in (2, 3, 1):
        for axis in (0, 1):
            rs1(axis, 1 - relay[line], line).start()
    for axis in (0, 1):
        rs0(axis, 0).start()
    tell(1)
    own_feat = split(feat[rep])
    self_parts = split(w_self[...])
    neigh_parts = split(w_neigh[...])
    pre_self = dot3(own_feat, self_parts) + bias[...]
    for line in lines:
        for axis in (0, 1):
            rs0(axis, line).wait_recv()
            way = relay[line]
            lo, n = spans[axis]
            y, x = at(axis, ways[way], line)
            far1[axis, line, pl.ds(0, n)] += sums[y, x, pl.ds(lo, n)]
            rs1(axis, way, line).start()
            if line == 1:
                rs1(axis, 1 - relay[0], 0).start()
    pl.semaphore_wait(near_in.at[0], 2)
    tell(2)
    for line in lines:
        for axis in (0, 1):
            for way in (0, 1):
                rs1(axis, way, line).wait_recv()
            lo, n = spans[axis]
            y, x = at(axis, 0, line)
            span = pl.ds(0, n)
            part1[axis, line, span] = sums[y, x, pl.ds(lo, n)] + (
                near1[axis, 0, line, span] + near1[axis, 1, line, span]
            )
            if line:
                rs2(axis, line).start()
    summed = []
    for axis in (0, 1):
        for off in far_first:
            rs2(axis, off).wait_recv()
        span = pl.ds(0, spans[axis][1])
        summed.append(
            (part1[axis, 0, span] + near2[axis, 0, span]) + (near2[axis, 1, span] + near2[axis, 2, span])
        )
    degree = summed[0][:1]
    inverse = 1.0 / jnp.maximum(degree, 1.0)
    inverse_down = jnp.broadcast_to(inverse, (block, block)).T
    total = jnp.concatenate([summed[0][DEG:], summed[1]], axis=0)
    aggregate = total * inverse_down
    preact = pre_self + dot3(aggregate, neigh_parts)
    gating = jax.nn.sigmoid(preact)
    grad_pre = cot[rep] * (gating * (1.0 + preact * (1.0 - gating)))
    grad_parts = split(grad_pre)
    y0, x0 = coords[1], coords[0]
    scaled = dot3(neigh_parts, grad_parts, ((1,), (1,))) * inverse
    gathered[y0, x0] = scaled

    def half_of(axis, first, second):
        y, x = at(axis, first, second)
        return gathered.at[y, x, pl.ds(axis * low, low)]

    def ag1(axis, off, arrives=False):
        ref = half_of(axis, -off if arrives else 0, 0)
        return remote(
            ref, ref, ag_send.at[axis, 0, off - 1], ag_recv.at[axis, 0, off - 1], row=device(axis, off, 0)
        )

    def ag2(axis, back, off, arrives=False):
        ref = half_of(axis, -back, -off if arrives else 0)
        return remote(
            ref, ref, ag_send.at[axis, 1 + back, off - 1], ag_recv.at[axis, 1 + back, off - 1],
            row=device(axis, 0, off),
        )

    def convert(axis, first, second):
        y, x = at(axis, first, second)
        span = pl.ds(axis * low, low)
        high, small = split(gathered[y, x, span])
        stacked[y * SIDE + x, span, :block] = high
        stacked[y * SIDE + x, span, block:] = small

    for off in far_first:
        for axis in (0, 1):
            ag1(axis, off).start()
    for off in far_first:
        for axis in (0, 1):
            ag2(axis, 0, off).start()
    hidden = preact * gating
    for core in (0, 1):
        hidden_half[core] = hidden[:, core * hid : (core + 1) * hid]
    hidden_pair = remote(hidden_half.at[other], hidden_got, pair_send.at[1], pair_recv.at[1], rep=other)
    hidden_pair.start()
    grad_self = dot3(feat[rep].T, grad_parts)
    grad_neigh = dot3(aggregate.T, grad_parts)
    grad_bias = jnp.sum(grad_pre, axis=0, keepdims=True)
    share = 2 * width // cols
    for core in (0, 1):
        span = slice(core * hid, (core + 1) * hid)
        grads[core, : cols // 2, :share] = grad_self[:, span].reshape(cols // 2, share, hid)
        grads[core, cols // 2 :, :share] = grad_neigh[:, span].reshape(cols // 2, share, hid)
        grads[core, :, share:] = jnp.broadcast_to(grad_bias[None, :, span], (cols, 8, hid))
    grads_pair = remote(grads.at[other], grads_got, pair_send.at[0], pair_recv.at[0], rep=other)
    grads_pair.start()
    for off in (1, 3, 2):
        for axis in (0, 1):
            ag1(axis, off, arrives=True).wait_recv()
            for ahead in far_first:
                ag2(axis, off, ahead).start()
    direct = dot3(self_parts, grad_parts, ((1,), (1,)))
    direct_half[...] = direct.reshape(2, width // 2, block)
    direct_pair = remote(direct_half.at[other], direct_got, pair_send.at[2], pair_recv.at[2], rep=other)
    direct_pair.start()
    grads_pair.wait_recv()
    grads[rep] += grads_got[...]

    def to_col(off, arrives=False):
        return remote(
            grads.at[rep, (z + off) % cols], grads_col.at[(z + cols - off) % cols if arrives else z],
            col_send.at[off - 1], col_recv.at[off - 1], col=(z + off) % cols,
        )

    pl.semaphore_wait(near_in.at[1], 2)
    for off in around:
        to_col(off).start()
    grads_col[z] = grads[rep, z]
    hidden_out[rep] = hidden_half[rep]
    direct_out[rep] = direct_half[rep]
    for axis in (0, 1):
        for off in (0, 1, 3, 2):
            convert(axis, -off, 0)
    hidden_pair.wait_recv()
    hidden_out[other] = hidden_got[...]
    direct_pair.wait_recv()
    direct_out[other] = direct_got[...]
    for axis in (0, 1):
        for line in lines:
            rs0(axis, line).wait_send()
            for way in (0, 1):
                rs1(axis, way, line).wait_send()
        for off in far_first:
            rs2(axis, off).wait_send()
            ag1(axis, off).wait_send()
    for copy in (grads_pair, hidden_pair, direct_pair):
        copy.wait_send()
    for back in (0, 1, 3, 2):
        for ahead in (1, 3, 2):
            for axis in (0, 1):
                ag2(axis, back, ahead, arrives=True).wait_recv()
                convert(axis, -back, -ahead)
    for off in around:
        to_col(off, arrives=True).wait_recv()
    value = grads_col[0]
    for place in range(1, cols):
        value = value + grads_col[place]
    grad_part[...] = value
    for axis in (0, 1):
        for off in far_first:
            for back in range(SIDE):
                ag2(axis, back, off).wait_send()
    for off in around:
        to_col(off).wait_send()


def middle(sums, feat, cot, w_self, w_neigh, bias, cols):
    block, width = feat.shape[1:]
    hid = w_self.shape[1] // 2
    rows = SIDE * SIDE
    n = DEG + block // 2
    share = 2 * width // cols + 8
    vmem = pl.BlockSpec(memory_space=VMEM)
    shape = jax.ShapeDtypeStruct
    return pl.pallas_call(
        middle_kernel,
        out_shape=(
            shape((2, block, hid), F32),
            shape((rows, width, 2 * block), BF16),
            shape((2, width // 2, block), F32),
            shape((share, hid), F32),
        ),
        in_specs=[vmem] * 6,
        out_specs=(vmem,) * 4,
        scratch_shapes=[
            VMEM((2, SIDE, n, width), F32),
            VMEM((2, 2, SIDE, n, width), F32),
            VMEM((2, SIDE, n, width), F32),
            VMEM((2, SIDE - 1, n, width), F32),
            VMEM((SIDE, SIDE, width, block), F32),
            VMEM((2, block, hid), F32),
            VMEM((block, hid), F32),
            VMEM((2, width // 2, block), F32),
            VMEM((width // 2, block), F32),
            VMEM((2, cols, share, hid), F32),
            VMEM((cols, share, hid), F32),
            VMEM((cols, share, hid), F32),
            DMA((2, 4, SIDE)),
            DMA((2, 4, SIDE)),
            DMA((2, SIDE + 1, SIDE - 1)),
            DMA((2, SIDE + 1, SIDE - 1)),
            DMA((3,)),
            DMA((3,)),
            DMA((cols - 1,)),
            DMA((cols - 1,)),
            pltpu.SemaphoreType.REGULAR((2,)),
        ],
        compiler_params=pltpu.CompilerParams(
            collective_id=1, has_side_effects=True, vmem_limit_bytes=20 * MIB
        ),
        name="middle",
    )(sums, feat, cot, w_self, w_neigh, bias)


def last_kernel(
    cols, factor, sums, direct, grad_part,
    grad_feat, grad_weights, grad_bias,
    own, pair_got, got_one, got_two, got_three, got_four, got_x, line, got_y, final,
    pair_send, pair_recv, ring_send, ring_recv, col_send, col_recv, row_send, row_recv, near_in,
):
    row = lax.axis_index("row")
    z = lax.axis_index("col")
    rep = lax.axis_index("rep")
    other = 1 - rep
    half = sums.shape[1] // 2
    share = final.shape[1]
    ways = (1, -1)
    x, y = row % SIDE, row // SIDE
    far_first = (2, 1, 3)
    x_peers = {off: y * SIDE + (x + off) % SIDE for off in far_first}
    y_peers = {off: ((y + off) % SIDE) * SIDE + x for off in far_first}
    next_to = (
        [{"col": (z + off + cols) % cols} for off in (1, -1)],
        [{"row": x_peers[off]} for off in (1, 3)],
        [{"row": y_peers[off]} for off in (1, 3)],
    )
    greet(next_to[0] + next_to[1] + next_to[2] + [{"rep": other}])

    def ahead(off):
        return (z + off + 2 * cols) % cols

    def pair(off):
        at = ahead(off)
        return remote(
            sums.at[pl.ds(2 * at, 2), pl.ds(other * half, half)], pair_got.at[at],
            pair_send.at[off + 3], pair_recv.at[off + 3], rep=other,
        )

    def merge(off):
        at = ahead(off)
        pair(off).wait_recv()
        own[at] = sums[pl.ds(2 * at, 2), pl.ds(pl.multiple_of(rep * half, half), half)] + pair_got[at]

    hops = (1, 2, 1, 2, 2)
    got = (got_one, got_two, got_three, got_four, got_two)

    def ring(way, kind):
        at = ahead(ways[way] * (kind % 4 + 1 if kind < 4 else 2))
        src, dst = own.at[at], got[kind].at[way]
        if kind in (1, 3, 4):
            part = 1 - way if kind == 4 else way
            src = src.at[part]
            if kind != 3:
                dst = dst.at[part]
        return remote(
            src, dst, ring_send.at[way, kind], ring_recv.at[way, kind], col=ahead(ways[way] * hops[kind])
        )

    def to_x(off, arrives=False):
        return remote(
            grad_part, got_x.at[(x + SIDE - off) % SIDE if arrives else x],
            row_send.at[0, off - 1], row_recv.at[0, off - 1], row=x_peers[off],
        )

    def to_y(off, arrives=False):
        return remote(
            line, got_y.at[(y + SIDE - off) % SIDE if arrives else y],
            row_send.at[1, off - 1], row_recv.at[1, off - 1], row=y_peers[off],
        )

    def to_col(off, arrives=False):
        ref = final.at[ahead(-off) if arrives else z]
        return remote(ref, ref, col_send.at[off - 1], col_recv.at[off - 1], col=ahead(off))

    order = (3, -3, 4, 1, -1, 2, -2, 0)
    around = (4, 3, 5, 2, 6, 1, 7)
    for off in order:
        pair(off).start()
    for off in (1, 3):
        to_x(off).start()
    for axis in range(3):
        for where in next_to[axis]:
            pl.semaphore_signal(near_in.at[axis], inc=1, device_id=where, device_id_type=MESH)
    got_x[x] = grad_part[...]
    for off in order[:5]:
        if off == 4:
            pl.semaphore_wait(near_in.at[0], 2)
            pl.semaphore_wait(near_in.at[1], 2)
            to_x(2).start()
        merge(off)
        for way in (0, 1):
            if off == 4 or off * ways[way] > 0:
                ring(way, abs(off) - 1).start()
    merge(2)
    merge(-2)
    for off in far_first:
        to_x(off, arrives=True).wait_recv()
    line[...] = (got_x[0] + got_x[1]) + (got_x[2] + got_x[3])
    pl.semaphore_wait(near_in.at[2], 2)
    for off in far_first:
        to_y(off).start()
    got_y[y] = line[...]
    for way in (0, 1):
        ring(way, 2).wait_recv()
        own[ahead(2 * ways[way])] += got_three[way]
        ring(way, 4).start()
    for way in (0, 1):
        ring(way, 3).wait_recv()
        own[ahead(2 * ways[way]), way] += got_four[way]
        ring(way, 1).start()
    merge(0)
    for off in far_first:
        to_y(off, arrives=True).wait_recv()
    value = ((got_y[0] + got_y[1]) + (got_y[2] + got_y[3])) * factor
    final[z] = value[:share]
    for off in around:
        to_col(off).start()
    grad_bias[...] = value[share:]
    for way in (0, 1):
        ring(way, 0).wait_recv()
    grad_feat[...] = (direct[...] + own[z]) + (got_one[0] + got_one[1])
    for off in order:
        pair(off).wait_send()
    for way in (0, 1):
        for kind in (0, 2, 3):
            ring(way, kind).wait_send()
    for off in far_first:
        to_x(off).wait_send()
        to_y(off).wait_send()
    for way in (0, 1):
        ring(way, 4).wait_recv()
        ring(way, 1).wait_recv()
    grad_feat[...] += got_two[0] + got_two[1]
    for off in around:
        to_col(off, arrives=True).wait_recv()
    grad_weights[...] = final[...]
    for way in (0, 1):
        for kind in (1, 4):
            ring(way, kind).wait_send()
    for off in around:
        to_col(off).wait_send()


def last(sums, direct, grad_part, cols, factor):
    width, block = sums.shape[1:]
    hid = grad_part.shape[1]
    share = 2 * width // cols
    vmem = pl.BlockSpec(memory_space=VMEM)
    return pl.pallas_call(
        functools.partial(last_kernel, cols, factor),
        out_shape=(
            VMEM((2, width // 2, block), F32),
            VMEM((cols, share, hid), F32),
            VMEM((8, hid), F32),
        ),
        in_specs=[vmem] * 3,
        out_specs=(vmem,) * 3,
        scratch_shapes=[
            VMEM((cols, 2, width // 2, block), F32),
            VMEM((cols, 2, width // 2, block), F32),
            VMEM((2, 2, width // 2, block), F32),
            VMEM((2, 2, width // 2, block), F32),
            VMEM((2, 2, width // 2, block), F32),
            VMEM((2, width // 2, block), F32),
            VMEM((SIDE, share + 8, hid), F32),
            VMEM((share + 8, hid), F32),
            VMEM((SIDE, share + 8, hid), F32),
            VMEM((cols, share, hid), F32),
            DMA((cols,)),
            DMA((cols,)),
            DMA((2, 5)),
            DMA((2, 5)),
            DMA((cols - 1,)),
            DMA((cols - 1,)),
            DMA((2, SIDE - 1)),
            DMA((2, SIDE - 1)),
            pltpu.SemaphoreType.REGULAR((3,)),
        ],
        compiler_params=pltpu.CompilerParams(
            collective_id=2, has_side_effects=True, vmem_limit_bytes=16 * MIB
        ),
        name="last",
    )(sums, direct, grad_part)


def finish_kernel(grad_feat, grad_weights, grad_bias, feat_out, self_out, neigh_out, bias_out, sems):
    block = grad_feat.shape[2]
    pieces = [
        (grad_feat.at[0], feat_out.at[:, pl.ds(0, block)]),
        (grad_feat.at[1], feat_out.at[:, pl.ds(block, block)]),
        (grad_weights.at[0], self_out),
        (grad_weights.at[1], neigh_out),
        (grad_bias.at[pl.ds(0, 1)], bias_out),
    ]
    copies = [pltpu.make_async_copy(src, dst, sems.at[at]) for at, (src, dst) in enumerate(pieces)]
    for copy in copies:
        copy.start()
    for copy in copies:
        copy.wait()


def finish(grad_feat, grad_weights, grad_bias):
    half, block = grad_feat.shape[1:]
    hid = grad_bias.shape[1]
    vmem = pl.BlockSpec(memory_space=VMEM)
    far = pl.BlockSpec(memory_space=pl.ANY)
    shape = jax.ShapeDtypeStruct
    return pl.pallas_call(
        finish_kernel,
        out_shape=(
            shape((half, 2 * block), F32), shape((2 * half, hid), F32), shape((2 * half, hid), F32), shape((1, hid), F32)
        ),
        in_specs=[vmem] * 3,
        out_specs=(far,) * 4,
        scratch_shapes=[DMA((5,))],
        compiler_params=pltpu.CompilerParams(vmem_limit_bytes=8 * MIB),
        name="finish",
    )(grad_feat, grad_weights.reshape(2, 2 * half, hid), grad_bias)


def shards(features, cotangent, w_self, w_neigh, bias, tiles, tile_dst, tile_src, tile_count):
    slots, block = tiles.shape[2:4]
    width = features.shape[1]
    hid = w_self.shape[1]
    cols = lax.axis_size("col")
    rows = lax.axis_size("row")
    tiles = tiles.reshape(slots, block, block)
    feat = features.reshape(2, block, width)
    cot = cotangent.reshape(2, block, hid)

    stacked, lists, tiles = gather_features(tile_count, tile_dst, tile_src, feat, tiles, cols, rows)
    sums = forward(lists, tiles, stacked, (SIDE + 1, SIDE, block + DEG, width))
    hidden, scaled, direct, grad_part = middle(sums, feat, cot, w_self, w_neigh, bias.reshape(1, hid), cols)
    back, hidden = backward(lists, tiles, scaled, hidden, (2 * cols + 1, width, block))
    factor = float(features.shape[0] * rows * cols) ** (-0.5)
    grad_feat, grad_self, grad_neigh, grad_bias = finish(*last(back, direct, grad_part, cols, factor))
    return (
        hidden.reshape(2 * block, hid // 2), grad_feat.T, grad_self, grad_neigh, grad_bias.reshape(hid // 2)
    )


def solution(mesh):
    return jax.shard_map(
        shards,
        mesh=mesh,
        in_specs=(
            P(("row", "col"), None),
            P(("row", "col"), None),
            P(),
            P(),
            P(),
            P("row", "col", None, None, None),
            P("row", "col", None),
            P("row", "col", None),
            P("row", "col"),
        ),
        out_specs=(
            P(("row", "col"), "rep"),
            P(("row", "col"), "rep"),
            P(None, "rep"),
            P(None, "rep"),
            P("rep"),
        ),
        check_vma=False,
    )
```

```python
import functools

import jax
import jax.numpy as jnp
from jax import lax
from jax.experimental import pallas as pl
from jax.experimental.pallas import tpu as pltpu
from jax.sharding import PartitionSpec as P

MESH = pl.DeviceIdType.MESH
F32 = jnp.float32
BF16 = jnp.bfloat16
VMEM = pltpu.VMEM
DMA = pltpu.SemaphoreType.DMA
MIB = 1 << 20


def split(value):
    high = value.astype(BF16)
    low = (value - high.astype(F32)).astype(BF16)
    return high, low


def dot3(left, right, dims=((1,), (0,))):
    left_high, left_low = left if isinstance(left, tuple) else split(left)
    right_high, right_low = right if isinstance(right, tuple) else split(right)

    def one(a, b):
        return lax.dot_general(a, b, (dims, ((), ())), preferred_element_type=F32)

    return one(left_high, right_high) + (one(left_high, right_low) + one(left_low, right_high))


def remote(src, dst, send, recv, **where):
    return pltpu.make_async_remote_copy(
        src_ref=src, dst_ref=dst, send_sem=send, recv_sem=recv, device_id=where, device_id_type=MESH
    )


def greet(partners):
    barrier = pltpu.get_barrier_semaphore()
    for where in partners:
        pl.semaphore_signal(barrier, inc=1, device_id=where, device_id_type=MESH)
    pl.semaphore_wait(barrier, len(partners))


LIST = 256


def make_lists(count, dst, src, lists, line, dummies):
    rep = lax.axis_index("rep")
    slots = dst.shape[2]
    line[...] = jnp.zeros_like(line)
    line[0:1, :slots] = dst[0]
    line[8:9, :slots] = src[0]
    wide = (8, LIST)
    block = jnp.broadcast_to(line[0:1], wide)
    source = jnp.broadcast_to(line[8:9], wide)
    slot = lax.broadcasted_iota(jnp.int32, wide, 1)
    own = ((block & 1) == rep) & (slot < count[0, 0]) & (slot < slots)
    own = own.astype(jnp.int32).astype(F32)
    square = (LIST, LIST)
    down = lax.broadcasted_iota(jnp.int32, square, 0)
    before = (down < lax.broadcasted_iota(jnp.int32, square, 1)).astype(jnp.int32).astype(F32).astype(BF16)
    place = jnp.dot(own.astype(BF16), before, preferred_element_type=F32)
    place = jnp.where(own > 0.5, place, -1.0)
    total = jnp.broadcast_to(jnp.sum(own, axis=1, keepdims=True), wide)
    chosen = (jnp.broadcast_to(place[0:1], square) == down.astype(F32)).astype(jnp.int32).astype(F32).astype(BF16)
    kind = lax.broadcasted_iota(jnp.int32, wide, 0)
    values = jnp.where(kind == 0, slot, jnp.where(kind % 2 == 1, block >> 1, source)).astype(F32).astype(BF16)
    listed = lax.dot_general(values, chosen, (((1,), (1,)), ((), ())), preferred_element_type=F32)
    beyond = slot.astype(F32) >= total
    listed = jnp.where(beyond & (kind == 3), float(dummies[0]), listed)
    listed = jnp.where(beyond & (kind == 4), float(dummies[1]), listed)
    listed = jnp.where(kind == 5, total, listed)
    lists[...] = listed.astype(jnp.int32)


def gather_kernel(
    cols, dummies, count, dst_far, src_far, feat_far, tiles,
    stacked, lists, tiles_here,
    feat, dst, src, held, line, ring_send, ring_recv, pair_send, pair_recv, load_sems,
):
    loads = [
        pltpu.make_async_copy(far, here, load_sems.at[at])
        for at, (far, here) in enumerate(((feat_far, feat), (dst_far, dst), (src_far, src), (tiles, tiles_here)))
    ]
    for load in loads:
        load.start()
    z = lax.axis_index("col")
    rep = lax.axis_index("rep")
    other = 1 - rep
    rows = feat.shape[1]
    ways = (1, -1)
    greet([{"col": (z + off + cols) % cols} for off in (1, -1, 2, -2)] + [{"rep": other}])
    for load in loads[:3]:
        load.wait()

    def put(block, value):
        high, low = split(value)
        width = value.shape[1]
        stacked[block, :width, :width] = high
        stacked[block, :width, width:] = low
        stacked[block, width:, :width] = high
        stacked[block, width:, width:] = jnp.zeros_like(high)

    hops = (1, 2, 1, 2)

    def spot(way, kind, core, steps, turn):
        origin = (z - ways[way] * steps + cols) % cols
        part = way if turn == 0 else 1 - way
        return held.at[origin, core, pl.ds(part * (rows // 2), rows // 2)]

    def ring(way, kind, turn, arrives=False):
        back = 2 * (kind // 2)
        dst = spot(way, kind, rep, back + (hops[kind] if arrives else 0), turn)
        part = way if turn == 0 else 1 - way
        src = feat.at[rep, pl.ds(part * (rows // 2), rows // 2)] if kind < 2 and not arrives else dst
        return remote(
            src, dst, ring_send.at[way, kind, turn], ring_recv.at[way, kind, turn],
            col=(z + ways[way] * hops[kind] + cols) % cols,
        )

    def pair(way, kind, turn, core):
        dst = spot(way, kind, core, 2 * (kind // 2) + hops[kind], turn)
        return remote(dst, dst, pair_send.at[way, kind, turn], pair_recv.at[way, kind, turn], rep=other)

    def take(kind, way, core):
        steps = 2 * (kind // 2) + hops[kind]
        origin = (z - ways[way] * steps + cols) % cols
        put(origin * 2 + core, held[origin, core])

    both = (0, 1)
    for turn in both:
        for way in both:
            ring(way, 1, turn).start()
    for turn in both:
        for way in both:
            ring(way, 1, turn).wait_send()
            ring(way, 0, turn).start()
    for turn in both:
        for way in both:
            ring(way, 1, turn, arrives=True).wait_recv()
            if turn == 0:
                ring(way, 3, 0).start()
            ring(way, 2, turn).start()
            pair(way, 1, turn, rep).start()
    for turn in both:
        for way in both:
            ring(way, 0, turn, arrives=True).wait_recv()
            pair(way, 0, turn, rep).start()
    for core in both:
        put(z * 2 + core, feat[core])
    make_lists(count, dst, src, lists, line, dummies)
    for kind in (0, 1):
        for way in both:
            take(kind, way, rep)
    for turn in both:
        for kind in (2, 3) if turn == 0 else (2,):
            for way in both:
                ring(way, kind, turn, arrives=True).wait_recv()
                pair(way, kind, turn, rep).start()
    for kind in (1, 0):
        for way in both:
            for turn in both:
                pair(way, kind, turn, other).wait_recv()
            take(kind, way, other)
    for way in both:
        take(2, way, rep)
    take(3, 0, rep)
    loads[3].wait()
    for way in both:
        for turn in both:
            for kind in (0, 2):
                ring(way, kind, turn).wait_send()
            for kind in (0, 1):
                pair(way, kind, turn, rep).wait_send()
        ring(way, 3, 0).wait_send()
    for way in both:
        for turn in both:
            pair(way, 2, turn, other).wait_recv()
        take(2, way, other)
    for way in both:
        pair(way, 3, 0, other).wait_recv()
    take(3, 0, other)
    for kind in (2, 3):
        for way in both:
            for turn in both if kind < 3 else (0,):
                pair(way, kind, turn, rep).wait_send()


def gather_features(count, dst, src, feat, tiles, cols, rows):
    block, width = feat.shape[1:]
    sems = (2, 4, 2)
    vmem = pl.BlockSpec(memory_space=VMEM)
    far = pl.BlockSpec(memory_space=pl.ANY)
    return pl.pallas_call(
        functools.partial(gather_kernel, cols, (rows, 2 * cols)),
        out_shape=(
            jax.ShapeDtypeStruct((cols * 2, 2 * width, 2 * width), BF16),
            jax.ShapeDtypeStruct((8, LIST), jnp.int32),
            VMEM(tiles.shape, F32),
        ),
        in_specs=[pl.BlockSpec(memory_space=pltpu.SMEM), far, far, far, far],
        out_specs=(vmem, vmem, vmem),
        scratch_shapes=[
            VMEM(feat.shape, F32), VMEM(dst.shape, jnp.int32), VMEM(src.shape, jnp.int32),
            VMEM((cols, 2, block, width), F32), VMEM((16, LIST), jnp.int32),
            DMA(sems), DMA(sems), DMA(sems), DMA(sems), DMA((4,)),
        ],
        compiler_params=pltpu.CompilerParams(
            collective_id=0, has_side_effects=True, vmem_limit_bytes=24 * MIB
        ),
        name="gather_features",
    )(*[pltpu.with_memory_space_constraint(x, pltpu.HBM) if x is not count else x for x in (count, dst, src, feat, tiles)])


LARGE, SMALL = 32, 8
SLOT, LOAD_DST, LOAD_SRC, ADD_DST, ADD_SRC, TOTAL = range(6)


def over_tiles(lists, step):
    total = lists[TOTAL, 0]
    large = total // LARGE

    def run(size, start):
        def body(group, carry):
            step(start + group * size, size)
            return carry

        return body

    lax.fori_loop(0, large, run(LARGE, 0), 0)
    rest = total - large * LARGE
    lax.fori_loop(0, (rest + (SMALL - 1)) // SMALL, run(SMALL, large * LARGE), 0)


def forward_kernel(lists, tiles, stacked, sums, weight):
    block = tiles.shape[1]
    live = sums.shape[0] - 1
    sums[...] = jnp.zeros_like(sums)
    weight[...] = jnp.zeros_like(weight)

    def step(start, size):
        parts = []
        for u in range(size):
            place = start + u
            tile = tiles[lists[SLOT, place]]
            high, low = split(tile)
            product = jnp.dot(
                jnp.concatenate([high, low], axis=1), stacked[lists[LOAD_SRC, place]], preferred_element_type=F32
            )
            parts.append((lists[ADD_DST, place], product[:, :block] + product[:, block:], tile))
        for target, value, tile in parts:
            sums[target >> 2, target & 3, pl.ds(8, block)] += value
            weight[target] += tile

    over_tiles(lists, step)
    for target in range(4 * live):
        degree = jnp.sum(weight[target].T, axis=0, keepdims=True)
        sums[target >> 2, target & 3, pl.ds(0, 8)] = jnp.broadcast_to(degree, (8, block))


def backward_kernel(lists, tiles, stacked, hidden, sums, hidden_out, out_sem):
    copy = pltpu.make_async_copy(hidden, hidden_out, out_sem)
    copy.start()
    block = tiles.shape[1]
    sums[...] = jnp.zeros_like(sums)

    def step(start, size):
        parts = []
        for u in range(size):
            place = start + u
            high, low = split(tiles[lists[SLOT, place]])
            right = jnp.concatenate(
                [
                    jnp.concatenate([high, low], axis=1),
                    jnp.concatenate([high, jnp.zeros_like(high)], axis=1),
                ],
                axis=0,
            )
            product = jnp.dot(stacked[lists[LOAD_DST, place]], right, preferred_element_type=F32)
            parts.append((lists[ADD_SRC, place], product[:, :block] + product[:, block:]))
        for target, value in parts:
            sums[target] += value

    over_tiles(lists, step)
    copy.wait()


def forward(lists, tiles, stacked, out_shape):
    vmem = pl.BlockSpec(memory_space=VMEM)
    block = tiles.shape[1]
    return pl.pallas_call(
        forward_kernel,
        out_shape=jax.ShapeDtypeStruct(out_shape, F32),
        in_specs=[pl.BlockSpec(memory_space=pltpu.SMEM), vmem, vmem],
        out_specs=vmem,
        scratch_shapes=[VMEM((4 * out_shape[0] - 3, block, block), F32)],
        compiler_params=pltpu.CompilerParams(vmem_limit_bytes=32 * MIB),
        name="forward",
    )(lists, tiles, stacked)


def backward(lists, tiles, stacked, hidden, out_shape):
    vmem = pl.BlockSpec(memory_space=VMEM)
    shape = jax.ShapeDtypeStruct
    return pl.pallas_call(
        backward_kernel,
        out_shape=(shape(out_shape, F32), shape(hidden.shape, F32)),
        in_specs=[pl.BlockSpec(memory_space=pltpu.SMEM), vmem, vmem, vmem],
        out_specs=(vmem, pl.BlockSpec(memory_space=pl.ANY)),
        scratch_shapes=[DMA],
        compiler_params=pltpu.CompilerParams(vmem_limit_bytes=32 * MIB),
        name="backward",
    )(lists, tiles, stacked, hidden)


SIDE = 4
DEG = 8


def middle_kernel(
    sums, feat, cot, w_self, w_neigh, bias,
    hidden_out, stacked, direct_out, grad_part,
    far1, near1, part1, near2, gathered, hidden_half, hidden_got, direct_half, direct_got,
    grads, grads_got, grads_col,
    rs_send, rs_recv, ag_send, ag_recv, pair_send, pair_recv, col_send, col_recv, near_in,
):
    row = lax.axis_index("row")
    rep = lax.axis_index("rep")
    other = 1 - rep
    rows = SIDE * SIDE
    block = feat.shape[1]
    width = feat.shape[2]
    hid = w_self.shape[1] // 2
    coords = (row % SIDE, row // SIDE)
    low = block // 2
    spans = ((0, DEG + low), (DEG + low, low))
    far_first = (2, 1, 3)

    def at(axis, first, second):
        one = (coords[axis] + first + SIDE) % SIDE
        two = (coords[1 - axis] + second + SIDE) % SIDE
        return (two, one) if axis == 0 else (one, two)

    def device(axis, first, second):
        y, x = at(axis, first, second)
        return y * SIDE + x

    z = lax.axis_index("col")
    cols = grads.shape[1]
    around = (4, 3, 5, 2, 6, 1, 7)
    greet(
        [{"row": device(axis, off, 0)} for axis in (0, 1) for off in (1, -1)]
        + [{"col": (z + off + cols) % cols} for off in (1, -1)]
        + [{"rep": other}]
    )

    def tell(reach):
        for off in (reach, -reach):
            pl.semaphore_signal(
                near_in.at[reach - 1], inc=1, device_id={"col": (z + off + cols) % cols}, device_id_type=MESH
            )

    relay = {2: 0, 1: 0, 3: 1, 0: 1}
    ways = (1, -1)

    def rs0(axis, line):
        lo, n = spans[axis]
        y, x = at(axis, 2, line)
        return remote(
            sums.at[y, x, pl.ds(lo, n)], far1.at[axis, line, pl.ds(0, n)],
            rs_send.at[axis, 0, line], rs_recv.at[axis, 0, line], row=device(axis, ways[relay[line]], 0),
        )

    def rs1(axis, way, line):
        lo, n = spans[axis]
        y, x = at(axis, ways[way], line)
        if relay[line] == way:
            src = far1.at[axis, line, pl.ds(0, n)]
        else:
            src = sums.at[y, x, pl.ds(lo, n)]
        return remote(
            src, near1.at[axis, way, line, pl.ds(0, n)],
            rs_send.at[axis, 1 + way, line], rs_recv.at[axis, 1 + way, line], row=device(axis, ways[way], 0),
        )

    def rs2(axis, off):
        n = spans[axis][1]
        return remote(
            part1.at[axis, off, pl.ds(0, n)], near2.at[axis, off - 1, pl.ds(0, n)],
            rs_send.at[axis, 3, off], rs_recv.at[axis, 3, off], row=device(axis, 0, off),
        )

    lines = (2, 3, 1, 0)
    for line in (2, 3, 1):
        for axis in (0, 1):
            rs0(axis, line).start()
    for line in (2, 3, 1):
        for axis in (0, 1):
            rs1(axis, 1 - relay[line], line).start()
    for axis in (0, 1):
        rs0(axis, 0).start()
    tell(1)
    own_feat = split(feat[rep])
    self_parts = split(w_self[...])
    neigh_parts = split(w_neigh[...])
    pre_self = dot3(own_feat, self_parts) + bias[...]
    for line in lines:
        for axis in (0, 1):
            rs0(axis, line).wait_recv()
            way = relay[line]
            lo, n = spans[axis]
            y, x = at(axis, ways[way], line)
            far1[axis, line, pl.ds(0, n)] += sums[y, x, pl.ds(lo, n)]
            rs1(axis, way, line).start()
            if line == 1:
                rs1(axis, 1 - relay[0], 0).start()
    pl.semaphore_wait(near_in.at[0], 2)
    tell(2)
    for line in lines:
        for axis in (0, 1):
            for way in (0, 1):
                rs1(axis, way, line).wait_recv()
            lo, n = spans[axis]
            y, x = at(axis, 0, line)
            span = pl.ds(0, n)
            part1[axis, line, span] = sums[y, x, pl.ds(lo, n)] + (
                near1[axis, 0, line, span] + near1[axis, 1, line, span]
            )
            if line:
                rs2(axis, line).start()
    summed = []
    for axis in (0, 1):
        for off in far_first:
            rs2(axis, off).wait_recv()
        span = pl.ds(0, spans[axis][1])
        summed.append(
            (part1[axis, 0, span] + near2[axis, 0, span]) + (near2[axis, 1, span] + near2[axis, 2, span])
        )
    degree = summed[0][:1]
    inverse = 1.0 / jnp.maximum(degree, 1.0)
    inverse_down = jnp.broadcast_to(inverse, (block, block)).T
    total = jnp.concatenate([summed[0][DEG:], summed[1]], axis=0)
    aggregate = total * inverse_down
    preact = pre_self + dot3(aggregate, neigh_parts)
    gating = jax.nn.sigmoid(preact)
    grad_pre = cot[rep] * (gating * (1.0 + preact * (1.0 - gating)))
    grad_parts = split(grad_pre)
    y0, x0 = coords[1], coords[0]
    scaled = dot3(neigh_parts, grad_parts, ((1,), (1,))) * inverse
    gathered[y0, x0] = scaled

    def half_of(axis, first, second):
        y, x = at(axis, first, second)
        return gathered.at[y, x, pl.ds(axis * low, low)]

    def ag1(axis, off, arrives=False):
        ref = half_of(axis, -off if arrives else 0, 0)
        return remote(
            ref, ref, ag_send.at[axis, 0, off - 1], ag_recv.at[axis, 0, off - 1], row=device(axis, off, 0)
        )

    def ag2(axis, back, off, arrives=False):
        ref = half_of(axis, -back, -off if arrives else 0)
        return remote(
            ref, ref, ag_send.at[axis, 1 + back, off - 1], ag_recv.at[axis, 1 + back, off - 1],
            row=device(axis, 0, off),
        )

    def convert(axis, first, second):
        y, x = at(axis, first, second)
        span = pl.ds(axis * low, low)
        high, small = split(gathered[y, x, span])
        stacked[y * SIDE + x, span, :block] = high
        stacked[y * SIDE + x, span, block:] = small

    for off in far_first:
        for axis in (0, 1):
            ag1(axis, off).start()
    for off in far_first:
        for axis in (0, 1):
            ag2(axis, 0, off).start()
    grad_self = dot3(feat[rep].T, grad_parts)
    grad_neigh = dot3(aggregate.T, grad_parts)
    grad_bias = jnp.sum(grad_pre, axis=0, keepdims=True)
    share = 2 * width // cols
    for core in (0, 1):
        span = slice(core * hid, (core + 1) * hid)
        grads[core, : cols // 2, :share] = grad_self[:, span].reshape(cols // 2, share, hid)
        grads[core, cols // 2 :, :share] = grad_neigh[:, span].reshape(cols // 2, share, hid)
        grads[core, :, share:] = jnp.broadcast_to(grad_bias[None, :, span], (cols, 8, hid))
    grads_pair = remote(grads.at[other], grads_got, pair_send.at[0], pair_recv.at[0], rep=other)
    grads_pair.start()
    hidden = preact * gating
    for core in (0, 1):
        hidden_half[core] = hidden[:, core * hid : (core + 1) * hid]
    hidden_pair = remote(hidden_half.at[other], hidden_got, pair_send.at[1], pair_recv.at[1], rep=other)
    hidden_pair.start()
    for off in (1, 3, 2):
        for axis in (0, 1):
            ag1(axis, off, arrives=True).wait_recv()
            for ahead in far_first:
                ag2(axis, off, ahead).start()
    grads_pair.wait_recv()
    grads[rep] += grads_got[...]

    def to_col(off, arrives=False):
        return remote(
            grads.at[rep, (z + off) % cols], grads_col.at[(z + cols - off) % cols if arrives else z],
            col_send.at[off - 1], col_recv.at[off - 1], col=(z + off) % cols,
        )

    pl.semaphore_wait(near_in.at[1], 2)
    for off in around:
        to_col(off).start()
    grads_col[z] = grads[rep, z]
    direct = dot3(self_parts, grad_parts, ((1,), (1,)))
    direct_half[...] = direct.reshape(2, width // 2, block)
    direct_pair = remote(direct_half.at[other], direct_got, pair_send.at[2], pair_recv.at[2], rep=other)
    direct_pair.start()
    hidden_out[rep] = hidden_half[rep]
    direct_out[rep] = direct_half[rep]
    for axis in (0, 1):
        for off in (0, 1, 3, 2):
            convert(axis, -off, 0)
    hidden_pair.wait_recv()
    hidden_out[other] = hidden_got[...]
    direct_pair.wait_recv()
    direct_out[other] = direct_got[...]
    for axis in (0, 1):
        for line in lines:
            rs0(axis, line).wait_send()
            for way in (0, 1):
                rs1(axis, way, line).wait_send()
        for off in far_first:
            rs2(axis, off).wait_send()
            ag1(axis, off).wait_send()
    for copy in (grads_pair, hidden_pair, direct_pair):
        copy.wait_send()
    for back in (0, 1, 3, 2):
        for ahead in (1, 3, 2):
            for axis in (0, 1):
                ag2(axis, back, ahead, arrives=True).wait_recv()
                convert(axis, -back, -ahead)
    for off in around:
        to_col(off, arrives=True).wait_recv()
    value = grads_col[0]
    for place in range(1, cols):
        value = value + grads_col[place]
    grad_part[...] = value
    for axis in (0, 1):
        for off in far_first:
            for back in range(SIDE):
                ag2(axis, back, off).wait_send()
    for off in around:
        to_col(off).wait_send()


def middle(sums, feat, cot, w_self, w_neigh, bias, cols):
    block, width = feat.shape[1:]
    hid = w_self.shape[1] // 2
    rows = SIDE * SIDE
    n = DEG + block // 2
    share = 2 * width // cols + 8
    vmem = pl.BlockSpec(memory_space=VMEM)
    shape = jax.ShapeDtypeStruct
    return pl.pallas_call(
        middle_kernel,
        out_shape=(
            shape((2, block, hid), F32),
            shape((rows, width, 2 * block), BF16),
            shape((2, width // 2, block), F32),
            shape((share, hid), F32),
        ),
        in_specs=[vmem] * 6,
        out_specs=(vmem,) * 4,
        scratch_shapes=[
            VMEM((2, SIDE, n, width), F32),
            VMEM((2, 2, SIDE, n, width), F32),
            VMEM((2, SIDE, n, width), F32),
            VMEM((2, SIDE - 1, n, width), F32),
            VMEM((SIDE, SIDE, width, block), F32),
            VMEM((2, block, hid), F32),
            VMEM((block, hid), F32),
            VMEM((2, width // 2, block), F32),
            VMEM((width // 2, block), F32),
            VMEM((2, cols, share, hid), F32),
            VMEM((cols, share, hid), F32),
            VMEM((cols, share, hid), F32),
            DMA((2, 4, SIDE)),
            DMA((2, 4, SIDE)),
            DMA((2, SIDE + 1, SIDE - 1)),
            DMA((2, SIDE + 1, SIDE - 1)),
            DMA((3,)),
            DMA((3,)),
            DMA((cols - 1,)),
            DMA((cols - 1,)),
            pltpu.SemaphoreType.REGULAR((2,)),
        ],
        compiler_params=pltpu.CompilerParams(
            collective_id=1, has_side_effects=True, vmem_limit_bytes=20 * MIB
        ),
        name="middle",
    )(sums, feat, cot, w_self, w_neigh, bias)


def last_kernel(
    cols, factor, sums, direct, grad_part,
    grad_feat, grad_weights, grad_bias,
    own, pair_got, got_one, got_two, got_three, got_four, got_x, line, got_y, final,
    pair_send, pair_recv, ring_send, ring_recv, col_send, col_recv, row_send, row_recv, near_in,
):
    row = lax.axis_index("row")
    z = lax.axis_index("col")
    rep = lax.axis_index("rep")
    other = 1 - rep
    half = sums.shape[1] // 2
    share = final.shape[1]
    ways = (1, -1)
    x, y = row % SIDE, row // SIDE
    far_first = (2, 1, 3)
    x_peers = {off: y * SIDE + (x + off) % SIDE for off in far_first}
    y_peers = {off: ((y + off) % SIDE) * SIDE + x for off in far_first}
    next_to = (
        [{"col": (z + off + cols) % cols} for off in (1, -1)],
        [{"row": x_peers[off]} for off in (1, 3)],
        [{"row": y_peers[off]} for off in (1, 3)],
    )
    greet(next_to[0] + next_to[1] + next_to[2] + [{"rep": other}])

    def ahead(off):
        return (z + off + 2 * cols) % cols

    def pair(off):
        at = ahead(off)
        return remote(
            sums.at[pl.ds(2 * at, 2), pl.ds(other * half, half)], pair_got.at[at],
            pair_send.at[off + 3], pair_recv.at[off + 3], rep=other,
        )

    def merge(off):
        at = ahead(off)
        pair(off).wait_recv()
        own[at] = sums[pl.ds(2 * at, 2), pl.ds(pl.multiple_of(rep * half, half), half)] + pair_got[at]

    hops = (1, 2, 1, 2, 2)
    got = (got_one, got_two, got_three, got_four, got_two)

    def ring(way, kind):
        at = ahead(ways[way] * (kind % 4 + 1 if kind < 4 else 2))
        src, dst = own.at[at], got[kind].at[way]
        if kind in (1, 3, 4):
            part = 1 - way if kind == 4 else way
            src = src.at[part]
            if kind != 3:
                dst = dst.at[part]
        return remote(
            src, dst, ring_send.at[way, kind], ring_recv.at[way, kind], col=ahead(ways[way] * hops[kind])
        )

    def to_x(off, arrives=False):
        return remote(
            grad_part, got_x.at[(x + SIDE - off) % SIDE if arrives else x],
            row_send.at[0, off - 1], row_recv.at[0, off - 1], row=x_peers[off],
        )

    def to_y(off, arrives=False):
        return remote(
            line, got_y.at[(y + SIDE - off) % SIDE if arrives else y],
            row_send.at[1, off - 1], row_recv.at[1, off - 1], row=y_peers[off],
        )

    def to_col(off, arrives=False):
        ref = final.at[ahead(-off) if arrives else z]
        return remote(ref, ref, col_send.at[off - 1], col_recv.at[off - 1], col=ahead(off))

    order = (3, -3, 4, 1, -1, 2, -2, 0)
    around = (4, 3, 5, 2, 6, 1, 7)
    for off in order:
        pair(off).start()
    for off in (1, 3):
        to_x(off).start()
    for axis in range(3):
        for where in next_to[axis]:
            pl.semaphore_signal(near_in.at[axis], inc=1, device_id=where, device_id_type=MESH)
    got_x[x] = grad_part[...]
    for off in order[:5]:
        if off == 4:
            pl.semaphore_wait(near_in.at[0], 2)
            pl.semaphore_wait(near_in.at[1], 2)
            to_x(2).start()
        merge(off)
        for way in (0, 1):
            if off == 4 or off * ways[way] > 0:
                ring(way, abs(off) - 1).start()
    merge(2)
    merge(-2)
    for off in far_first:
        to_x(off, arrives=True).wait_recv()
    line[...] = (got_x[0] + got_x[1]) + (got_x[2] + got_x[3])
    pl.semaphore_wait(near_in.at[2], 2)
    for off in far_first:
        to_y(off).start()
    got_y[y] = line[...]
    for way in (0, 1):
        ring(way, 2).wait_recv()
        own[ahead(2 * ways[way])] += got_three[way]
        ring(way, 4).start()
    for way in (0, 1):
        ring(way, 3).wait_recv()
        own[ahead(2 * ways[way]), way] += got_four[way]
        ring(way, 1).start()
    merge(0)
    for off in far_first:
        to_y(off, arrives=True).wait_recv()
    value = ((got_y[0] + got_y[1]) + (got_y[2] + got_y[3])) * factor
    final[z] = value[:share]
    for off in around:
        to_col(off).start()
    grad_bias[...] = value[share:]
    for way in (0, 1):
        ring(way, 0).wait_recv()
    grad_feat[...] = (direct[...] + own[z]) + (got_one[0] + got_one[1])
    for off in order:
        pair(off).wait_send()
    for way in (0, 1):
        for kind in (0, 2, 3):
            ring(way, kind).wait_send()
    for off in far_first:
        to_x(off).wait_send()
        to_y(off).wait_send()
    for way in (0, 1):
        ring(way, 4).wait_recv()
        ring(way, 1).wait_recv()
    grad_feat[...] += got_two[0] + got_two[1]
    for off in around:
        to_col(off, arrives=True).wait_recv()
    grad_weights[...] = final[...]
    for way in (0, 1):
        for kind in (1, 4):
            ring(way, kind).wait_send()
    for off in around:
        to_col(off).wait_send()


def last(sums, direct, grad_part, cols, factor):
    width, block = sums.shape[1:]
    hid = grad_part.shape[1]
    share = 2 * width // cols
    vmem = pl.BlockSpec(memory_space=VMEM)
    return pl.pallas_call(
        functools.partial(last_kernel, cols, factor),
        out_shape=(
            VMEM((2, width // 2, block), F32),
            VMEM((cols, share, hid), F32),
            VMEM((8, hid), F32),
        ),
        in_specs=[vmem] * 3,
        out_specs=(vmem,) * 3,
        scratch_shapes=[
            VMEM((cols, 2, width // 2, block), F32),
            VMEM((cols, 2, width // 2, block), F32),
            VMEM((2, 2, width // 2, block), F32),
            VMEM((2, 2, width // 2, block), F32),
            VMEM((2, 2, width // 2, block), F32),
            VMEM((2, width // 2, block), F32),
            VMEM((SIDE, share + 8, hid), F32),
            VMEM((share + 8, hid), F32),
            VMEM((SIDE, share + 8, hid), F32),
            VMEM((cols, share, hid), F32),
            DMA((cols,)),
            DMA((cols,)),
            DMA((2, 5)),
            DMA((2, 5)),
            DMA((cols - 1,)),
            DMA((cols - 1,)),
            DMA((2, SIDE - 1)),
            DMA((2, SIDE - 1)),
            pltpu.SemaphoreType.REGULAR((3,)),
        ],
        compiler_params=pltpu.CompilerParams(
            collective_id=2, has_side_effects=True, vmem_limit_bytes=16 * MIB
        ),
        name="last",
    )(sums, direct, grad_part)


def finish_kernel(grad_feat, grad_weights, grad_bias, feat_out, self_out, neigh_out, bias_out, sems):
    block = grad_feat.shape[2]
    pieces = [
        (grad_feat.at[0], feat_out.at[:, pl.ds(0, block)]),
        (grad_feat.at[1], feat_out.at[:, pl.ds(block, block)]),
        (grad_weights.at[0], self_out),
        (grad_weights.at[1], neigh_out),
        (grad_bias.at[pl.ds(0, 1)], bias_out),
    ]
    copies = [pltpu.make_async_copy(src, dst, sems.at[at]) for at, (src, dst) in enumerate(pieces)]
    for copy in copies:
        copy.start()
    for copy in copies:
        copy.wait()


def finish(grad_feat, grad_weights, grad_bias):
    half, block = grad_feat.shape[1:]
    hid = grad_bias.shape[1]
    vmem = pl.BlockSpec(memory_space=VMEM)
    far = pl.BlockSpec(memory_space=pl.ANY)
    shape = jax.ShapeDtypeStruct
    return pl.pallas_call(
        finish_kernel,
        out_shape=(
            shape((half, 2 * block), F32), shape((2 * half, hid), F32), shape((2 * half, hid), F32), shape((1, hid), F32)
        ),
        in_specs=[vmem] * 3,
        out_specs=(far,) * 4,
        scratch_shapes=[DMA((5,))],
        compiler_params=pltpu.CompilerParams(vmem_limit_bytes=8 * MIB),
        name="finish",
    )(grad_feat, grad_weights.reshape(2, 2 * half, hid), grad_bias)


def shards(features, cotangent, w_self, w_neigh, bias, tiles, tile_dst, tile_src, tile_count):
    slots, block = tiles.shape[2:4]
    width = features.shape[1]
    hid = w_self.shape[1]
    cols = lax.axis_size("col")
    rows = lax.axis_size("row")
    tiles = tiles.reshape(slots, block, block)
    feat = features.reshape(2, block, width)
    cot = cotangent.reshape(2, block, hid)

    stacked, lists, tiles = gather_features(tile_count, tile_dst, tile_src, feat, tiles, cols, rows)
    sums = forward(lists, tiles, stacked, (SIDE + 1, SIDE, block + DEG, width))
    hidden, scaled, direct, grad_part = middle(sums, feat, cot, w_self, w_neigh, bias.reshape(1, hid), cols)
    back, hidden = backward(lists, tiles, scaled, hidden, (2 * cols + 1, width, block))
    factor = float(features.shape[0] * rows * cols) ** (-0.5)
    grad_feat, grad_self, grad_neigh, grad_bias = finish(*last(back, direct, grad_part, cols, factor))
    return (
        hidden.reshape(2 * block, hid // 2), grad_feat.T, grad_self, grad_neigh, grad_bias.reshape(hid // 2)
    )


def solution(mesh):
    return jax.shard_map(
        shards,
        mesh=mesh,
        in_specs=(
            P(("row", "col"), None),
            P(("row", "col"), None),
            P(),
            P(),
            P(),
            P("row", "col", None, None, None),
            P("row", "col", None),
            P("row", "col", None),
            P("row", "col"),
        ),
        out_specs=(
            P(("row", "col"), "rep"),
            P(("row", "col"), "rep"),
            P(None, "rep"),
            P(None, "rep"),
            P("rep"),
        ),
        check_vma=False,
    )
```
